128 devices in a mesh: dp: 8 (over y, core), store: 16 (over x, z).
Axes of the slice: x: 4, y: 4, z: 4, core: 2. Of those that a mesh axis runs over, the one named last changes fastest.
Arguments:
- node_table: bfloat16 [32768, 1024], P('store'), may hold values from -160 to 160
- touched: int32 [128, 16, 40], P(('dp', 'store')), may hold values from -1 to 2047, as said below
- member_slot: int32 [256, 256], P(('dp', 'store')), may hold values from 0 to 639, as said below
- distances: int32 [256, 256, 256], P(('dp', 'store')), may hold values from 0 to 31, as said below
- cotangent: bfloat16 [256, 256, 1024], P(('dp', 'store')), may hold values from -6 to 6
- w_qkv: bfloat16 [1024, 3072], replicated, may hold values from -0.1875 to 0.1875
- w_out: bfloat16 [1024, 1024], replicated, may hold values from -0.1875 to 0.1875
- w_up: bfloat16 [1024, 1024], replicated, may hold values from -0.1875 to 0.1875
- w_down: bfloat16 [1024, 1024], replicated, may hold values from -0.1875 to 0.1875
- gains: float32 [2, 1024], replicated, may hold values from 0.25 to 1.75
- bias_table: float32 [32, 32], replicated, may hold values from -3 to 300
Outputs:
- layer_out: bfloat16 [256, 256, 1024], P(('dp', 'store'))
- grad_table: bfloat16 [32768, 1024], P('store', 'dp')
- grad_qkv: bfloat16 [1024, 3072], P(('dp', 'store'))
- grad_out: bfloat16 [1024, 1024], P(('dp', 'store'))
- grad_up: bfloat16 [1024, 1024], P(('dp', 'store'))
- grad_down: bfloat16 [1024, 1024], P(('dp', 'store'))
- grad_gains: float32 [2, 1024], replicated
- grad_bias: float32 [32, 32], replicated
The draws below stay inside these ranges and needn't reach their ends.
Inputs may be any that keep to these rules, and one draw needn't show every extreme that they name: touched[r, o, c] is a row within store shard o (shard o holds rows o * 2048 to o * 2048 + 2047), or -1 for an unused slot. In each [r, o] the used slots come first, name distinct rows, and number at least 16; every reader uses all 40 slots of one shard, the same shard for all readers of one index of dp. member_slot[e, n] = o * 40 + c names a used slot [o, c] of touched for the reader that holds ego-net e; the 256 slots of one ego-net are distinct. `distances`: symmetric in the two node dimensions, zero exactly on the diagonal.
All inputs are finite; a program needn't handle non-finite values.
Results may differ from the reference program's by a relative error of at most 0.017.
Values may be sent and summed in bfloat16 or wider, within the bound.
A program may use at most 192 MiB of HBM per device.

```python
import math
import jax
import jax.numpy as jnp
from jax import lax

D = 1024
FF = 1024
HEADS = 32
SPD = 32
NODES = 256
EGO_DEV = 2
SLOTS = 640
ROWS = 2048
CAP = 40
EGONETS = 256
TABLE_ROWS = 32768
N_DP = 8
N_STORE = 16


def plan_counts(key):
    readers = N_DP * N_STORE
    low = 2 * CAP // 5
    base = jax.random.randint(jax.random.fold_in(key, 11), (readers, N_STORE), low, CAP // 2 + 1)
    hot = jax.random.randint(jax.random.fold_in(key, 12), (N_DP,), 0, N_STORE)
    hot = hot.at[0].set(N_STORE - 1)
    group_hot = jnp.repeat(hot, N_STORE)[:, None]
    owners = jnp.arange(N_STORE)[None, :]
    return jnp.where(owners == group_hot, CAP, base).astype(jnp.int32)


def draw_touched(key, part):
    readers = N_DP * N_STORE
    counts = plan_counts(key)
    scores = jax.random.randint(jax.random.fold_in(key, 13), (readers, N_STORE, ROWS), 0, 4096) * ROWS + jnp.arange(ROWS)[None, None, :]
    first_reader = jnp.arange(readers)[:, None, None] == 0
    last_row = jnp.arange(ROWS)[None, None, :] == ROWS - 1
    scores = jnp.where(first_reader & last_row, -1, scores)
    order = jnp.argsort(scores, axis=-1)[:, :, :CAP].astype(jnp.int32)
    live = jnp.arange(CAP)[None, None, :] < counts[:, :, None]
    return jnp.where(live, order, -1).astype(jnp.int32)


def draw_member_slot(key, part):
    counts = plan_counts(key)
    slot_ids = jnp.arange(SLOTS)
    live = (slot_ids % CAP)[None, :] < counts[:, slot_ids // CAP]
    live_ego = jnp.repeat(live, EGO_DEV, axis=0).astype(jnp.int32)
    noise = jax.random.randint(jax.random.fold_in(key, 14), (EGONETS, SLOTS), 0, 4096)
    last_slot = (slot_ids == SLOTS - 1).astype(jnp.int32)[None, :]
    scores = noise * SLOTS + slot_ids[None, :] + live_ego * (4096 * SLOTS) + live_ego * last_slot * (4096 * SLOTS)
    chosen = jax.lax.top_k(scores, NODES)[1]
    return chosen.astype(jnp.int32)


def draw_distances(key, part):
    raw = jax.random.randint(jax.random.fold_in(key, 15), (EGONETS, NODES, NODES), 1, SPD)
    rows = jnp.arange(NODES)[:, None]
    cols = jnp.arange(NODES)[None, :]
    symmetric = jnp.where(rows < cols, raw, jnp.swapaxes(raw, 1, 2))
    return jnp.where(rows == cols, 0, symmetric).astype(jnp.int32)


def draw_node_table(key, part):
    shape = (TABLE_ROWS, D)
    base = jnp.clip(jax.random.normal(jax.random.fold_in(key, 1), shape), -6.0, 6.0)
    row_scale = jnp.exp(jax.random.uniform(jax.random.fold_in(key, 2), (TABLE_ROWS, 1), minval=math.log(0.3), maxval=math.log(3.0)))
    col_scale = jnp.exp(jax.random.uniform(jax.random.fold_in(key, 3), (1, D), minval=math.log(0.3), maxval=math.log(3.0)))
    return (base * row_scale * col_scale).astype(jnp.bfloat16)


def draw_bias_table(key, part):
    values = jax.random.uniform(jax.random.fold_in(key, 6), (SPD, HEADS), minval=-3.0, maxval=3.0)
    return values.astype(jnp.float32)


def level_of(own_key, extent, cuts, low, high):
    loudness, own = 1.0, jax.random.fold_in(own_key, 6)
    for position, parts in cuts:
        draws = jnp.exp(jax.random.uniform(jax.random.fold_in(own, position), (parts,), jnp.float32, low / len(cuts), high / len(cuts)))
        loudness = loudness * jnp.repeat(draws, extent[position] // parts).reshape([-1 if axis == position else 1 for axis in range(len(extent))])
    return loudness


def normal_values(key, dims, scale, limit, pieces=(), kind=jnp.bfloat16):
    values = scale * jax.random.normal(key, dims, jnp.float32)
    if pieces:
        values = values * level_of(key, dims, pieces, -0.22, 0.18)
    return jnp.clip(values, -limit, limit).astype(kind)


def setup_inputs(seed: int = 0) -> dict:
    key_list = jax.random.split(jax.random.key(seed), 12)
    return {
        "node_table": draw_node_table(jax.random.fold_in(key_list[11], 71), 0),
        "touched": draw_touched(jax.random.fold_in(key_list[11], 71), 0),
        "member_slot": draw_member_slot(jax.random.fold_in(key_list[11], 71), 0),
        "distances": draw_distances(jax.random.fold_in(key_list[11], 71), 0),
        "cotangent": normal_values(key_list[4], (EGONETS, NODES, D), 1.0, 6.0, ((0, 128),)),
        "w_qkv": normal_values(key_list[5], (D, 3 * D), D ** -0.5, 0.1875),
        "w_out": normal_values(key_list[6], (D, D), D ** -0.5, 0.1875),
        "w_up": normal_values(key_list[7], (D, FF), D ** -0.5, 0.1875),
        "w_down": normal_values(key_list[8], (FF, D), FF ** -0.5, 0.1875),
        "gains": jnp.clip(1.0 + 0.15 * jax.random.normal(key_list[9], (2, D), jnp.float32), 0.25, 1.75),
        "bias_table": draw_bias_table(jax.random.fold_in(key_list[11], 71), 0),
    }


EPS = 1e-05
ROOT_HALF = 1.0 / math.sqrt(2.0)
ROOT_TWO_PI = 1.0 / math.sqrt(2.0 * math.pi)

def layer_normalize(value, gain):
    mean = lax.optimization_barrier(jnp.mean(value, -1, keepdims=True))
    centred = value - mean
    rstd = lax.rsqrt(lax.optimization_barrier(jnp.mean(centred * centred, -1, keepdims=True)) + EPS)
    vhat = centred * rstd
    return (vhat * gain, vhat, rstd)

def layer_normalize_backward(grad, gain, vhat, rstd):
    scaled = grad * gain
    first = lax.optimization_barrier(jnp.mean(scaled, -1, keepdims=True))
    second = lax.optimization_barrier(jnp.mean(scaled * vhat, -1, keepdims=True))
    return (rstd * (scaled - first - vhat * second), lax.optimization_barrier(jnp.sum(grad * vhat, 0)))

def gelu_parts(upper):
    normal_cdf = 0.5 * (1.0 + jax.scipy.special.erf(upper * ROOT_HALF))
    activation_slope = normal_cdf + upper * jnp.exp(-0.5 * upper * upper) * ROOT_TWO_PI
    return (upper * normal_cdf, activation_slope)

def one_hot_buckets(spd, buckets):
    return (spd[None] == jnp.arange(buckets)[:, None, None]).astype(jnp.float32)

def attend(query_rows, key_matrix_rows, value_matrix_rows, spd, table):
    scale = query_rows.shape[2] ** (-0.5)
    onehot = one_hot_buckets(spd, table.shape[0])
    bias = jnp.einsum('bnm,bh->hnm', onehot, table, precision=lax.Precision.HIGHEST)
    scores = jnp.einsum('nhc,mhc->hnm', query_rows.astype(jnp.float32), key_matrix_rows.astype(jnp.float32)) * scale + bias
    attention_probabilities = jax.nn.softmax(scores, axis=-1)
    probs_b = attention_probabilities.astype(jnp.bfloat16)
    attention_mixed = jnp.einsum('hnm,mhc->nhc', probs_b.astype(jnp.float32), value_matrix_rows.astype(jnp.float32))
    return (attention_mixed.astype(jnp.bfloat16), attention_probabilities)

def attend_back(dattn, query_rows, key_matrix_rows, value_matrix_rows, attention_probabilities, spd, table):
    scale = query_rows.shape[2] ** (-0.5)
    probs_b = attention_probabilities.astype(jnp.bfloat16).astype(jnp.float32)
    dattn_f = dattn.astype(jnp.float32)
    dprobs = jnp.einsum('nhc,mhc->hnm', dattn_f, value_matrix_rows.astype(jnp.float32))
    dscores = attention_probabilities * (dprobs - lax.optimization_barrier(jnp.sum(dprobs * attention_probabilities, -1, keepdims=True)))
    onehot = one_hot_buckets(spd, table.shape[0])
    table_grad = jnp.einsum('bnm,hnm->bh', onehot, dscores, precision=lax.Precision.HIGHEST)
    dscores_b = (dscores * scale).astype(jnp.bfloat16).astype(jnp.float32)
    grad_q = jnp.einsum('hnm,mhc->nhc', dscores_b, key_matrix_rows.astype(jnp.float32))
    grad_k = jnp.einsum('hnm,nhc->mhc', dscores_b, query_rows.astype(jnp.float32))
    grad_v = jnp.einsum('hnm,nhc->mhc', probs_b, dattn_f)
    count = query_rows.shape[0]
    joined = jnp.concatenate([grad_q.reshape(count, -1), grad_k.reshape(count, -1), grad_v.reshape(count, -1)], axis=1)
    return (joined.astype(jnp.bfloat16), table_grad)

def layer_forward(x_rows, spd, w_qkv, w_out, w_up, w_down, gains, table):
    egos, count, width = x_rows.shape
    heads = table.shape[1]
    flattened_rows = x_rows.reshape(egos * count, width).astype(jnp.float32)
    first_hidden_float, normalized_input, first_inverse_deviation = layer_normalize(flattened_rows, gains[0])
    first_hidden = first_hidden_float.astype(jnp.bfloat16)
    qkv = jnp.dot(first_hidden, w_qkv, preferred_element_type=jnp.float32).astype(jnp.bfloat16)
    qkv = qkv.reshape(egos, count, 3, heads, width // heads)
    query_rows, key_matrix_rows, value_matrix_rows = (qkv[:, :, 0], qkv[:, :, 1], qkv[:, :, 2])
    attention_mixed, attention_probabilities = jax.vmap(attend, in_axes=(0, 0, 0, 0, None))(query_rows, key_matrix_rows, value_matrix_rows, spd, table)
    attention_mixed = attention_mixed.reshape(egos * count, width)
    y_rows = flattened_rows + jnp.dot(attention_mixed, w_out, preferred_element_type=jnp.float32)
    h2f, normalized_output, second_inverse_deviation = layer_normalize(y_rows, gains[1])
    second_hidden = h2f.astype(jnp.bfloat16)
    upper = jnp.dot(second_hidden, w_up, preferred_element_type=jnp.float32)
    act_f, activation_slope = gelu_parts(upper)
    activation_values = act_f.astype(jnp.bfloat16)
    result = (y_rows + jnp.dot(activation_values, w_down, preferred_element_type=jnp.float32)).astype(jnp.bfloat16)
    saved_residuals = (first_hidden, normalized_input, first_inverse_deviation, query_rows, key_matrix_rows, value_matrix_rows, attention_probabilities, attention_mixed, normalized_output, second_inverse_deviation, second_hidden, activation_slope, activation_values)
    return (result.reshape(egos, count, width), saved_residuals)

def ffn_back(dout, saved_residuals, w_up, w_down, gains):
    first_hidden, normalized_input, first_inverse_deviation, query_rows, key_matrix_rows, value_matrix_rows, attention_probabilities, attention_mixed, normalized_output, second_inverse_deviation, second_hidden, activation_slope, activation_values = saved_residuals
    grad_down = jnp.dot(activation_values.T, dout, preferred_element_type=jnp.float32)
    dgate = jnp.dot(dout, w_down.T, preferred_element_type=jnp.float32)
    grad_u = (dgate * activation_slope).astype(jnp.bfloat16)
    grad_up = jnp.dot(second_hidden.T, grad_u, preferred_element_type=jnp.float32)
    dh2 = jnp.dot(grad_u, w_up.T, preferred_element_type=jnp.float32)
    norm_input_gradient, gain_two = layer_normalize_backward(dh2, gains[1], normalized_output, second_inverse_deviation)
    return (grad_down, grad_up, dout.astype(jnp.float32) + norm_input_gradient, gain_two)

def attn_back(grad_y, saved_residuals, spd, w_qkv, w_out, gains, table):
    first_hidden, normalized_input, first_inverse_deviation, query_rows, key_matrix_rows, value_matrix_rows, attention_probabilities, attention_mixed, normalized_output, second_inverse_deviation, second_hidden, activation_slope, activation_values = saved_residuals
    egos, count = (query_rows.shape[0], query_rows.shape[1])
    grad_yb = grad_y.astype(jnp.bfloat16)
    grad_out = jnp.dot(attention_mixed.T, grad_yb, preferred_element_type=jnp.float32)
    dattn = jnp.dot(grad_yb, w_out.T, preferred_element_type=jnp.float32).astype(jnp.bfloat16)
    dattn = dattn.reshape(query_rows.shape)
    grad_qkv_rows, table_grads = jax.vmap(attend_back, in_axes=(0, 0, 0, 0, 0, 0, None))(dattn, query_rows, key_matrix_rows, value_matrix_rows, attention_probabilities, spd, table)
    grad_qkv_rows = grad_qkv_rows.reshape(egos * count, -1)
    grad_qkv = jnp.dot(first_hidden.T, grad_qkv_rows, preferred_element_type=jnp.float32)
    first_hidden_gradient = jnp.dot(grad_qkv_rows, w_qkv.T, preferred_element_type=jnp.float32)
    norm_input_gradient, first_norm_gain = layer_normalize_backward(first_hidden_gradient, gains[0], normalized_input, first_inverse_deviation)
    return (grad_qkv, grad_out, lax.optimization_barrier(jnp.sum(table_grads, 0)), grad_y + norm_input_gradient, first_norm_gain)

def reference(node_table, touched, member_slot, distances, cotangent, w_qkv, w_out, w_up, w_down, gains, bias_table):
    readers = N_DP * N_STORE
    table_rows = ROWS * N_STORE
    owner_base = (jnp.arange(N_STORE) * ROWS).astype(jnp.int32)[:, None]

    def one_reader(index, carry):
        acc_table, acc_qkv, acc_out, acc_up, acc_down, acc_gains, acc_bias, outputs = carry
        reader = jnp.asarray(index).astype(jnp.int32)
        requests = lax.dynamic_index_in_dim(touched, reader, 0, keepdims=False)
        valid = requests >= 0
        rows = (owner_base + jnp.maximum(requests, 0)).astype(jnp.int32)
        fetched = jnp.where(valid[..., None], node_table[rows], jnp.zeros((), jnp.bfloat16))
        slots = fetched.reshape(SLOTS, D)
        start = (reader * EGO_DEV).astype(jnp.int32)
        members = lax.dynamic_slice_in_dim(member_slot, start, EGO_DEV, 0)
        spd = lax.dynamic_slice_in_dim(distances, start, EGO_DEV, 0)
        dout = lax.dynamic_slice_in_dim(cotangent, start, EGO_DEV, 0).reshape(EGO_DEV * NODES, D)
        x_rows = slots[members]
        result, saved_residuals = layer_forward(x_rows, spd, w_qkv, w_out, w_up, w_down, gains, bias_table)
        grad_down, grad_up, grad_y, gain_two = ffn_back(dout, saved_residuals, w_up, w_down, gains)
        grad_qkv, grad_out, table_grad, grad_x, first_norm_gain = attn_back(grad_y, saved_residuals, spd, w_qkv, w_out, gains, bias_table)
        slot_grads = jax.ops.segment_sum(grad_x, members.reshape(-1), num_segments=SLOTS)
        target = jnp.where(valid, rows, table_rows).reshape(-1).astype(jnp.int32)
        acc_table = acc_table.at[target].add(slot_grads, mode='drop')
        acc_gains = acc_gains + jnp.stack([first_norm_gain, gain_two])
        outputs = lax.dynamic_update_slice_in_dim(outputs, result, start, 0)
        return (acc_table, acc_qkv + grad_qkv, acc_out + grad_out, acc_up + grad_up, acc_down + grad_down, acc_gains, acc_bias + table_grad, outputs)
    start_carry = (jnp.zeros((table_rows, D), jnp.float32), jnp.zeros((D, 3 * D), jnp.float32), jnp.zeros((D, D), jnp.float32), jnp.zeros((D, FF), jnp.float32), jnp.zeros((FF, D), jnp.float32), jnp.zeros((2, D), jnp.float32), jnp.zeros((SPD, HEADS), jnp.float32), jnp.zeros((EGONETS, NODES, D), jnp.bfloat16))
    acc_table, acc_qkv, acc_out, acc_up, acc_down, acc_gains, acc_bias, outputs = lax.fori_loop(0, readers, one_reader, start_carry)
    return (outputs, acc_table.astype(jnp.bfloat16), acc_qkv.astype(jnp.bfloat16), acc_out.astype(jnp.bfloat16), acc_up.astype(jnp.bfloat16), acc_down.astype(jnp.bfloat16), acc_gains, acc_bias)
```

```python
import math

import jax
import jax.numpy as jnp
from jax import lax
from jax.experimental import pallas as pl
from jax.experimental.pallas import tpu as pltpu
from jax.sharding import PartitionSpec as P

EPS = 1e-05
ROOT_HALF = 1.0 / math.sqrt(2.0)
ROOT_TWO_PI = 1.0 / math.sqrt(2.0 * math.pi)


def layer_normalize(value, gain):
    mean = jnp.mean(value, -1, keepdims=True)
    centred = value - mean
    rstd = lax.rsqrt(jnp.mean(centred * centred, -1, keepdims=True) + EPS)
    vhat = centred * rstd
    return (vhat * gain, vhat, rstd)


def layer_normalize_backward(grad, gain, vhat, rstd):
    scaled = grad * gain
    first = jnp.mean(scaled, -1, keepdims=True)
    second = jnp.mean(scaled * vhat, -1, keepdims=True)
    return (rstd * (scaled - first - vhat * second), jnp.sum(grad * vhat, 0))


def gelu_parts(upper):
    normal_cdf = 0.5 * (1.0 + jax.scipy.special.erf(upper * ROOT_HALF))
    activation_slope = normal_cdf + upper * jnp.exp(-0.5 * upper * upper) * ROOT_TWO_PI
    return (upper * normal_cdf, activation_slope)


def one_hot_buckets(spd, buckets):
    return (spd[None] == jnp.arange(buckets)[:, None, None]).astype(jnp.float32)


def attend(query_rows, key_matrix_rows, value_matrix_rows, spd, table):
    scale = query_rows.shape[2] ** (-0.5)
    onehot = one_hot_buckets(spd, table.shape[0])
    bias = jnp.einsum("bnm,bh->hnm", onehot, table, precision=lax.Precision.HIGHEST)
    scores = (
        jnp.einsum("nhc,mhc->hnm", query_rows, key_matrix_rows, preferred_element_type=jnp.float32)
        * scale
        + bias
    )
    attention_probabilities = jax.nn.softmax(scores, axis=-1)
    probs_b = attention_probabilities.astype(jnp.bfloat16)
    attention_mixed = jnp.einsum(
        "hnm,mhc->nhc", probs_b, value_matrix_rows, preferred_element_type=jnp.float32
    )
    return (attention_mixed.astype(jnp.bfloat16), attention_probabilities)


def attend_back(
    dattn, query_rows, key_matrix_rows, value_matrix_rows, attention_probabilities, spd, table
):
    scale = query_rows.shape[2] ** (-0.5)
    probs_b = attention_probabilities.astype(jnp.bfloat16)
    dprobs = jnp.einsum(
        "nhc,mhc->hnm", dattn, value_matrix_rows, preferred_element_type=jnp.float32
    )
    dscores = attention_probabilities * (
        dprobs - jnp.sum(dprobs * attention_probabilities, -1, keepdims=True)
    )
    onehot = one_hot_buckets(spd, table.shape[0])
    table_grad = jnp.einsum("bnm,hnm->bh", onehot, dscores, precision=lax.Precision.HIGHEST)
    dscores_b = (dscores * scale).astype(jnp.bfloat16)
    grad_q = jnp.einsum(
        "hnm,mhc->nhc", dscores_b, key_matrix_rows, preferred_element_type=jnp.float32
    )
    grad_k = jnp.einsum("hnm,nhc->mhc", dscores_b, query_rows, preferred_element_type=jnp.float32)
    grad_v = jnp.einsum("hnm,nhc->mhc", probs_b, dattn, preferred_element_type=jnp.float32)
    count = query_rows.shape[0]
    joined = jnp.concatenate(
        [grad_q.reshape(count, -1), grad_k.reshape(count, -1), grad_v.reshape(count, -1)], axis=1
    )
    return (joined.astype(jnp.bfloat16), table_grad)


def layer_forward(x_rows, spd, w_qkv, w_out, w_up, w_down, gains, table):
    egos, count, width = x_rows.shape
    heads = table.shape[1]
    flattened_rows = x_rows.reshape(egos * count, width).astype(jnp.float32)
    first_hidden_float, normalized_input, first_inverse_deviation = layer_normalize(
        flattened_rows, gains[0]
    )
    first_hidden = first_hidden_float.astype(jnp.bfloat16)
    qkv = jnp.dot(first_hidden, w_qkv, preferred_element_type=jnp.float32).astype(jnp.bfloat16)
    qkv = qkv.reshape(egos, count, 3, heads, width // heads)
    query_rows, key_matrix_rows, value_matrix_rows = (qkv[:, :, 0], qkv[:, :, 1], qkv[:, :, 2])
    attention_mixed, attention_probabilities = jax.vmap(attend, in_axes=(0, 0, 0, 0, None))(
        query_rows, key_matrix_rows, value_matrix_rows, spd, table
    )
    attention_mixed = attention_mixed.reshape(egos * count, width)
    y_rows = flattened_rows + jnp.dot(attention_mixed, w_out, preferred_element_type=jnp.float32)
    h2f, normalized_output, second_inverse_deviation = layer_normalize(y_rows, gains[1])
    second_hidden = h2f.astype(jnp.bfloat16)
    upper = jnp.dot(second_hidden, w_up, preferred_element_type=jnp.float32)
    act_f, activation_slope = gelu_parts(upper)
    activation_values = act_f.astype(jnp.bfloat16)
    result = (
        y_rows + jnp.dot(activation_values, w_down, preferred_element_type=jnp.float32)
    ).astype(jnp.bfloat16)
    saved_residuals = (
        first_hidden,
        normalized_input,
        first_inverse_deviation,
        query_rows,
        key_matrix_rows,
        value_matrix_rows,
        attention_probabilities,
        attention_mixed,
        normalized_output,
        second_inverse_deviation,
        second_hidden,
        activation_slope,
        activation_values,
    )
    return (result.reshape(egos, count, width), saved_residuals)


def ffn_back(dout, saved_residuals, w_up, w_down, gains):
    (
        first_hidden,
        normalized_input,
        first_inverse_deviation,
        query_rows,
        key_matrix_rows,
        value_matrix_rows,
        attention_probabilities,
        attention_mixed,
        normalized_output,
        second_inverse_deviation,
        second_hidden,
        activation_slope,
        activation_values,
    ) = saved_residuals
    grad_down = jnp.dot(activation_values.T, dout, preferred_element_type=jnp.float32)
    dgate = jnp.dot(dout, w_down.T, preferred_element_type=jnp.float32)
    grad_u = (dgate * activation_slope).astype(jnp.bfloat16)
    grad_up = jnp.dot(second_hidden.T, grad_u, preferred_element_type=jnp.float32)
    dh2 = jnp.dot(grad_u, w_up.T, preferred_element_type=jnp.float32)
    norm_input_gradient, gain_two = layer_normalize_backward(
        dh2, gains[1], normalized_output, second_inverse_deviation
    )
    return (grad_down, grad_up, dout.astype(jnp.float32) + norm_input_gradient, gain_two)


def attn_back(grad_y, saved_residuals, spd, w_qkv, w_out, gains, table):
    (
        first_hidden,
        normalized_input,
        first_inverse_deviation,
        query_rows,
        key_matrix_rows,
        value_matrix_rows,
        attention_probabilities,
        attention_mixed,
        normalized_output,
        second_inverse_deviation,
        second_hidden,
        activation_slope,
        activation_values,
    ) = saved_residuals
    egos, count = (query_rows.shape[0], query_rows.shape[1])
    grad_yb = grad_y.astype(jnp.bfloat16)
    grad_out = jnp.dot(attention_mixed.T, grad_yb, preferred_element_type=jnp.float32)
    dattn = jnp.dot(grad_yb, w_out.T, preferred_element_type=jnp.float32).astype(jnp.bfloat16)
    dattn = dattn.reshape(query_rows.shape)
    grad_qkv_rows, table_grads = jax.vmap(attend_back, in_axes=(0, 0, 0, 0, 0, 0, None))(
        dattn, query_rows, key_matrix_rows, value_matrix_rows, attention_probabilities, spd, table
    )
    grad_qkv_rows = grad_qkv_rows.reshape(egos * count, -1)
    grad_qkv = jnp.dot(first_hidden.T, grad_qkv_rows, preferred_element_type=jnp.float32)
    first_hidden_gradient = jnp.dot(grad_qkv_rows, w_qkv.T, preferred_element_type=jnp.float32)
    norm_input_gradient, first_norm_gain = layer_normalize_backward(
        first_hidden_gradient, gains[0], normalized_input, first_inverse_deviation
    )
    return (
        grad_qkv,
        grad_out,
        jnp.sum(table_grads, 0),
        grad_y + norm_input_gradient,
        first_norm_gain,
    )


MESH = pl.DeviceIdType.MESH
ORDERS = ((0, 1, 2), (1, 2, 0), (2, 0, 1))
PIECES = 6


def coordinates():
    dp, store = lax.axis_index("dp"), lax.axis_index("store")
    return lax.div(dp, 2), lax.rem(dp, 2), lax.div(store, 4), lax.rem(store, 4)


def peer(y, core, x, z):
    return (y * 2 + core, x * 4 + z)


def along(axis, offset):
    y, core, x, z = coordinates()
    place = [y, x, z]
    place[axis] = lax.rem(place[axis] + offset, 4)
    return peer(place[0], core, place[1], place[2]), place[axis]


def reduce_kernel(
    g_qkv, g_out, g_up, g_down, small,
    o_qkv, o_out, o_up, o_down, o_small,
    own, got, part0, recv0, part1, recv1, part2, recv2, small_core, small_all,
    own_sem, core_send, core_recv, send, recv, sc_send, sc_recv, s_send, s_recv,
):
    y, core, x, z = coordinates()
    here = (y, x, z)
    other = peer(y, 1 - core, x, z)
    everyone = [other] + [along(a, k)[0] for a in range(3) for k in (1, 2, 3)]

    barrier = pltpu.get_barrier_semaphore()
    for device in everyone:
        pl.semaphore_signal(barrier, inc=1, device_id=device, device_id_type=MESH)
    pl.semaphore_wait(barrier, len(everyone))

    sources = [g_down, g_up, g_out] + [g_qkv] * 3
    outs = [o_down, o_up, o_out] + [o_qkv] * 3
    columns = [0, 0, 0, 0, 1024, 2048]
    sends = []

    local, cross = [], []
    tiny = pltpu.make_async_remote_copy(
        src_ref=small, dst_ref=small_core, send_sem=sc_send, recv_sem=sc_recv,
        device_id=other, device_id_type=MESH)
    tiny.start()
    for j in range(PIECES):
        cols = pl.ds(columns[j], 1024)
        remote = pltpu.make_async_remote_copy(
            src_ref=sources[j].at[:, 1 - core, :, cols], dst_ref=got.at[j],
            send_sem=core_send.at[j], recv_sem=core_recv.at[j],
            device_id=other, device_id_type=MESH)
        remote.start()
        cross.append(remote)
        keep = pltpu.make_async_copy(sources[j].at[:, core, :, cols], own.at[j], own_sem.at[j])
        keep.start()
        local.append(keep)

    tiny.wait()

    def spread_small(axis):
        copies = []
        for k in (1, 2, 3):
            device, _ = along(axis, k)
            copy = pltpu.make_async_remote_copy(
                src_ref=small_all.at[axis, here[axis]], dst_ref=small_all.at[axis, here[axis]],
                send_sem=s_send.at[axis, k - 1], recv_sem=s_recv.at[axis, k - 1],
                device_id=device, device_id_type=MESH)
            copy.start()
            copies.append(copy)
        return copies

    def total_small(axis):
        return (small_all[axis, 0] + small_all[axis, 1]) + (small_all[axis, 2] + small_all[axis, 3])

    small_all[0, here[0]] = small[...] + small_core[...]
    tiny_copies = spread_small(0)

    def scatter(j, stage, part):
        order = ORDERS[j % 3]
        axis = order[stage]
        left = [a for a in (0, 1, 2) if a not in order[:stage]]
        where = left.index(axis)
        landing = (recv0, recv1, recv2)[stage]
        copies = []
        for k in (1, 2, 3):
            device, place = along(axis, k)
            block = (j,) + (slice(None),) * where + (place,)
            copy = pltpu.make_async_remote_copy(
                src_ref=part.at[block], dst_ref=landing.at[j, k - 1],
                send_sem=send.at[stage, j, k - 1], recv_sem=recv.at[stage, j, k - 1],
                device_id=device, device_id_type=MESH)
            copy.start()
            copies.append(copy)
        return copies

    flight = [None] * PIECES
    for j in range(PIECES):
        local[j].wait()
        cross[j].wait_recv()

        def add_cores(i, carry, j=j):
            yy, xx = lax.div(i, 4), lax.rem(i, 4)
            rows = pl.ds(pl.multiple_of(xx * 32, 32), 32)
            total = own[j, yy, rows, :].astype(jnp.float32) + got[j, yy, rows, :].astype(jnp.float32)
            for zz in range(4):
                mine = total[8 * zz : 8 * zz + 8]
                part0[j, yy, xx, zz] = jnp.concatenate([mine[:, :512], mine[:, 512:]], 0).astype(jnp.bfloat16)
            return carry

        lax.fori_loop(0, 16, add_cores, 0)
        flight[j] = scatter(j, 0, part0)

    for copy in tiny_copies:
        copy.wait()
    small_all[1, here[1]] = total_small(0)
    tiny_copies = spread_small(1)

    for j in range(PIECES):
        for copy in flight[j]:
            copy.wait_recv()
        sends += flight[j]
        axis = ORDERS[j % 3][0]

        def add_first(i, carry, j=j, axis=axis):
            a, b = lax.div(i, 4), lax.rem(i, 4)
            block = [a, b]
            block.insert(axis, here[axis])
            total = part0[(j,) + tuple(block)].astype(jnp.float32)
            for k in range(3):
                total = total + recv0[j, k, a, b].astype(jnp.float32)
            part1[j, a, b] = total.astype(jnp.bfloat16)
            return carry

        lax.fori_loop(0, 16, add_first, 0)
        flight[j] = scatter(j, 1, part1)

    for copy in tiny_copies:
        copy.wait()
    small_all[2, here[2]] = total_small(1)
    tiny_copies = spread_small(2)

    for j in range(PIECES):
        for copy in flight[j]:
            copy.wait_recv()
        sends += flight[j]
        order = ORDERS[j % 3]
        where = [a for a in (0, 1, 2) if a != order[0]].index(order[1])

        def add_second(i, carry, j=j, axis=order[1], where=where):
            block = [i]
            block.insert(where, here[axis])
            total = part1[(j,) + tuple(block)].astype(jnp.float32)
            for k in range(3):
                total = total + recv1[j, k, i].astype(jnp.float32)
            part2[j, i] = total.astype(jnp.bfloat16)
            return carry

        lax.fori_loop(0, 4, add_second, 0)
        flight[j] = scatter(j, 2, part2)

    for copy in tiny_copies:
        copy.wait()
    o_small[...] = total_small(2)

    for j in range(PIECES):
        for copy in flight[j]:
            copy.wait_recv()
        sends += flight[j]
        axis = ORDERS[j % 3][2]
        total = part2[j, here[axis]].astype(jnp.float32)
        for k in range(3):
            total = total + recv2[j, k].astype(jnp.float32)
        joined = jnp.concatenate([total[:8], total[8:]], 1).astype(jnp.bfloat16)
        outs[j][:, columns[j] : columns[j] + 1024] = joined

    for copy in cross + sends:
        copy.wait_send()


def reduce_gradients(g_qkv, g_out, g_up, g_down, small):
    bf16, f32 = jnp.bfloat16, jnp.float32
    hbm = pl.BlockSpec(memory_space=pl.ANY)
    vmem = pl.BlockSpec(memory_space=pltpu.VMEM)
    dma = pltpu.SemaphoreType.DMA
    split = lambda g: g.reshape(4, 2, 128, g.shape[1])
    return pl.pallas_call(
        reduce_kernel,
        name="reduce_gradients",
        out_shape=(
            jax.ShapeDtypeStruct((8, 3072), bf16),
            jax.ShapeDtypeStruct((8, 1024), bf16),
            jax.ShapeDtypeStruct((8, 1024), bf16),
            jax.ShapeDtypeStruct((8, 1024), bf16),
            jax.ShapeDtypeStruct(small.shape, f32),
        ),
        in_specs=[hbm] * 4 + [vmem],
        out_specs=[vmem] * 5,
        scratch_shapes=[
            pltpu.VMEM((PIECES, 4, 128, 1024), bf16),
            pltpu.VMEM((PIECES, 4, 128, 1024), bf16),
            pltpu.VMEM((PIECES, 4, 4, 4, 16, 512), bf16),
            pltpu.VMEM((PIECES, 3, 4, 4, 16, 512), bf16),
            pltpu.VMEM((PIECES, 4, 4, 16, 512), bf16),
            pltpu.VMEM((PIECES, 3, 4, 16, 512), bf16),
            pltpu.VMEM((PIECES, 4, 16, 512), bf16),
            pltpu.VMEM((PIECES, 3, 16, 512), bf16),
            pltpu.VMEM(small.shape, f32),
            pltpu.VMEM((3, 4) + small.shape, f32),
            dma((PIECES,)),
            dma((PIECES,)),
            dma((PIECES,)),
            dma((3, PIECES, 3)),
            dma((3, PIECES, 3)),
            dma,
            dma,
            dma((3, 3)),
            dma((3, 3)),
        ],
        compiler_params=pltpu.CompilerParams(
            collective_id=0, has_side_effects=True, vmem_limit_bytes=40 * 1024 * 1024
        ),
    )(split(g_qkv), split(g_out), split(g_up), split(g_down), small)


def body(
    node_table,
    touched,
    member_slot,
    distances,
    cotangent,
    w_qkv,
    w_out,
    w_up,
    w_down,
    gains,
    bias_table,
):
    shard_rows = node_table.shape[0]
    width = node_table.shape[1]
    requests = lax.all_to_all(touched, "store", split_axis=1, concat_axis=1, tiled=True)
    valid = requests >= 0
    picked = jnp.take(node_table, jnp.maximum(requests, 0), axis=0)
    picked = jnp.where(valid[..., None], picked, jnp.zeros((), picked.dtype))
    returned = lax.all_to_all(picked, "store", split_axis=1, concat_axis=1, tiled=True)
    fetched = returned
    lists = lax.all_gather(requests[0], "dp", axis=1, tiled=True)
    owners, cap = (fetched.shape[1], fetched.shape[2])
    slots = fetched.reshape(owners * cap, width)
    x_rows = jnp.take(slots, member_slot, axis=0)
    egos, count = member_slot.shape
    result, saved_residuals = layer_forward(
        x_rows, distances, w_qkv, w_out, w_up, w_down, gains, bias_table
    )
    dout = cotangent.reshape(egos * count, width)
    grad_down, grad_up, grad_y, gain_two = ffn_back(dout, saved_residuals, w_up, w_down, gains)
    grad_qkv, grad_out, table_grad, grad_x, first_norm_gain = attn_back(
        grad_y, saved_residuals, distances, w_qkv, w_out, gains, bias_table
    )
    slot_grads = jax.ops.segment_sum(grad_x, member_slot.reshape(-1), num_segments=owners * cap)
    slot_grads = slot_grads.reshape(owners, cap, width)
    returned = lax.all_to_all(
        lax.all_to_all(
            slot_grads.astype(jnp.bfloat16), "dp", split_axis=2, concat_axis=1, tiled=True
        ),
        "store",
        split_axis=0,
        concat_axis=0,
        tiled=True,
    ).astype(slot_grads.dtype)
    target = jnp.where(lists >= 0, lists, shard_rows).reshape(-1)
    summed = jax.ops.segment_sum(
        returned.reshape(-1, returned.shape[2]), target, num_segments=shard_rows + 1
    )
    grad_table = summed[:shard_rows].astype(jnp.bfloat16)
    grad_qkv, grad_out, grad_up, grad_down = (
        g.astype(jnp.bfloat16) for g in (grad_qkv, grad_out, grad_up, grad_down)
    )
    small = jnp.concatenate(
        [first_norm_gain.reshape(8, 128), gain_two.reshape(8, 128), table_grad.reshape(8, 128)]
    )
    sum_qkv, sum_out, sum_up, sum_down, small = reduce_gradients(
        grad_qkv, grad_out, grad_up, grad_down, small
    )
    grad_gains, grad_bias = small[:16].reshape(2, 1024), small[16:].reshape(32, 32)
    return (
        result,
        grad_table,
        sum_qkv,
        sum_out,
        sum_up,
        sum_down,
        grad_gains,
        grad_bias,
    )


def solution(mesh):
    in_specs = (
        P("store", None),
        P(("dp", "store"), None, None),
        P(("dp", "store"), None),
        P(("dp", "store"), None, None),
        P(("dp", "store"), None, None),
        P(),
        P(),
        P(),
        P(),
        P(),
        P(),
    )
    out_specs = (
        P(("dp", "store"), None, None),
        P("store", "dp"),
        P(("dp", "store"), None),
        P(("dp", "store"), None),
        P(("dp", "store"), None),
        P(("dp", "store"), None),
        P(),
        P(),
    )
    return jax.shard_map(body, mesh=mesh, in_specs=in_specs, out_specs=out_specs, check_vma=False)
```

```python
import math

import jax
import jax.numpy as jnp
from jax import lax
from jax.experimental import pallas as pl
from jax.experimental.pallas import tpu as pltpu
from jax.sharding import PartitionSpec as P

EPS = 1e-05
ROOT_HALF = 1.0 / math.sqrt(2.0)
ROOT_TWO_PI = 1.0 / math.sqrt(2.0 * math.pi)


def layer_normalize(value, gain):
    mean = jnp.mean(value, -1, keepdims=True)
    centred = value - mean
    rstd = lax.rsqrt(jnp.mean(centred * centred, -1, keepdims=True) + EPS)
    vhat = centred * rstd
    return (vhat * gain, vhat, rstd)


def layer_normalize_backward(grad, gain, vhat, rstd):
    scaled = grad * gain
    first = jnp.mean(scaled, -1, keepdims=True)
    second = jnp.mean(scaled * vhat, -1, keepdims=True)
    return (rstd * (scaled - first - vhat * second), jnp.sum(grad * vhat, 0))


def gelu_parts(upper):
    normal_cdf = 0.5 * (1.0 + jax.scipy.special.erf(upper * ROOT_HALF))
    activation_slope = normal_cdf + upper * jnp.exp(-0.5 * upper * upper) * ROOT_TWO_PI
    return (upper * normal_cdf, activation_slope)


GROUP = 8
LOG2E = math.log2(math.e)


def head_mask(rows, width, head):
    lanes = lax.broadcasted_iota(jnp.int32, (rows, width), 1)
    return lax.div(lanes, width // GROUP) == head


def only_head(value, head):
    return jnp.where(head_mask(value.shape[0], value.shape[1], head), value, jnp.zeros((), value.dtype))


def attend_kernel(q_ref, k_ref, v_ref, spd_ref, table_ref, mixed_ref, probs_ref, scores):
    group = pl.program_id(1)
    count = q_ref.shape[0]
    head_width = q_ref.shape[1] // GROUP
    scale = LOG2E * head_width ** (-0.5)
    chunk = 32
    q, k, v = q_ref[...], k_ref[...], v_ref[...]
    lookups = [
        jnp.broadcast_to(table_ref[pl.ds(group * GROUP + j, 1), :], (8, 128)) for j in range(GROUP)
    ]

    def look_up(n, carry):
        rows = pl.ds(pl.multiple_of(n * 8, 8), 8)
        for a in range(0, count, 128):
            spd = spd_ref[0, rows, a : a + 128]
            for j in range(GROUP):
                scores[j, rows, a : a + 128] = jnp.take_along_axis(
                    lookups[j], spd, axis=1, mode="promise_in_bounds"
                )
        return carry

    lax.fori_loop(0, count // 8, look_up, 0, unroll=4)
    mixed = jnp.zeros(q.shape, jnp.float32)
    for j in range(GROUP):
        raw = lax.dot_general(
            q, only_head(k, j), (((1,), (1,)), ((), ())), preferred_element_type=jnp.float32
        )
        parts = []
        for c in range(count // chunk):
            rows = slice(c * chunk, c * chunk + chunk)
            logits = raw[rows] * scale + scores[j, rows, :]
            power = jnp.exp2(logits - jnp.max(logits, -1, keepdims=True))
            probs = power * (1.0 / jnp.sum(power, -1, keepdims=True))
            probs_ref[0, j, rows, :] = probs
            parts.append(probs.astype(jnp.bfloat16))
        mixed = mixed + jnp.dot(
            jnp.concatenate(parts, 0), only_head(v, j), preferred_element_type=jnp.float32
        )
    mixed_ref[...] = mixed.astype(mixed_ref.dtype)


def attend_back_kernel(
    q_ref, k_ref, v_ref, dattn_ref, probs_ref, spd_ref,
    dq_ref, dk_ref, dv_ref, bias_ref, slopes, onehot, corner,
):
    ego, group = pl.program_id(0), pl.program_id(1)
    count, width = q_ref.shape
    scale = (width // GROUP) ** (-0.5)
    buckets = 32
    chunk = 32
    q, k, v, dattn = q_ref[...], k_ref[...], v_ref[...], dattn_ref[...]

    @pl.when(group == 0)
    def _():
        def fill(n, carry):
            row = jnp.broadcast_to(spd_ref[0, pl.ds(n, 1), :], (buckets, count))
            hit = row == lax.broadcasted_iota(jnp.int32, (buckets, count), 0)
            onehot[pl.ds(pl.multiple_of(n * buckets, buckets), buckets), :] = jnp.where(hit, 1.0, 0.0).astype(jnp.bfloat16)
            return carry

        lax.fori_loop(0, count, fill, 0, unroll=8)

    dq = jnp.zeros((count, width), jnp.float32)
    dk = jnp.zeros((count, width), jnp.float32)
    dv = jnp.zeros((count, width), jnp.float32)
    over_rows = (((0,), (0,)), ((), ()))
    for j in range(GROUP):
        dprobs = lax.dot_general(
            dattn, only_head(v, j), (((1,), (1,)), ((), ())), preferred_element_type=jnp.float32
        )
        slope_parts, prob_parts = [], []
        for c in range(count // chunk):
            rows = slice(c * chunk, c * chunk + chunk)
            probs = probs_ref[0, j, rows, :]
            part = dprobs[rows]
            slope = probs * (part - jnp.sum(part * probs, -1, keepdims=True))
            for a in range(count // 128):
                slopes[group * (count // 128) + a, pl.ds(c * chunk * GROUP + j, chunk, stride=GROUP), :] = slope[:, a * 128 : a * 128 + 128]
            slope_parts.append((slope * scale).astype(jnp.bfloat16))
            prob_parts.append(probs.astype(jnp.bfloat16))
        slope_b = jnp.concatenate(slope_parts, 0)
        probs_b = jnp.concatenate(prob_parts, 0)
        dq = dq + jnp.dot(slope_b, only_head(k, j), preferred_element_type=jnp.float32)
        dk = dk + lax.dot_general(slope_b, only_head(q, j), over_rows, preferred_element_type=jnp.float32)
        dv = dv + lax.dot_general(probs_b, only_head(dattn, j), over_rows, preferred_element_type=jnp.float32)
    dq_ref[...] = dq.astype(dq_ref.dtype)
    dk_ref[...] = dk.astype(dk_ref.dtype)
    dv_ref[...] = dv.astype(dv_ref.dtype)

    @pl.when(group == pl.num_programs(1) - 1)
    def _():
        halves = count // 128
        groups = slopes.shape[0] // halves
        corner[...] = jnp.zeros_like(corner)

        def collect(i, carry):
            total = corner[...]
            for n in range(4):
                first = pl.multiple_of((i * 4 + n) * 8 * GROUP, 8 * GROUP)
                rows = pl.ds(first, 8 * GROUP)
                left = jnp.concatenate(
                    [
                        jnp.concatenate([slopes[g * halves + a, rows, :] for a in range(halves)], 1)
                        for g in range(groups)
                    ],
                    0,
                ).astype(jnp.bfloat16)
                first = pl.multiple_of((i * 4 + n) * 8 * buckets, 8 * buckets)
                right = onehot[pl.ds(first, 8 * buckets), :]
                total = total + lax.dot_general(
                    left, right, (((1,), (1,)), ((), ())), preferred_element_type=jnp.float32
                )
            corner[...] = total
            return carry

        lax.fori_loop(0, count // 32, collect, 0)
        shape = corner.shape
        node_row = lax.rem(lax.div(lax.broadcasted_iota(jnp.int32, shape, 0), GROUP), 8)
        node_col = lax.div(lax.broadcasted_iota(jnp.int32, shape, 1), buckets)
        kept = jnp.where(node_row == node_col, corner[...], 0.0)
        tall = []
        for g in range(groups):
            heads = kept[g * 8 * GROUP : g * 8 * GROUP + GROUP]
            for n in range(1, 8):
                heads = heads + kept[(g * 8 + n) * GROUP : (g * 8 + n) * GROUP + GROUP]
            tall.append(heads)
        bias_ref[0] = jnp.concatenate(tall, 0)


def attention_specs(count, width, heads):
    wide = width // heads * GROUP
    groups = heads // GROUP
    column = lambda part: pl.BlockSpec((count, wide), lambda e, g, part=part: (e, part * groups + g))
    probs = pl.BlockSpec((1, GROUP, count, count), lambda e, g: (e, g, 0, 0))
    spd = pl.BlockSpec((1, count, count), lambda e, g: (e, 0, 0))
    return column, probs, spd, groups


def attention_forward(qkv, spd, table):
    egos, count, _ = spd.shape
    heads, width = table.shape[1], qkv.shape[1] // 3
    column, probs, spd_spec, groups = attention_specs(count, width, heads)
    lookup = jnp.pad((table * LOG2E).T, ((0, 0), (0, 128 - table.shape[0])))
    return pl.pallas_call(
        attend_kernel,
        name="attend",
        grid=(egos, groups),
        out_shape=(
            jax.ShapeDtypeStruct((egos * count, width), jnp.bfloat16),
            jax.ShapeDtypeStruct((egos, heads, count, count), jnp.float32),
        ),
        in_specs=[column(0), column(1), column(2), spd_spec, pl.BlockSpec((heads, 128), lambda e, g: (0, 0))],
        out_specs=(column(0), probs),
        scratch_shapes=[pltpu.VMEM((GROUP, count, count), jnp.float32)],
        compiler_params=pltpu.CompilerParams(vmem_limit_bytes=40 * 1024 * 1024),
    )(qkv, qkv, qkv, spd, lookup)


def attention_backward(qkv, dattn, probs, spd, table):
    egos, count, _ = spd.shape
    heads, width = table.shape[1], qkv.shape[1] // 3
    column, probs_spec, spd_spec, groups = attention_specs(count, width, heads)
    flat = jax.ShapeDtypeStruct((egos * count, width), jnp.bfloat16)
    dq, dk, dv, bias = pl.pallas_call(
        attend_back_kernel,
        name="attend_back",
        grid=(egos, groups),
        out_shape=(flat, flat, flat, jax.ShapeDtypeStruct((egos, heads, 256), jnp.float32)),
        in_specs=[column(0), column(1), column(2), column(0), probs_spec, spd_spec],
        out_specs=(column(0), column(0), column(0), pl.BlockSpec((1, heads, 256), lambda e, g: (e, 0, 0))),
        scratch_shapes=[
            pltpu.VMEM((groups * (count // 128), count * GROUP, 128), jnp.float32),
            pltpu.VMEM((count * 32, count), jnp.bfloat16),
            pltpu.VMEM((groups * 8 * GROUP, 256), jnp.float32),
        ],
        compiler_params=pltpu.CompilerParams(vmem_limit_bytes=48 * 1024 * 1024),
    )(qkv, qkv, qkv, dattn, probs, spd)
    return dq, dk, dv, bias.reshape(egos, heads, 8, 32).sum((0, 2)).T


def pick_kernel(rows_ref, table_ref, out_ref, chosen):
    @pl.when(pl.program_id(0) == 0)
    def _():
        shape = chosen.shape
        hit = jnp.broadcast_to(rows_ref[...], shape) == lax.broadcasted_iota(jnp.int32, shape, 1)
        chosen[...] = jnp.where(hit, 1.0, 0.0).astype(jnp.bfloat16)

    out_ref[...] = jnp.dot(chosen[...], table_ref[...], preferred_element_type=jnp.float32).astype(out_ref.dtype)


def pick_rows(requests, node_table):
    rows, width = node_table.shape
    count = requests.size
    return pl.pallas_call(
        pick_kernel,
        name="pick_rows",
        grid=(width // 256,),
        out_shape=jax.ShapeDtypeStruct((count, width), node_table.dtype),
        in_specs=[pl.BlockSpec((count, 1), lambda i: (0, 0)), pl.BlockSpec((rows, 256), lambda i: (0, i))],
        out_specs=pl.BlockSpec((count, 256), lambda i: (0, i)),
        scratch_shapes=[pltpu.VMEM((count, rows), jnp.bfloat16)],
        compiler_params=pltpu.CompilerParams(vmem_limit_bytes=40 * 1024 * 1024),
    )(requests.reshape(count, 1), node_table)


def slot_kernel(member_ref, dx_ref, out_ref):
    slots, tokens = out_ref.shape[1], dx_ref.shape[0]
    shape = (slots, tokens)
    hit = jnp.broadcast_to(member_ref[...], shape) == lax.broadcasted_iota(jnp.int32, shape, 0)
    placed = jnp.where(hit, 1.0, 0.0).astype(jnp.bfloat16)
    dx = dx_ref[...]
    high = dx.astype(jnp.bfloat16)
    low = (dx - high.astype(jnp.float32)).astype(jnp.bfloat16)
    total = jnp.dot(placed, high, preferred_element_type=jnp.float32) + jnp.dot(
        placed, low, preferred_element_type=jnp.float32
    )
    for c in range(out_ref.shape[0]):
        out_ref[c] = total[:, c * 128 : c * 128 + 128].astype(out_ref.dtype)


def slot_gradients(member_slot, dx, slots):
    tokens, width = dx.shape
    return pl.pallas_call(
        slot_kernel,
        name="slot_gradients",
        grid=(width // 256,),
        out_shape=jax.ShapeDtypeStruct((width // 128, slots, 128), jnp.bfloat16),
        in_specs=[pl.BlockSpec((1, tokens), lambda i: (0, 0)), pl.BlockSpec((tokens, 256), lambda i: (0, i))],
        out_specs=pl.BlockSpec((2, slots, 128), lambda i: (i, 0, 0)),
        compiler_params=pltpu.CompilerParams(vmem_limit_bytes=40 * 1024 * 1024),
    )(member_slot.reshape(1, tokens), dx)


def place_kernel(lists_ref, grads_ref, out_ref):
    block, entries = out_ref.shape[0], lists_ref.shape[1]
    base = pl.program_id(0) * block
    total = jnp.zeros(out_ref.shape, jnp.float32)
    step = 1024
    for a in range(0, entries, step):
        shape = (block, step)
        hit = jnp.broadcast_to(lists_ref[:, a : a + step], shape) == lax.broadcasted_iota(jnp.int32, shape, 0) + base
        total = total + jnp.dot(
            jnp.where(hit, 1.0, 0.0).astype(jnp.bfloat16), grads_ref[a : a + step], preferred_element_type=jnp.float32
        )
    out_ref[...] = total.astype(out_ref.dtype)


def place_gradients(lists, grads, rows):
    entries, width = grads.shape
    return pl.pallas_call(
        place_kernel,
        name="place_gradients",
        grid=(rows // 256,),
        out_shape=jax.ShapeDtypeStruct((rows, width), jnp.bfloat16),
        in_specs=[pl.BlockSpec((1, entries), lambda i: (0, 0)), pl.BlockSpec((entries, width), lambda i: (0, 0))],
        out_specs=pl.BlockSpec((256, width), lambda i: (i, 0)),
        compiler_params=pltpu.CompilerParams(vmem_limit_bytes=40 * 1024 * 1024),
    )(lists.reshape(1, entries), grads)


MESH = pl.DeviceIdType.MESH
ORDERS = ((0, 1, 2), (1, 2, 0), (2, 0, 1))
PIECES = 6


def coordinates():
    dp, store = lax.axis_index("dp"), lax.axis_index("store")
    return lax.div(dp, 2), lax.rem(dp, 2), lax.div(store, 4), lax.rem(store, 4)


def peer(y, core, x, z):
    return (y * 2 + core, x * 4 + z)


def along(axis, offset):
    y, core, x, z = coordinates()
    place = [y, x, z]
    place[axis] = lax.rem(place[axis] + offset, 4)
    return peer(place[0], core, place[1], place[2]), place[axis]


def reduce_kernel(
    g_down, g_up, g_out, g_q, g_k, g_v, small,
    o_qkv, o_out, o_up, o_down, o_small,
    own, got, part0, recv0, part1, recv1, part2, recv2, small_core, small_all,
    own_sem, core_send, core_recv, send, recv, sc_send, sc_recv, s_send, s_recv,
):
    y, core, x, z = coordinates()
    here = (y, x, z)
    other = peer(y, 1 - core, x, z)
    everyone = [other] + [along(a, k)[0] for a in range(3) for k in (1, 2, 3)]

    barrier = pltpu.get_barrier_semaphore()
    for device in everyone:
        pl.semaphore_signal(barrier, inc=1, device_id=device, device_id_type=MESH)
    pl.semaphore_wait(barrier, len(everyone))

    sources = [g_down, g_up, g_out, g_q, g_k, g_v]
    outs = [o_down, o_up, o_out] + [o_qkv] * 3
    columns = [0, 0, 0, 0, 1024, 2048]
    sends = []

    local, cross = [], []
    tiny = pltpu.make_async_remote_copy(
        src_ref=small, dst_ref=small_core, send_sem=sc_send, recv_sem=sc_recv,
        device_id=other, device_id_type=MESH)
    tiny.start()
    for j in range(PIECES):
        remote = pltpu.make_async_remote_copy(
            src_ref=sources[j].at[:, 1 - core], dst_ref=got.at[j],
            send_sem=core_send.at[j], recv_sem=core_recv.at[j],
            device_id=other, device_id_type=MESH)
        remote.start()
        cross.append(remote)
        keep = pltpu.make_async_copy(sources[j].at[:, core], own.at[j], own_sem.at[j])
        keep.start()
        local.append(keep)

    tiny.wait()

    def spread_small(axis):
        copies = []
        for k in (1, 2, 3):
            device, _ = along(axis, k)
            copy = pltpu.make_async_remote_copy(
                src_ref=small_all.at[axis, here[axis]], dst_ref=small_all.at[axis, here[axis]],
                send_sem=s_send.at[axis, k - 1], recv_sem=s_recv.at[axis, k - 1],
                device_id=device, device_id_type=MESH)
            copy.start()
            copies.append(copy)
        return copies

    def total_small(axis):
        return (small_all[axis, 0] + small_all[axis, 1]) + (small_all[axis, 2] + small_all[axis, 3])

    small_all[0, here[0]] = small[...] + small_core[...]
    tiny_copies = spread_small(0)

    def scatter(j, stage, part):
        order = ORDERS[j % 3]
        axis = order[stage]
        left = [a for a in (0, 1, 2) if a not in order[:stage]]
        where = left.index(axis)
        landing = (recv0, recv1, recv2)[stage]
        copies = []
        for k in (1, 2, 3):
            device, place = along(axis, k)
            block = (j,) + (slice(None),) * where + (place,)
            copy = pltpu.make_async_remote_copy(
                src_ref=part.at[block], dst_ref=landing.at[j, k - 1],
                send_sem=send.at[stage, j, k - 1], recv_sem=recv.at[stage, j, k - 1],
                device_id=device, device_id_type=MESH)
            copy.start()
            copies.append(copy)
        return copies

    flight = [None] * PIECES
    for j in range(PIECES):
        local[j].wait()
        cross[j].wait_recv()

        def add_cores(i, carry, j=j):
            yy, xx = lax.div(i, 4), lax.rem(i, 4)
            rows = pl.ds(pl.multiple_of(xx * 32, 32), 32)
            total = own[j, yy, rows, :].astype(jnp.float32) + got[j, yy, rows, :].astype(jnp.float32)
            for zz in range(4):
                mine = total[8 * zz : 8 * zz + 8]
                part0[j, yy, xx, zz] = jnp.concatenate([mine[:, :512], mine[:, 512:]], 0).astype(jnp.bfloat16)
            return carry

        lax.fori_loop(0, 16, add_cores, 0)
        flight[j] = scatter(j, 0, part0)

    for copy in tiny_copies:
        copy.wait()
    small_all[1, here[1]] = total_small(0)
    tiny_copies = spread_small(1)

    for j in range(PIECES):
        for copy in flight[j]:
            copy.wait_recv()
        sends += flight[j]
        axis = ORDERS[j % 3][0]

        def add_first(i, carry, j=j, axis=axis):
            a, b = lax.div(i, 4), lax.rem(i, 4)
            block = [a, b]
            block.insert(axis, here[axis])
            total = part0[(j,) + tuple(block)].astype(jnp.float32)
            for k in range(3):
                total = total + recv0[j, k, a, b].astype(jnp.float32)
            part1[j, a, b] = total.astype(jnp.bfloat16)
            return carry

        lax.fori_loop(0, 16, add_first, 0)
        flight[j] = scatter(j, 1, part1)

    for copy in tiny_copies:
        copy.wait()
    small_all[2, here[2]] = total_small(1)
    tiny_copies = spread_small(2)

    for j in range(PIECES):
        for copy in flight[j]:
            copy.wait_recv()
        sends += flight[j]
        order = ORDERS[j % 3]
        where = [a for a in (0, 1, 2) if a != order[0]].index(order[1])

        def add_second(i, carry, j=j, axis=order[1], where=where):
            block = [i]
            block.insert(where, here[axis])
            total = part1[(j,) + tuple(block)].astype(jnp.float32)
            for k in range(3):
                total = total + recv1[j, k, i].astype(jnp.float32)
            part2[j, i] = total.astype(jnp.bfloat16)
            return carry

        lax.fori_loop(0, 4, add_second, 0)
        flight[j] = scatter(j, 2, part2)

    for copy in tiny_copies:
        copy.wait()
    o_small[...] = total_small(2)

    for j in range(PIECES):
        for copy in flight[j]:
            copy.wait_recv()
        sends += flight[j]
        axis = ORDERS[j % 3][2]
        total = part2[j, here[axis]].astype(jnp.float32)
        for k in range(3):
            total = total + recv2[j, k].astype(jnp.float32)
        joined = jnp.concatenate([total[:8], total[8:]], 1).astype(jnp.bfloat16)
        outs[j][:, columns[j] : columns[j] + 1024] = joined

    for copy in cross + sends:
        copy.wait_send()


def reduce_gradients(gradients, small):
    bf16, f32 = jnp.bfloat16, jnp.float32
    hbm = pl.BlockSpec(memory_space=pl.ANY)
    vmem = pl.BlockSpec(memory_space=pltpu.VMEM)
    dma = pltpu.SemaphoreType.DMA
    split = lambda g: g.reshape(4, 2, 128, g.shape[1])
    return pl.pallas_call(
        reduce_kernel,
        name="reduce_gradients",
        out_shape=(
            jax.ShapeDtypeStruct((8, 3072), bf16),
            jax.ShapeDtypeStruct((8, 1024), bf16),
            jax.ShapeDtypeStruct((8, 1024), bf16),
            jax.ShapeDtypeStruct((8, 1024), bf16),
            jax.ShapeDtypeStruct(small.shape, f32),
        ),
        in_specs=[hbm] * PIECES + [vmem],
        out_specs=[vmem] * 5,
        scratch_shapes=[
            pltpu.VMEM((PIECES, 4, 128, 1024), bf16),
            pltpu.VMEM((PIECES, 4, 128, 1024), bf16),
            pltpu.VMEM((PIECES, 4, 4, 4, 16, 512), bf16),
            pltpu.VMEM((PIECES, 3, 4, 4, 16, 512), bf16),
            pltpu.VMEM((PIECES, 4, 4, 16, 512), bf16),
            pltpu.VMEM((PIECES, 3, 4, 16, 512), bf16),
            pltpu.VMEM((PIECES, 4, 16, 512), bf16),
            pltpu.VMEM((PIECES, 3, 16, 512), bf16),
            pltpu.VMEM(small.shape, f32),
            pltpu.VMEM((3, 4) + small.shape, f32),
            dma((PIECES,)),
            dma((PIECES,)),
            dma((PIECES,)),
            dma((3, PIECES, 3)),
            dma((3, PIECES, 3)),
            dma,
            dma,
            dma((3, 3)),
            dma((3, 3)),
        ],
        compiler_params=pltpu.CompilerParams(
            collective_id=0, has_side_effects=True, vmem_limit_bytes=40 * 1024 * 1024
        ),
    )(*[split(g) for g in gradients], small)


def body(
    node_table,
    touched,
    member_slot,
    distances,
    cotangent,
    w_qkv,
    w_out,
    w_up,
    w_down,
    gains,
    bias_table,
):
    bf16, f32 = jnp.bfloat16, jnp.float32
    both = ("dp", "store")
    shard_rows, width = node_table.shape
    owners, cap = touched.shape[1:]
    egos, count = member_slot.shape
    tokens, slots_held = egos * count, owners * cap
    dot = lambda a, b: jnp.dot(a, b, preferred_element_type=f32)
    back = lambda a, b: lax.dot_general(a, b, (((1,), (1,)), ((), ())), preferred_element_type=f32)
    weight = lambda a, b: lax.dot_general(
        a, b, (((0,), (0,)), ((), ())), preferred_element_type=f32
    ).astype(bf16)

    asked = jnp.broadcast_to(touched, (lax.axis_size("dp"), owners, cap)).reshape(-1, cap)
    lists = lax.all_to_all(asked, both, split_axis=0, concat_axis=0, tiled=True)
    requests = lax.dynamic_slice_in_dim(lists, lax.axis_index("dp") * owners, owners, 0)
    picked = pick_rows(requests, node_table)
    slots = lax.all_to_all(
        picked.reshape(owners, cap, width), "store", split_axis=0, concat_axis=0, tiled=True
    ).reshape(slots_held, width)
    x = jnp.take(slots, member_slot.reshape(-1), axis=0, mode="clip").astype(f32)
    dout = cotangent.reshape(tokens, width)

    h1, x_hat, x_rstd = layer_normalize(x, gains[0])
    h1 = h1.astype(bf16)
    qkv = dot(h1, w_qkv).astype(bf16)
    attended, probs = attention_forward(qkv, distances, bias_table)
    y = x + dot(attended, w_out)
    h2, y_hat, y_rstd = layer_normalize(y, gains[1])
    h2 = h2.astype(bf16)
    act, slope = gelu_parts(dot(h2, w_up))
    act = act.astype(bf16)
    layer_out = (y + dot(act, w_down)).astype(bf16)

    du = (back(dout, w_down) * slope).astype(bf16)
    dy, gain_two = layer_normalize_backward(back(du, w_up), gains[1], y_hat, y_rstd)
    dy = dout.astype(f32) + dy
    dyb = dy.astype(bf16)
    dattn = back(dyb, w_out).astype(bf16)
    dq, dk, dv, grad_bias = attention_backward(qkv, dattn, probs, distances, bias_table)
    dh1 = (
        back(dq, w_qkv[:, :width])
        + back(dk, w_qkv[:, width : 2 * width])
        + back(dv, w_qkv[:, 2 * width :])
    )
    dx, gain_one = layer_normalize_backward(dh1, gains[0], x_hat, x_rstd)
    dx = dy + dx

    slot_grads = slot_gradients(member_slot, dx, slots_held)
    returned = lax.all_to_all(
        slot_grads.reshape(-1, cap, 128), both, split_axis=0, concat_axis=0, tiled=True
    )
    gradients = (
        weight(act, dout), weight(h2, du), weight(attended, dyb),
        weight(h1, dq), weight(h1, dk), weight(h1, dv),
    )
    small = jnp.concatenate(
        [gain_one.reshape(8, 128), gain_two.reshape(8, 128), grad_bias.reshape(8, 128)]
    )
    sum_qkv, sum_out, sum_up, sum_down, small = reduce_gradients(gradients, small)
    grad_table = place_gradients(lists, returned.reshape(-1, 128), shard_rows)
    return (
        layer_out.reshape(egos, count, width),
        grad_table,
        sum_qkv,
        sum_out,
        sum_up,
        sum_down,
        small[:16].reshape(2, width),
        small[16:].reshape(32, 32),
    )


def solution(mesh):
    in_specs = (
        P("store", None),
        P(("dp", "store"), None, None),
        P(("dp", "store"), None),
        P(("dp", "store"), None, None),
        P(("dp", "store"), None, None),
        P(),
        P(),
        P(),
        P(),
        P(),
        P(),
    )
    out_specs = (
        P(("dp", "store"), None, None),
        P("store", "dp"),
        P(("dp", "store"), None),
        P(("dp", "store"), None),
        P(("dp", "store"), None),
        P(("dp", "store"), None),
        P(),
        P(),
    )
    return jax.shard_map(body, mesh=mesh, in_specs=in_specs, out_specs=out_specs, check_vma=False)
```

```python
import math

import jax
import jax.numpy as jnp
from jax import lax
from jax.experimental import pallas as pl
from jax.experimental.pallas import tpu as pltpu
from jax.sharding import PartitionSpec as P

MESH = pl.DeviceIdType.MESH
ORDERS = ((0, 1, 2), (1, 2, 0), (2, 0, 1))
PIECES = 6


EPS = 1e-05
ROOT_HALF = 1.0 / math.sqrt(2.0)
ROOT_TWO_PI = 1.0 / math.sqrt(2.0 * math.pi)


def layer_normalize(value, gain):
    mean = jnp.mean(value, -1, keepdims=True)
    centred = value - mean
    rstd = lax.rsqrt(jnp.mean(centred * centred, -1, keepdims=True) + EPS)
    vhat = centred * rstd
    return (vhat * gain, vhat, rstd)


def layer_normalize_backward(grad, gain, vhat, rstd):
    scaled = grad * gain
    first = jnp.mean(scaled, -1, keepdims=True)
    second = jnp.mean(scaled * vhat, -1, keepdims=True)
    return (rstd * (scaled - first - vhat * second), jnp.sum(grad * vhat, 0))


def gelu_parts(upper):
    normal_cdf = 0.5 * (1.0 + jax.scipy.special.erf(upper * ROOT_HALF))
    activation_slope = normal_cdf + upper * jnp.exp(-0.5 * upper * upper) * ROOT_TWO_PI
    return (upper * normal_cdf, activation_slope)


LISTED = 128


def fetch_kernel(
    touched, members, table_hbm, spd, lookup,
    x_out, lists_out, bias_hbm,
    table, asked, lists, chosen, outgoing, slots, bias,
    table_sem, ask_send, ask_recv, list_send, list_recv, row_send, row_recv, bias_sem,
):
    dp, store = lax.axis_index("dp"), lax.axis_index("store")
    shards, groups = asked.shape[0], lists.shape[0]
    rows, width = table.shape
    cap = slots.shape[1] // 2
    half = width // 2
    egos, heads, count, _ = bias.shape
    turn = lambda here, k, size: lax.rem(here + k, size)
    owners = [(dp, turn(store, k, shards)) for k in range(shards)]
    copies_of_shard = [(turn(dp, k, groups), store) for k in range(groups)]

    load = pltpu.make_async_copy(table_hbm, table, table_sem)
    load.start()
    barrier = pltpu.get_barrier_semaphore()
    for device in owners[1:] + copies_of_shard[1:]:
        pl.semaphore_signal(barrier, inc=1, device_id=device, device_id_type=MESH)
    pl.semaphore_wait(barrier, shards + groups - 2)

    requests = []
    for k in range(1, shards):
        copy = pltpu.make_async_remote_copy(
            src_ref=touched.at[owners[k][1]], dst_ref=asked.at[store],
            send_sem=ask_send.at[k], recv_sem=ask_recv.at[k],
            device_id=owners[k], device_id_type=MESH)
        copy.start()
        requests.append(copy)
    asked[store] = touched[store]

    bias_copies = []

    def look_up(ego, first, many):
        def step(n, carry):
            at = pl.ds(pl.multiple_of(n * 8, 8), 8)
            for a in range(0, count, 128):
                distance = spd[ego, at, a : a + 128]
                for h in range(first, first + many):
                    row = jnp.broadcast_to(lookup[h : h + 1, :], (8, 128))
                    bias[ego, h, at, a : a + 128] = jnp.take_along_axis(
                        row, distance, axis=1, mode="promise_in_bounds"
                    )
            return carry

        lax.fori_loop(0, count // 8, step, 0, unroll=2)
        part = pl.ds(first, many)
        copy = pltpu.make_async_copy(
            bias.at[ego, part], bias_hbm.at[ego, part], bias_sem.at[len(bias_copies)])
        copy.start()
        bias_copies.append(copy)

    look_up(0, 0, 8)
    for copy in requests:
        copy.wait_recv()
    shared = []
    for k in range(1, groups):
        copy = pltpu.make_async_remote_copy(
            src_ref=asked, dst_ref=lists.at[dp],
            send_sem=list_send.at[k], recv_sem=list_recv.at[k],
            device_id=copies_of_shard[k], device_id_type=MESH)
        copy.start()
        shared.append(copy)
    lists[dp] = asked[...]

    order = list(range(1, shards)) + [0]
    turned = jnp.concatenate(
        [asked[owners[k][1]] for k in order] + [jnp.full((LISTED - shards, LISTED), -1, jnp.int32)], 0
    ).T
    for p in range(0, shards, 2):
        pair = jnp.concatenate([turned[:cap, p : p + 1], turned[:cap, p + 1 : p + 2]], 0)
        shape = (2 * cap, rows)
        hit = jnp.broadcast_to(pair, shape) == lax.broadcasted_iota(jnp.int32, shape, 1)
        chosen[p * cap : (p + 2) * cap, :] = jnp.where(hit, 1.0, 0.0).astype(jnp.bfloat16)
    load.wait()
    sent = []
    for first in range(0, shards, 4):
        picks = chosen[first * cap : (first + 4) * cap, :]
        left = jnp.dot(picks, table[:, :half], preferred_element_type=jnp.float32)
        right = jnp.dot(picks, table[:, half:], preferred_element_type=jnp.float32)
        for i in range(4):
            k = order[first + i]
            mine = slice(i * cap, i * cap + cap)
            block = jnp.concatenate([left[mine], right[mine]], 0).astype(jnp.bfloat16)
            if k == 0:
                slots[store] = block
                continue
            outgoing[k] = block
            copy = pltpu.make_async_remote_copy(
                src_ref=outgoing.at[k], dst_ref=slots.at[store],
                send_sem=row_send.at[k], recv_sem=row_recv.at[k],
                device_id=owners[k], device_id_type=MESH)
            copy.start()
            sent.append(copy)

    look_up(0, 8, heads - 8)
    look_up(1, 0, heads)
    for copy in sent:
        copy.wait_recv()
    tokens = members.shape[0]
    shape = (tokens, shards * 2 * cap)
    held = slots[...].reshape(shards * 2 * cap, half)
    places = lax.broadcasted_iota(jnp.int32, shape, 1)
    for part in range(2):
        hit = jnp.broadcast_to(members[...] + part * cap, shape) == places
        x_out[:, part * half : part * half + half] = jnp.dot(
            jnp.where(hit, 1.0, 0.0).astype(jnp.bfloat16), held, preferred_element_type=jnp.float32
        ).astype(x_out.dtype)
    for copy in shared:
        copy.wait()
    lists_out[...] = lists[...]
    for copy in requests + sent:
        copy.wait_send()
    for copy in bias_copies:
        copy.wait()


def fetch(node_table, touched, member_slot, spd, table):
    bf16, f32, i32 = jnp.bfloat16, jnp.float32, jnp.int32
    _, shards, cap = touched.shape
    groups = lax.axis_size("dp")
    egos, count = member_slot.shape
    heads = table.shape[1]
    rows, width = node_table.shape
    lookup = jnp.pad((table * LOG2E).T, ((0, 0), (0, 128 - table.shape[0])))
    listed = jnp.pad(
        touched.reshape(shards, 1, cap), ((0, 0), (0, 0), (0, LISTED - cap)), constant_values=-1
    )
    members = (member_slot + cap * lax.div(member_slot, cap)).reshape(egos * count, 1)
    hbm = pl.BlockSpec(memory_space=pl.ANY)
    vmem = pl.BlockSpec(memory_space=pltpu.VMEM)
    dma = pltpu.SemaphoreType.DMA
    x, lists, bias = pl.pallas_call(
        fetch_kernel,
        name="fetch",
        out_shape=(
            jax.ShapeDtypeStruct((egos * count, width), bf16),
            jax.ShapeDtypeStruct((groups, shards, 1, LISTED), i32),
            jax.ShapeDtypeStruct((egos, heads, count, count), f32),
        ),
        in_specs=[vmem, vmem, hbm, vmem, vmem],
        out_specs=(vmem, vmem, hbm),
        scratch_shapes=[
            pltpu.VMEM((rows, width), bf16),
            pltpu.VMEM((shards, 1, LISTED), i32),
            pltpu.VMEM((groups, shards, 1, LISTED), i32),
            pltpu.VMEM((shards * cap, rows), bf16),
            pltpu.VMEM((shards, 2 * cap, width // 2), bf16),
            pltpu.VMEM((shards, 2 * cap, width // 2), bf16),
            pltpu.VMEM((egos, heads, count, count), f32),
            dma,
            dma((shards,)),
            dma((shards,)),
            dma((groups,)),
            dma((groups,)),
            dma((shards,)),
            dma((shards,)),
            dma((3,)),
        ],
        compiler_params=pltpu.CompilerParams(
            collective_id=1, has_side_effects=True, vmem_limit_bytes=48 * 1024 * 1024
        ),
    )(listed, members, node_table, spd, lookup)
    return x, lists[:, :, 0, :cap].reshape(-1), bias


GROUP = 8
LOG2E = math.log2(math.e)


def head_mask(rows, width, head):
    lanes = lax.broadcasted_iota(jnp.int32, (rows, width), 1)
    return lax.div(lanes, width // GROUP) == head


def only_head(value, head):
    return jnp.where(head_mask(value.shape[0], value.shape[1], head), value, jnp.zeros((), value.dtype))


def attend_kernel(q_ref, k_ref, v_ref, bias_ref, mixed_ref, probs_ref):
    count = q_ref.shape[0]
    head_width = q_ref.shape[1] // GROUP
    scale = LOG2E * head_width ** (-0.5)
    chunk = 32
    q, k, v = q_ref[...], k_ref[...], v_ref[...]
    mixed = jnp.zeros(q.shape, jnp.float32)
    for j in range(GROUP):
        raw = lax.dot_general(
            q, only_head(k, j), (((1,), (1,)), ((), ())), preferred_element_type=jnp.float32
        )
        parts = []
        for c in range(count // chunk):
            rows = slice(c * chunk, c * chunk + chunk)
            logits = raw[rows] * scale + bias_ref[0, j, rows, :]
            power = jnp.exp2(logits - jnp.max(logits, -1, keepdims=True))
            probs = power * (1.0 / jnp.sum(power, -1, keepdims=True))
            probs_ref[0, j, rows, :] = probs
            parts.append(probs.astype(jnp.bfloat16))
        mixed = mixed + jnp.dot(
            jnp.concatenate(parts, 0), only_head(v, j), preferred_element_type=jnp.float32
        )
    mixed_ref[...] = mixed.astype(mixed_ref.dtype)


def attend_back_kernel(
    q_ref, k_ref, v_ref, dattn_ref, probs_ref, spd_ref,
    dq_ref, dk_ref, dv_ref, bias_ref, slopes, onehot, corner,
):
    ego, group = pl.program_id(0), pl.program_id(1)
    count, width = q_ref.shape
    scale = (width // GROUP) ** (-0.5)
    buckets = 32
    chunk = 32
    q, k, v, dattn = q_ref[...], k_ref[...], v_ref[...], dattn_ref[...]

    @pl.when(group == 0)
    def _():
        def fill(n, carry):
            row = jnp.broadcast_to(spd_ref[0, pl.ds(n, 1), :], (buckets, count))
            hit = row == lax.broadcasted_iota(jnp.int32, (buckets, count), 0)
            onehot[pl.ds(pl.multiple_of(n * buckets, buckets), buckets), :] = jnp.where(hit, 1.0, 0.0).astype(jnp.bfloat16)
            return carry

        lax.fori_loop(0, count, fill, 0, unroll=8)

    dq = jnp.zeros((count, width), jnp.float32)
    dk = jnp.zeros((count, width), jnp.float32)
    dv = jnp.zeros((count, width), jnp.float32)
    over_rows = (((0,), (0,)), ((), ()))
    for j in range(GROUP):
        dprobs = lax.dot_general(
            dattn, only_head(v, j), (((1,), (1,)), ((), ())), preferred_element_type=jnp.float32
        )
        slope_parts, prob_parts = [], []
        for c in range(count // chunk):
            rows = slice(c * chunk, c * chunk + chunk)
            probs = probs_ref[0, j, rows, :]
            part = dprobs[rows]
            slope = probs * (part - jnp.sum(part * probs, -1, keepdims=True))
            for a in range(count // 128):
                slopes[group * (count // 128) + a, pl.ds(c * chunk * GROUP + j, chunk, stride=GROUP), :] = slope[:, a * 128 : a * 128 + 128]
            slope_parts.append((slope * scale).astype(jnp.bfloat16))
            prob_parts.append(probs.astype(jnp.bfloat16))
        slope_b = jnp.concatenate(slope_parts, 0)
        probs_b = jnp.concatenate(prob_parts, 0)
        dq = dq + jnp.dot(slope_b, only_head(k, j), preferred_element_type=jnp.float32)
        dk = dk + lax.dot_general(slope_b, only_head(q, j), over_rows, preferred_element_type=jnp.float32)
        dv = dv + lax.dot_general(probs_b, only_head(dattn, j), over_rows, preferred_element_type=jnp.float32)
    dq_ref[...] = dq.astype(dq_ref.dtype)
    dk_ref[...] = dk.astype(dk_ref.dtype)
    dv_ref[...] = dv.astype(dv_ref.dtype)

    @pl.when(group == pl.num_programs(1) - 1)
    def _():
        halves = count // 128
        groups = slopes.shape[0] // halves
        corner[...] = jnp.zeros_like(corner)

        def collect(i, carry):
            total = corner[...]
            for n in range(4):
                first = pl.multiple_of((i * 4 + n) * 8 * GROUP, 8 * GROUP)
                rows = pl.ds(first, 8 * GROUP)
                left = jnp.concatenate(
                    [
                        jnp.concatenate([slopes[g * halves + a, rows, :] for a in range(halves)], 1)
                        for g in range(groups)
                    ],
                    0,
                ).astype(jnp.bfloat16)
                first = pl.multiple_of((i * 4 + n) * 8 * buckets, 8 * buckets)
                right = onehot[pl.ds(first, 8 * buckets), :]
                total = total + lax.dot_general(
                    left, right, (((1,), (1,)), ((), ())), preferred_element_type=jnp.float32
                )
            corner[...] = total
            return carry

        lax.fori_loop(0, count // 32, collect, 0)
        shape = corner.shape
        node_row = lax.rem(lax.div(lax.broadcasted_iota(jnp.int32, shape, 0), GROUP), 8)
        node_col = lax.div(lax.broadcasted_iota(jnp.int32, shape, 1), buckets)
        kept = jnp.where(node_row == node_col, corner[...], 0.0)
        tall = []
        for g in range(groups):
            heads = kept[g * 8 * GROUP : g * 8 * GROUP + GROUP]
            for n in range(1, 8):
                heads = heads + kept[(g * 8 + n) * GROUP : (g * 8 + n) * GROUP + GROUP]
            tall.append(heads)
        bias_ref[0] = jnp.concatenate(tall, 0)


def attention_specs(count, width, heads):
    wide = width // heads * GROUP
    groups = heads // GROUP
    column = lambda part: pl.BlockSpec((count, wide), lambda e, g, part=part: (e, part * groups + g))
    probs = pl.BlockSpec((1, GROUP, count, count), lambda e, g: (e, g, 0, 0))
    spd = pl.BlockSpec((1, count, count), lambda e, g: (e, 0, 0))
    return column, probs, spd, groups


def attention_forward(qkv, bias):
    egos, heads, count, _ = bias.shape
    width = qkv.shape[1] // 3
    column, probs, _, groups = attention_specs(count, width, heads)
    return pl.pallas_call(
        attend_kernel,
        name="attend",
        grid=(egos, groups),
        out_shape=(
            jax.ShapeDtypeStruct((egos * count, width), jnp.bfloat16),
            jax.ShapeDtypeStruct((egos, heads, count, count), jnp.float32),
        ),
        in_specs=[column(0), column(1), column(2), probs],
        out_specs=(column(0), probs),
        compiler_params=pltpu.CompilerParams(vmem_limit_bytes=40 * 1024 * 1024),
    )(qkv, qkv, qkv, bias)


def attention_backward(qkv, dattn, probs, spd):
    egos, heads, count, _ = probs.shape
    width = qkv.shape[1] // 3
    column, probs_spec, spd_spec, groups = attention_specs(count, width, heads)
    flat = jax.ShapeDtypeStruct((egos * count, width), jnp.bfloat16)
    dq, dk, dv, bias = pl.pallas_call(
        attend_back_kernel,
        name="attend_back",
        grid=(egos, groups),
        out_shape=(flat, flat, flat, jax.ShapeDtypeStruct((egos, heads, 256), jnp.float32)),
        in_specs=[column(0), column(1), column(2), column(0), probs_spec, spd_spec],
        out_specs=(column(0), column(0), column(0), pl.BlockSpec((1, heads, 256), lambda e, g: (e, 0, 0))),
        scratch_shapes=[
            pltpu.VMEM((groups * (count // 128), count * GROUP, 128), jnp.float32),
            pltpu.VMEM((count * 32, count), jnp.bfloat16),
            pltpu.VMEM((groups * 8 * GROUP, 256), jnp.float32),
        ],
        compiler_params=pltpu.CompilerParams(vmem_limit_bytes=48 * 1024 * 1024),
    )(qkv, qkv, qkv, dattn, probs, spd)
    return dq, dk, dv, bias.reshape(egos, heads, 8, 32).sum((0, 2)).T


def slot_kernel(member_ref, dx_ref, out_ref):
    slots, tokens = out_ref.shape[1], dx_ref.shape[0]
    shape = (slots, tokens)
    hit = jnp.broadcast_to(member_ref[...], shape) == lax.broadcasted_iota(jnp.int32, shape, 0)
    placed = jnp.where(hit, 1.0, 0.0).astype(jnp.bfloat16)
    dx = dx_ref[...]
    high = dx.astype(jnp.bfloat16)
    low = (dx - high.astype(jnp.float32)).astype(jnp.bfloat16)
    total = jnp.dot(placed, high, preferred_element_type=jnp.float32) + jnp.dot(
        placed, low, preferred_element_type=jnp.float32
    )
    for c in range(out_ref.shape[0]):
        out_ref[c] = total[:, c * 128 : c * 128 + 128].astype(out_ref.dtype)


def slot_gradients(member_slot, dx, slots):
    tokens, width = dx.shape
    return pl.pallas_call(
        slot_kernel,
        name="slot_gradients",
        grid=(width // 256,),
        out_shape=jax.ShapeDtypeStruct((width // 128, slots, 128), jnp.bfloat16),
        in_specs=[pl.BlockSpec((1, tokens), lambda i: (0, 0)), pl.BlockSpec((tokens, 256), lambda i: (0, i))],
        out_specs=pl.BlockSpec((2, slots, 128), lambda i: (i, 0, 0)),
        compiler_params=pltpu.CompilerParams(vmem_limit_bytes=40 * 1024 * 1024),
    )(member_slot.reshape(1, tokens), dx)


def place_kernel(lists_ref, grads_ref, out_ref):
    block, entries = out_ref.shape[0], lists_ref.shape[1]
    base = pl.program_id(0) * block
    total = jnp.zeros(out_ref.shape, jnp.float32)
    step = 1024
    for a in range(0, entries, step):
        shape = (block, step)
        hit = jnp.broadcast_to(lists_ref[:, a : a + step], shape) == lax.broadcasted_iota(jnp.int32, shape, 0) + base
        total = total + jnp.dot(
            jnp.where(hit, 1.0, 0.0).astype(jnp.bfloat16), grads_ref[a : a + step], preferred_element_type=jnp.float32
        )
    out_ref[...] = total.astype(out_ref.dtype)


def place_gradients(lists, grads, rows):
    entries, width = grads.shape
    return pl.pallas_call(
        place_kernel,
        name="place_gradients",
        grid=(rows // 256,),
        out_shape=jax.ShapeDtypeStruct((rows, width), jnp.bfloat16),
        in_specs=[pl.BlockSpec((1, entries), lambda i: (0, 0)), pl.BlockSpec((entries, width), lambda i: (0, 0))],
        out_specs=pl.BlockSpec((256, width), lambda i: (i, 0)),
        compiler_params=pltpu.CompilerParams(vmem_limit_bytes=40 * 1024 * 1024),
    )(lists.reshape(1, entries), grads)


def coordinates():
    dp, store = lax.axis_index("dp"), lax.axis_index("store")
    return lax.div(dp, 2), lax.rem(dp, 2), lax.div(store, 4), lax.rem(store, 4)


def peer(y, core, x, z):
    return (y * 2 + core, x * 4 + z)


def along(axis, offset):
    y, core, x, z = coordinates()
    place = [y, x, z]
    place[axis] = lax.rem(place[axis] + offset, 4)
    return peer(place[0], core, place[1], place[2]), place[axis]


def reduce_kernel(
    g_down, g_up, g_out, g_q, g_k, g_v, small,
    o_qkv, o_out, o_up, o_down, o_small,
    own, got, part0, recv0, part1, recv1, part2, recv2, small_core, small_all,
    own_sem, core_send, core_recv, send, recv, sc_send, sc_recv, s_send, s_recv,
):
    y, core, x, z = coordinates()
    here = (y, x, z)
    other = peer(y, 1 - core, x, z)
    everyone = [other] + [along(a, k)[0] for a in range(3) for k in (1, 2, 3)]

    barrier = pltpu.get_barrier_semaphore()
    for device in everyone:
        pl.semaphore_signal(barrier, inc=1, device_id=device, device_id_type=MESH)
    pl.semaphore_wait(barrier, len(everyone))

    sources = [g_down, g_up, g_out, g_q, g_k, g_v]
    outs = [o_down, o_up, o_out] + [o_qkv] * 3
    columns = [0, 0, 0, 0, 1024, 2048]
    sends = []

    local, cross = [], []
    tiny = pltpu.make_async_remote_copy(
        src_ref=small, dst_ref=small_core, send_sem=sc_send, recv_sem=sc_recv,
        device_id=other, device_id_type=MESH)
    tiny.start()
    for j in range(PIECES):
        remote = pltpu.make_async_remote_copy(
            src_ref=sources[j].at[:, 1 - core], dst_ref=got.at[j],
            send_sem=core_send.at[j], recv_sem=core_recv.at[j],
            device_id=other, device_id_type=MESH)
        remote.start()
        cross.append(remote)
        keep = pltpu.make_async_copy(sources[j].at[:, core], own.at[j], own_sem.at[j])
        keep.start()
        local.append(keep)

    tiny.wait()

    def spread_small(axis):
        copies = []
        for k in (1, 2, 3):
            device, _ = along(axis, k)
            copy = pltpu.make_async_remote_copy(
                src_ref=small_all.at[axis, here[axis]], dst_ref=small_all.at[axis, here[axis]],
                send_sem=s_send.at[axis, k - 1], recv_sem=s_recv.at[axis, k - 1],
                device_id=device, device_id_type=MESH)
            copy.start()
            copies.append(copy)
        return copies

    def total_small(axis):
        return (small_all[axis, 0] + small_all[axis, 1]) + (small_all[axis, 2] + small_all[axis, 3])

    small_all[0, here[0]] = small[...] + small_core[...]
    tiny_copies = spread_small(0)

    def scatter(j, stage, part):
        order = ORDERS[j % 3]
        axis = order[stage]
        left = [a for a in (0, 1, 2) if a not in order[:stage]]
        where = left.index(axis)
        landing = (recv0, recv1, recv2)[stage]
        copies = []
        for k in (1, 2, 3):
            device, place = along(axis, k)
            block = (j,) + (slice(None),) * where + (place,)
            copy = pltpu.make_async_remote_copy(
                src_ref=part.at[block], dst_ref=landing.at[j, k - 1],
                send_sem=send.at[stage, j, k - 1], recv_sem=recv.at[stage, j, k - 1],
                device_id=device, device_id_type=MESH)
            copy.start()
            copies.append(copy)
        return copies

    flight = [None] * PIECES
    for j in range(PIECES):
        local[j].wait()
        cross[j].wait_recv()

        def add_cores(i, carry, j=j):
            yy, xx = lax.div(i, 4), lax.rem(i, 4)
            rows = pl.ds(pl.multiple_of(xx * 32, 32), 32)
            total = own[j, yy, rows, :].astype(jnp.float32) + got[j, yy, rows, :].astype(jnp.float32)
            for zz in range(4):
                mine = total[8 * zz : 8 * zz + 8]
                part0[j, yy, xx, zz] = jnp.concatenate([mine[:, :512], mine[:, 512:]], 0).astype(jnp.bfloat16)
            return carry

        lax.fori_loop(0, 16, add_cores, 0)
        flight[j] = scatter(j, 0, part0)

    for copy in tiny_copies:
        copy.wait()
    small_all[1, here[1]] = total_small(0)
    tiny_copies = spread_small(1)

    for j in range(PIECES):
        for copy in flight[j]:
            copy.wait_recv()
        sends += flight[j]
        axis = ORDERS[j % 3][0]

        def add_first(i, carry, j=j, axis=axis):
            a, b = lax.div(i, 4), lax.rem(i, 4)
            block = [a, b]
            block.insert(axis, here[axis])
            total = part0[(j,) + tuple(block)].astype(jnp.float32)
            for k in range(3):
                total = total + recv0[j, k, a, b].astype(jnp.float32)
            part1[j, a, b] = total.astype(jnp.bfloat16)
            return carry

        lax.fori_loop(0, 16, add_first, 0)
        flight[j] = scatter(j, 1, part1)

    for copy in tiny_copies:
        copy.wait()
    small_all[2, here[2]] = total_small(1)
    tiny_copies = spread_small(2)

    for j in range(PIECES):
        for copy in flight[j]:
            copy.wait_recv()
        sends += flight[j]
        order = ORDERS[j % 3]
        where = [a for a in (0, 1, 2) if a != order[0]].index(order[1])

        def add_second(i, carry, j=j, axis=order[1], where=where):
            block = [i]
            block.insert(where, here[axis])
            total = part1[(j,) + tuple(block)].astype(jnp.float32)
            for k in range(3):
                total = total + recv1[j, k, i].astype(jnp.float32)
            part2[j, i] = total.astype(jnp.bfloat16)
            return carry

        lax.fori_loop(0, 4, add_second, 0)
        flight[j] = scatter(j, 2, part2)

    for copy in tiny_copies:
        copy.wait()
    o_small[...] = total_small(2)

    for j in range(PIECES):
        for copy in flight[j]:
            copy.wait_recv()
        sends += flight[j]
        axis = ORDERS[j % 3][2]
        total = part2[j, here[axis]].astype(jnp.float32)
        for k in range(3):
            total = total + recv2[j, k].astype(jnp.float32)
        joined = jnp.concatenate([total[:8], total[8:]], 1).astype(jnp.bfloat16)
        outs[j][:, columns[j] : columns[j] + 1024] = joined

    for copy in cross + sends:
        copy.wait_send()


def reduce_gradients(gradients, small):
    bf16, f32 = jnp.bfloat16, jnp.float32
    hbm = pl.BlockSpec(memory_space=pl.ANY)
    vmem = pl.BlockSpec(memory_space=pltpu.VMEM)
    dma = pltpu.SemaphoreType.DMA
    split = lambda g: g.reshape(4, 2, 128, g.shape[1])
    return pl.pallas_call(
        reduce_kernel,
        name="reduce_gradients",
        out_shape=(
            jax.ShapeDtypeStruct((8, 3072), bf16),
            jax.ShapeDtypeStruct((8, 1024), bf16),
            jax.ShapeDtypeStruct((8, 1024), bf16),
            jax.ShapeDtypeStruct((8, 1024), bf16),
            jax.ShapeDtypeStruct(small.shape, f32),
        ),
        in_specs=[hbm] * PIECES + [vmem],
        out_specs=[vmem] * 5,
        scratch_shapes=[
            pltpu.VMEM((PIECES, 4, 128, 1024), bf16),
            pltpu.VMEM((PIECES, 4, 128, 1024), bf16),
            pltpu.VMEM((PIECES, 4, 4, 4, 16, 512), bf16),
            pltpu.VMEM((PIECES, 3, 4, 4, 16, 512), bf16),
            pltpu.VMEM((PIECES, 4, 4, 16, 512), bf16),
            pltpu.VMEM((PIECES, 3, 4, 16, 512), bf16),
            pltpu.VMEM((PIECES, 4, 16, 512), bf16),
            pltpu.VMEM((PIECES, 3, 16, 512), bf16),
            pltpu.VMEM(small.shape, f32),
            pltpu.VMEM((3, 4) + small.shape, f32),
            dma((PIECES,)),
            dma((PIECES,)),
            dma((PIECES,)),
            dma((3, PIECES, 3)),
            dma((3, PIECES, 3)),
            dma,
            dma,
            dma((3, 3)),
            dma((3, 3)),
        ],
        compiler_params=pltpu.CompilerParams(
            collective_id=0, has_side_effects=True, vmem_limit_bytes=40 * 1024 * 1024
        ),
    )(*[split(g) for g in gradients], small)


def body(
    node_table,
    touched,
    member_slot,
    distances,
    cotangent,
    w_qkv,
    w_out,
    w_up,
    w_down,
    gains,
    bias_table,
):
    bf16, f32 = jnp.bfloat16, jnp.float32
    both = ("dp", "store")
    shard_rows, width = node_table.shape
    owners, cap = touched.shape[1:]
    egos, count = member_slot.shape
    tokens, slots_held = egos * count, owners * cap
    dot = lambda a, b: jnp.dot(a, b, preferred_element_type=f32)
    back = lambda a, b: lax.dot_general(a, b, (((1,), (1,)), ((), ())), preferred_element_type=f32)
    weight = lambda a, b: lax.dot_general(
        a, b, (((0,), (0,)), ((), ())), preferred_element_type=f32
    ).astype(bf16)

    x, lists, bias = fetch(node_table, touched, member_slot, distances, bias_table)
    x = x.astype(f32)
    dout = cotangent.reshape(tokens, width)

    h1, x_hat, x_rstd = layer_normalize(x, gains[0])
    h1 = h1.astype(bf16)
    qkv = dot(h1, w_qkv).astype(bf16)
    attended, probs = attention_forward(qkv, bias)
    y = x + dot(attended, w_out)
    h2, y_hat, y_rstd = layer_normalize(y, gains[1])
    h2 = h2.astype(bf16)
    act, slope = gelu_parts(dot(h2, w_up))
    act = act.astype(bf16)
    layer_out = (y + dot(act, w_down)).astype(bf16)

    du = (back(dout, w_down) * slope).astype(bf16)
    dy, gain_two = layer_normalize_backward(back(du, w_up), gains[1], y_hat, y_rstd)
    dy = dout.astype(f32) + dy
    dyb = dy.astype(bf16)
    dattn = back(dyb, w_out).astype(bf16)
    dq, dk, dv, grad_bias = attention_backward(qkv, dattn, probs, distances)
    dh1 = (
        back(dq, w_qkv[:, :width])
        + back(dk, w_qkv[:, width : 2 * width])
        + back(dv, w_qkv[:, 2 * width :])
    )
    dx, gain_one = layer_normalize_backward(dh1, gains[0], x_hat, x_rstd)
    dx = dy + dx

    slot_grads = slot_gradients(member_slot, dx, slots_held)
    returned = lax.all_to_all(
        slot_grads.reshape(-1, cap, 128), both, split_axis=0, concat_axis=0, tiled=True
    )
    gradients = (
        weight(act, dout), weight(h2, du), weight(attended, dyb),
        weight(h1, dq), weight(h1, dk), weight(h1, dv),
    )
    small = jnp.concatenate(
        [gain_one.reshape(8, 128), gain_two.reshape(8, 128), grad_bias.reshape(8, 128)]
    )
    sum_qkv, sum_out, sum_up, sum_down, small = reduce_gradients(gradients, small)
    grad_table = place_gradients(lists, returned.reshape(-1, 128), shard_rows)
    return (
        layer_out.reshape(egos, count, width),
        grad_table,
        sum_qkv,
        sum_out,
        sum_up,
        sum_down,
        small[:16].reshape(2, width),
        small[16:].reshape(32, 32),
    )


def solution(mesh):
    in_specs = (
        P("store", None),
        P(("dp", "store"), None, None),
        P(("dp", "store"), None),
        P(("dp", "store"), None, None),
        P(("dp", "store"), None, None),
        P(),
        P(),
        P(),
        P(),
        P(),
        P(),
    )
    out_specs = (
        P(("dp", "store"), None, None),
        P("store", "dp"),
        P(("dp", "store"), None),
        P(("dp", "store"), None),
        P(("dp", "store"), None),
        P(("dp", "store"), None),
        P(),
        P(),
    )
    return jax.shard_map(body, mesh=mesh, in_specs=in_specs, out_specs=out_specs, check_vma=False)
```

```python
import math

import jax
import jax.numpy as jnp
from jax import lax
from jax.experimental import pallas as pl
from jax.experimental.pallas import tpu as pltpu
from jax.sharding import PartitionSpec as P

EPS = 1e-05
ROOT_HALF = 1.0 / math.sqrt(2.0)
ROOT_TWO_PI = 1.0 / math.sqrt(2.0 * math.pi)


def layer_normalize(value, gain):
    mean = jnp.mean(value, -1, keepdims=True)
    centred = value - mean
    rstd = lax.rsqrt(jnp.mean(centred * centred, -1, keepdims=True) + EPS)
    vhat = centred * rstd
    return (vhat * gain, vhat, rstd)


def layer_normalize_backward(grad, gain, vhat, rstd):
    scaled = grad * gain
    first = jnp.mean(scaled, -1, keepdims=True)
    second = jnp.mean(scaled * vhat, -1, keepdims=True)
    return (rstd * (scaled - first - vhat * second), jnp.sum(grad * vhat, 0))


def gelu_parts(upper):
    normal_cdf = 0.5 * (1.0 + jax.scipy.special.erf(upper * ROOT_HALF))
    activation_slope = normal_cdf + upper * jnp.exp(-0.5 * upper * upper) * ROOT_TWO_PI
    return (upper * normal_cdf, activation_slope)


MESH = pl.DeviceIdType.MESH
ORDERS = ((0, 1, 2), (1, 2, 0), (2, 0, 1))
PIECES = 3


def coordinates():
    dp, store = lax.axis_index("dp"), lax.axis_index("store")
    return lax.div(dp, 2), lax.rem(dp, 2), lax.div(store, 4), lax.rem(store, 4)


def peer(y, core, x, z):
    return (y * 2 + core, x * 4 + z)


def along(axis, offset):
    y, core, x, z = coordinates()
    place = [y, x, z]
    place[axis] = lax.rem(place[axis] + offset, 4)
    return peer(place[0], core, place[1], place[2]), place[axis]


def other_core():
    y, core, x, z = coordinates()
    return peer(y, 1 - core, x, z)


def meet(devices):
    barrier = pltpu.get_barrier_semaphore()
    for device in devices:
        pl.semaphore_signal(barrier, inc=1, device_id=device, device_id_type=MESH)
    pl.semaphore_wait(barrier, len(devices))


class Reducer:
    SCRATCH = (
        (PIECES, 4, 128, 1024), (PIECES, 4, 4, 4, 16, 512), (PIECES, 3, 4, 4, 16, 512), (PIECES, 4, 4, 16, 512),
        (PIECES, 3, 4, 16, 512), (PIECES, 4, 16, 512), (PIECES, 3, 16, 512),
    )
    SEMAPHORES = ((PIECES,), (PIECES,), (3, PIECES, 3), (3, PIECES, 3))

    @classmethod
    def scratch(cls):
        return [pltpu.VMEM(s, jnp.bfloat16) for s in cls.SCRATCH] + [
            pltpu.SemaphoreType.DMA(s) for s in cls.SEMAPHORES
        ]

    def __init__(self, refs, given, kept):
        (self.got, part0, recv0, part1, recv1, part2, recv2,
         self.core_send, self.core_recv, self.send, self.recv) = refs
        self.parts, self.landing = (part0, part1, part2), (recv0, recv1, recv2)
        self.given, self.kept = given, kept
        y, self.core, x, z = coordinates()
        self.here = (y, x, z)

    def cross(self, j):
        return pltpu.make_async_remote_copy(
            src_ref=self.given(j), dst_ref=self.got.at[j],
            send_sem=self.core_send.at[j], recv_sem=self.core_recv.at[j],
            device_id=other_core(), device_id_type=MESH)

    def spread(self, stage, j):
        order = ORDERS[j]
        axis = order[stage]
        where = [a for a in (0, 1, 2) if a not in order[:stage]].index(axis)
        copies = []
        for k in (1, 2, 3):
            device, place = along(axis, k)
            block = (j,) + (slice(None),) * where + (place,)
            copies.append(
                pltpu.make_async_remote_copy(
                    src_ref=self.parts[stage].at[block], dst_ref=self.landing[stage].at[j, k - 1],
                    send_sem=self.send.at[stage, j, k - 1], recv_sem=self.recv.at[stage, j, k - 1],
                    device_id=device, device_id_type=MESH)
            )
        return copies

    def launch(self, stage, j):
        for copy in self.spread(stage, j):
            copy.start()

    def add_cores(self, j):
        self.cross(j).wait_recv()

        def step(i, carry):
            yy, xx = lax.div(i, 4), lax.rem(i, 4)
            rows = pl.ds(pl.multiple_of(xx * 32, 32), 32)
            total = self.kept(j, yy, rows).astype(jnp.float32) + self.got[j, yy, rows, :].astype(jnp.float32)
            for zz in range(4):
                mine = total[8 * zz : 8 * zz + 8]
                self.parts[0][j, yy, xx, zz] = jnp.concatenate(
                    [mine[:, :512], mine[:, 512:]], 0
                ).astype(jnp.bfloat16)
            return carry

        lax.fori_loop(0, 16, step, 0)
        self.launch(0, j)

    def total(self, stage, j, block):
        order = ORDERS[j]
        where = [a for a in (0, 1, 2) if a not in order[:stage]].index(order[stage])
        index = list(block)
        index.insert(where, self.here[order[stage]])
        total = self.parts[stage][(j,) + tuple(index)].astype(jnp.float32)
        for k in range(3):
            total = total + self.landing[stage][(j, k) + tuple(block)].astype(jnp.float32)
        return total

    def add(self, stage, j):
        for copy in self.spread(stage, j):
            copy.wait_recv()

        def step(i, carry):
            block = (lax.div(i, 4), lax.rem(i, 4)) if stage == 0 else (i,)
            self.parts[stage + 1][(j,) + block] = self.total(stage, j, block).astype(jnp.bfloat16)
            return carry

        lax.fori_loop(0, 16 if stage == 0 else 4, step, 0)
        self.launch(stage + 1, j)

    def result(self, j):
        for copy in self.spread(2, j):
            copy.wait_recv()
        total = self.total(2, j, ())
        return jnp.concatenate([total[:8], total[8:]], 1).astype(jnp.bfloat16)

    def close(self):
        for j in range(PIECES):
            self.cross(j).wait_send()
            for stage in range(3):
                for copy in self.spread(stage, j):
                    copy.wait_send()


def torus_peers():
    return [other_core()] + [along(a, k)[0] for a in range(3) for k in (1, 2, 3)]


def halves(g):
    return g.reshape(4, 2, 128, g.shape[1])


LISTED = 128


def fetch_kernel(
    touched, members, table_hbm, spd, lookup,
    x_out, lists_out, bias_hbm,
    table, asked, lists, chosen, outgoing, slots, bias,
    table_sem, ask_send, ask_recv, list_send, list_recv, row_send, row_recv, bias_sem,
):
    dp, store = lax.axis_index("dp"), lax.axis_index("store")
    shards, groups = asked.shape[0], lists.shape[0]
    rows, width = table.shape
    cap = slots.shape[1] // 2
    half = width // 2
    egos, heads, count, _ = bias.shape
    turn = lambda here, k, size: lax.rem(here + k, size)
    owners = [(dp, turn(store, k, shards)) for k in range(shards)]
    copies_of_shard = [(turn(dp, k, groups), store) for k in range(groups)]

    load = pltpu.make_async_copy(table_hbm, table, table_sem)
    load.start()
    barrier = pltpu.get_barrier_semaphore()
    for device in owners[1:] + copies_of_shard[1:]:
        pl.semaphore_signal(barrier, inc=1, device_id=device, device_id_type=MESH)
    pl.semaphore_wait(barrier, shards + groups - 2)

    requests = []
    for k in range(1, shards):
        copy = pltpu.make_async_remote_copy(
            src_ref=touched.at[owners[k][1]], dst_ref=asked.at[store],
            send_sem=ask_send.at[k], recv_sem=ask_recv.at[k],
            device_id=owners[k], device_id_type=MESH)
        copy.start()
        requests.append(copy)
    asked[store] = touched[store]

    bias_copies = []

    def look_up(ego, first, many):
        def step(n, carry):
            at = pl.ds(pl.multiple_of(n * 8, 8), 8)
            for a in range(0, count, 128):
                distance = spd[ego, at, a : a + 128]
                for h in range(first, first + many):
                    row = jnp.broadcast_to(lookup[h : h + 1, :], (8, 128))
                    bias[ego, h, at, a : a + 128] = jnp.take_along_axis(
                        row, distance, axis=1, mode="promise_in_bounds"
                    )
            return carry

        lax.fori_loop(0, count // 8, step, 0, unroll=2)
        part = pl.ds(first, many)
        copy = pltpu.make_async_copy(
            bias.at[ego, part], bias_hbm.at[ego, part], bias_sem.at[len(bias_copies)])
        copy.start()
        bias_copies.append(copy)

    look_up(0, 0, 8)
    for copy in requests:
        copy.wait_recv()
    shared = []
    for k in range(1, groups):
        copy = pltpu.make_async_remote_copy(
            src_ref=asked, dst_ref=lists.at[dp],
            send_sem=list_send.at[k], recv_sem=list_recv.at[k],
            device_id=copies_of_shard[k], device_id_type=MESH)
        copy.start()
        shared.append(copy)
    lists[dp] = asked[...]

    order = list(range(1, shards)) + [0]
    turned = jnp.concatenate(
        [asked[owners[k][1]] for k in order] + [jnp.full((LISTED - shards, LISTED), -1, jnp.int32)], 0
    ).T
    for p in range(0, shards, 2):
        pair = jnp.concatenate([turned[:cap, p : p + 1], turned[:cap, p + 1 : p + 2]], 0)
        shape = (2 * cap, rows)
        hit = jnp.broadcast_to(pair, shape) == lax.broadcasted_iota(jnp.int32, shape, 1)
        chosen[p * cap : (p + 2) * cap, :] = jnp.where(hit, 1.0, 0.0).astype(jnp.bfloat16)
    load.wait()
    sent = []
    for first in range(0, shards, 4):
        picks = chosen[first * cap : (first + 4) * cap, :]
        left = jnp.dot(picks, table[:, :half], preferred_element_type=jnp.float32)
        right = jnp.dot(picks, table[:, half:], preferred_element_type=jnp.float32)
        for i in range(4):
            k = order[first + i]
            mine = slice(i * cap, i * cap + cap)
            block = jnp.concatenate([left[mine], right[mine]], 0).astype(jnp.bfloat16)
            if k == 0:
                slots[store] = block
                continue
            outgoing[k] = block
            copy = pltpu.make_async_remote_copy(
                src_ref=outgoing.at[k], dst_ref=slots.at[store],
                send_sem=row_send.at[k], recv_sem=row_recv.at[k],
                device_id=owners[k], device_id_type=MESH)
            copy.start()
            sent.append(copy)

    look_up(0, 8, heads - 8)
    look_up(1, 0, heads)
    for copy in sent:
        copy.wait_recv()
    tokens = members.shape[0]
    shape = (tokens, shards * 2 * cap)
    held = slots[...].reshape(shards * 2 * cap, half)
    places = lax.broadcasted_iota(jnp.int32, shape, 1)
    for part in range(2):
        hit = jnp.broadcast_to(members[...] + part * cap, shape) == places
        x_out[:, part * half : part * half + half] = jnp.dot(
            jnp.where(hit, 1.0, 0.0).astype(jnp.bfloat16), held, preferred_element_type=jnp.float32
        ).astype(x_out.dtype)
    for copy in shared:
        copy.wait()
    lists_out[...] = lists[...]
    for copy in requests + sent:
        copy.wait_send()
    for copy in bias_copies:
        copy.wait()


def fetch(node_table, touched, member_slot, spd, table):
    bf16, f32, i32 = jnp.bfloat16, jnp.float32, jnp.int32
    _, shards, cap = touched.shape
    groups = lax.axis_size("dp")
    egos, count = member_slot.shape
    heads = table.shape[1]
    rows, width = node_table.shape
    lookup = jnp.pad((table * LOG2E).T, ((0, 0), (0, 128 - table.shape[0])))
    listed = jnp.pad(
        touched.reshape(shards, 1, cap), ((0, 0), (0, 0), (0, LISTED - cap)), constant_values=-1
    )
    members = (member_slot + cap * lax.div(member_slot, cap)).reshape(egos * count, 1)
    hbm = pl.BlockSpec(memory_space=pl.ANY)
    vmem = pl.BlockSpec(memory_space=pltpu.VMEM)
    dma = pltpu.SemaphoreType.DMA
    x, lists, bias = pl.pallas_call(
        fetch_kernel,
        name="fetch",
        out_shape=(
            jax.ShapeDtypeStruct((egos * count, width), bf16),
            jax.ShapeDtypeStruct((groups, shards, 1, LISTED), i32),
            jax.ShapeDtypeStruct((egos, heads, count, count), f32),
        ),
        in_specs=[vmem, vmem, hbm, vmem, vmem],
        out_specs=(vmem, vmem, hbm),
        scratch_shapes=[
            pltpu.VMEM((rows, width), bf16),
            pltpu.VMEM((shards, 1, LISTED), i32),
            pltpu.VMEM((groups, shards, 1, LISTED), i32),
            pltpu.VMEM((shards * cap, rows), bf16),
            pltpu.VMEM((shards, 2 * cap, width // 2), bf16),
            pltpu.VMEM((shards, 2 * cap, width // 2), bf16),
            pltpu.VMEM((egos, heads, count, count), f32),
            dma,
            dma((shards,)),
            dma((shards,)),
            dma((groups,)),
            dma((groups,)),
            dma((shards,)),
            dma((shards,)),
            dma((3,)),
        ],
        compiler_params=pltpu.CompilerParams(
            collective_id=1, has_side_effects=True, vmem_limit_bytes=48 * 1024 * 1024
        ),
    )(listed, members, node_table, spd, lookup)
    return x, lists[:, :, 0, :], bias


GROUP = 8
LOG2E = math.log2(math.e)


def head_mask(rows, width, head):
    lanes = lax.broadcasted_iota(jnp.int32, (rows, width), 1)
    return lax.div(lanes, width // GROUP) == head


def only_head(value, head):
    return jnp.where(head_mask(value.shape[0], value.shape[1], head), value, jnp.zeros((), value.dtype))


def attend_kernel(q_ref, k_ref, v_ref, bias_ref, mixed_ref, probs_ref):
    count = q_ref.shape[0]
    head_width = q_ref.shape[1] // GROUP
    scale = LOG2E * head_width ** (-0.5)
    chunk = 32
    q, k, v = q_ref[...], k_ref[...], v_ref[...]
    mixed = jnp.zeros(q.shape, jnp.float32)
    for j in range(GROUP):
        raw = lax.dot_general(
            q, only_head(k, j), (((1,), (1,)), ((), ())), preferred_element_type=jnp.float32
        )
        parts = []
        for c in range(count // chunk):
            rows = slice(c * chunk, c * chunk + chunk)
            logits = raw[rows] * scale + bias_ref[0, j, rows, :]
            power = jnp.exp2(logits - jnp.max(logits, -1, keepdims=True))
            probs = power * (1.0 / jnp.sum(power, -1, keepdims=True))
            probs_ref[0, j, rows, :] = probs
            parts.append(probs.astype(jnp.bfloat16))
        mixed = mixed + jnp.dot(
            jnp.concatenate(parts, 0), only_head(v, j), preferred_element_type=jnp.float32
        )
    mixed_ref[...] = mixed.astype(mixed_ref.dtype)


def attend_back_kernel(
    q_ref, k_ref, v_ref, dattn_ref, probs_ref, spd_ref, g_down, g_up, g_out,
    dq_ref, dk_ref, dv_ref, bias_ref, o_down, o_up, o_out, slopes, onehot, corner, own, own_sem, *rest,
):
    ego, group = pl.program_id(0), pl.program_id(1)
    step = ego * pl.num_programs(1) + group
    sources, sums = (g_down, g_up, g_out), (o_down, o_up, o_out)
    core = lax.rem(lax.axis_index("dp"), 2)
    reducer = Reducer(
        rest, lambda j: sources[j].at[:, 1 - core], lambda j, yy, rows: own[j, yy, rows, :]
    )
    keep = lambda j: pltpu.make_async_copy(sources[j].at[:, core], own.at[j], own_sem.at[j])

    @pl.when(step == 0)
    def _():
        for j in range(PIECES):
            keep(j).start()
        meet(torus_peers())
        for j in range(PIECES):
            reducer.cross(j).start()

    @pl.when(step == 1)
    def _():
        for j in range(PIECES):
            keep(j).wait()
            reducer.add_cores(j)

    @pl.when(step == 4)
    def _():
        for j in range(PIECES):
            reducer.add(0, j)

    @pl.when(step == 5)
    def _():
        for j in range(PIECES):
            reducer.add(1, j)

    @pl.when(step == 6)
    def _():
        for j in range(PIECES):
            sums[j][...] = reducer.result(j)
        reducer.close()

    count, width = q_ref.shape
    scale = (width // GROUP) ** (-0.5)
    buckets = 32
    chunk = 32
    q, k, v, dattn = q_ref[...], k_ref[...], v_ref[...], dattn_ref[...]

    @pl.when(group == 0)
    def _():
        def fill(n, carry):
            row = jnp.broadcast_to(spd_ref[0, pl.ds(n, 1), :], (buckets, count))
            hit = row == lax.broadcasted_iota(jnp.int32, (buckets, count), 0)
            onehot[pl.ds(pl.multiple_of(n * buckets, buckets), buckets), :] = jnp.where(hit, 1.0, 0.0).astype(jnp.bfloat16)
            return carry

        lax.fori_loop(0, count, fill, 0, unroll=8)

    dq = jnp.zeros((count, width), jnp.float32)
    dk = jnp.zeros((count, width), jnp.float32)
    dv = jnp.zeros((count, width), jnp.float32)
    over_rows = (((0,), (0,)), ((), ()))
    for j in range(GROUP):
        dprobs = lax.dot_general(
            dattn, only_head(v, j), (((1,), (1,)), ((), ())), preferred_element_type=jnp.float32
        )
        slope_parts, prob_parts = [], []
        for c in range(count // chunk):
            rows = slice(c * chunk, c * chunk + chunk)
            probs = probs_ref[0, j, rows, :]
            part = dprobs[rows]
            slope = probs * (part - jnp.sum(part * probs, -1, keepdims=True))
            for a in range(count // 128):
                slopes[group * (count // 128) + a, pl.ds(c * chunk * GROUP + j, chunk, stride=GROUP), :] = slope[:, a * 128 : a * 128 + 128]
            slope_parts.append((slope * scale).astype(jnp.bfloat16))
            prob_parts.append(probs.astype(jnp.bfloat16))
        slope_b = jnp.concatenate(slope_parts, 0)
        probs_b = jnp.concatenate(prob_parts, 0)
        dq = dq + jnp.dot(slope_b, only_head(k, j), preferred_element_type=jnp.float32)
        dk = dk + lax.dot_general(slope_b, only_head(q, j), over_rows, preferred_element_type=jnp.float32)
        dv = dv + lax.dot_general(probs_b, only_head(dattn, j), over_rows, preferred_element_type=jnp.float32)
    dq_ref[...] = dq.astype(dq_ref.dtype)
    dk_ref[...] = dk.astype(dk_ref.dtype)
    dv_ref[...] = dv.astype(dv_ref.dtype)

    @pl.when(group == pl.num_programs(1) - 1)
    def _():
        halves = count // 128
        groups = slopes.shape[0] // halves
        corner[...] = jnp.zeros_like(corner)

        def collect(i, carry):
            total = corner[...]
            for n in range(4):
                first = pl.multiple_of((i * 4 + n) * 8 * GROUP, 8 * GROUP)
                rows = pl.ds(first, 8 * GROUP)
                left = jnp.concatenate(
                    [
                        jnp.concatenate([slopes[g * halves + a, rows, :] for a in range(halves)], 1)
                        for g in range(groups)
                    ],
                    0,
                ).astype(jnp.bfloat16)
                first = pl.multiple_of((i * 4 + n) * 8 * buckets, 8 * buckets)
                right = onehot[pl.ds(first, 8 * buckets), :]
                total = total + lax.dot_general(
                    left, right, (((1,), (1,)), ((), ())), preferred_element_type=jnp.float32
                )
            corner[...] = total
            return carry

        lax.fori_loop(0, count // 32, collect, 0)
        shape = corner.shape
        node_row = lax.rem(lax.div(lax.broadcasted_iota(jnp.int32, shape, 0), GROUP), 8)
        node_col = lax.div(lax.broadcasted_iota(jnp.int32, shape, 1), buckets)
        kept = jnp.where(node_row == node_col, corner[...], 0.0)
        tall = []
        for g in range(groups):
            heads = kept[g * 8 * GROUP : g * 8 * GROUP + GROUP]
            for n in range(1, 8):
                heads = heads + kept[(g * 8 + n) * GROUP : (g * 8 + n) * GROUP + GROUP]
            tall.append(heads)
        bias_ref[0] = jnp.concatenate(tall, 0)


def attention_specs(count, width, heads):
    wide = width // heads * GROUP
    groups = heads // GROUP
    column = lambda part: pl.BlockSpec((count, wide), lambda e, g, part=part: (e, part * groups + g))
    probs = pl.BlockSpec((1, GROUP, count, count), lambda e, g: (e, g, 0, 0))
    spd = pl.BlockSpec((1, count, count), lambda e, g: (e, 0, 0))
    return column, probs, spd, groups


def attention_forward(qkv, bias):
    egos, heads, count, _ = bias.shape
    width = qkv.shape[1] // 3
    column, probs, _, groups = attention_specs(count, width, heads)
    return pl.pallas_call(
        attend_kernel,
        name="attend",
        grid=(egos, groups),
        out_shape=(
            jax.ShapeDtypeStruct((egos * count, width), jnp.bfloat16),
            jax.ShapeDtypeStruct((egos, heads, count, count), jnp.float32),
        ),
        in_specs=[column(0), column(1), column(2), probs],
        out_specs=(column(0), probs),
        compiler_params=pltpu.CompilerParams(vmem_limit_bytes=40 * 1024 * 1024),
    )(qkv, qkv, qkv, bias)


def attention_backward(qkv, dattn, probs, spd, gradients):
    egos, heads, count, _ = probs.shape
    width = qkv.shape[1] // 3
    column, probs_spec, spd_spec, groups = attention_specs(count, width, heads)
    flat = jax.ShapeDtypeStruct((egos * count, width), jnp.bfloat16)
    summed = jax.ShapeDtypeStruct((8, 1024), jnp.bfloat16)
    whole = pl.BlockSpec((8, 1024), lambda e, g: (0, 0))
    dq, dk, dv, bias, *sums = pl.pallas_call(
        attend_back_kernel,
        name="attend_back",
        grid=(egos, groups),
        out_shape=(flat, flat, flat, jax.ShapeDtypeStruct((egos, heads, 256), jnp.float32)) + (summed,) * 3,
        in_specs=[column(0), column(1), column(2), column(0), probs_spec, spd_spec]
        + [pl.BlockSpec(memory_space=pl.ANY)] * PIECES,
        out_specs=(column(0), column(0), column(0), pl.BlockSpec((1, heads, 256), lambda e, g: (e, 0, 0)))
        + (whole,) * 3,
        scratch_shapes=[
            pltpu.VMEM((groups * (count // 128), count * GROUP, 128), jnp.float32),
            pltpu.VMEM((count * 32, count), jnp.bfloat16),
            pltpu.VMEM((groups * 8 * GROUP, 256), jnp.float32),
            pltpu.VMEM((PIECES, 4, 128, 1024), jnp.bfloat16),
            pltpu.SemaphoreType.DMA((PIECES,)),
        ]
        + Reducer.scratch(),
        compiler_params=pltpu.CompilerParams(
            collective_id=2, has_side_effects=True, vmem_limit_bytes=48 * 1024 * 1024
        ),
    )(qkv, qkv, qkv, dattn, probs, spd, *[halves(g) for g in gradients])
    return dq, dk, dv, bias.reshape(egos, heads, 8, 32).sum((0, 2)).T, sums


def slot_kernel(member_ref, dx_ref, out_ref):
    slots, tokens = out_ref.shape[1], dx_ref.shape[0]
    shape = (slots, tokens)
    hit = jnp.broadcast_to(member_ref[...], shape) == lax.broadcasted_iota(jnp.int32, shape, 0)
    placed = jnp.where(hit, 1.0, 0.0).astype(jnp.bfloat16)
    dx = dx_ref[...]
    high = dx.astype(jnp.bfloat16)
    low = (dx - high.astype(jnp.float32)).astype(jnp.bfloat16)
    total = jnp.dot(placed, high, preferred_element_type=jnp.float32) + jnp.dot(
        placed, low, preferred_element_type=jnp.float32
    )
    for c in range(out_ref.shape[0]):
        out_ref[c] = total[:, c * 128 : c * 128 + 128].astype(out_ref.dtype)


def slot_gradients(member_slot, dx, slots):
    tokens, width = dx.shape
    return pl.pallas_call(
        slot_kernel,
        name="slot_gradients",
        grid=(width // 256,),
        out_shape=jax.ShapeDtypeStruct((width // 128, slots, 128), jnp.bfloat16),
        in_specs=[pl.BlockSpec((1, tokens), lambda i: (0, 0)), pl.BlockSpec((tokens, 256), lambda i: (0, i))],
        out_specs=pl.BlockSpec((2, slots, 128), lambda i: (i, 0, 0)),
        compiler_params=pltpu.CompilerParams(vmem_limit_bytes=40 * 1024 * 1024),
    )(member_slot.reshape(1, tokens), dx)


def finish_kernel(
    slot_grads, h1, dq, dk, dv, lists, small,
    o_qkv, o_small, o_table,
    by_column, by_owner, turned, grads, small_core, small_all, *rest,
):
    reducer = Reducer(
        rest[:-8],
        lambda j: grads.at[j, :, 1 - lax.rem(lax.axis_index("dp"), 2)],
        lambda j, yy, rows: grads[j, yy, lax.rem(lax.axis_index("dp"), 2), rows, :],
    )
    sc_send, sc_recv, s_send, s_recv, a_send, a_recv, b_send, b_recv = rest[-8:]
    dp, store = lax.axis_index("dp"), lax.axis_index("store")
    groups, owners = by_column.shape[0], by_owner.shape[0]
    columns = [(lax.rem(dp + k, groups), store) for k in range(groups)]
    shards = [(dp, lax.rem(store + k, owners)) for k in range(owners)]
    here = reducer.here
    meet(columns[1:] + shards[1:])

    to_columns = []
    for k in range(1, groups):
        copy = pltpu.make_async_remote_copy(
            src_ref=slot_grads.at[columns[k][0]], dst_ref=by_column.at[dp],
            send_sem=a_send.at[k], recv_sem=a_recv.at[k], device_id=columns[k], device_id_type=MESH)
        copy.start()
        to_columns.append(copy)
    tiny = pltpu.make_async_remote_copy(
        src_ref=small, dst_ref=small_core, send_sem=sc_send, recv_sem=sc_recv,
        device_id=other_core(), device_id_type=MESH)
    tiny.start()
    by_column[dp] = slot_grads[dp]

    def spread_small(axis):
        copies = []
        for k in (1, 2, 3):
            copy = pltpu.make_async_remote_copy(
                src_ref=small_all.at[axis, here[axis]], dst_ref=small_all.at[axis, here[axis]],
                send_sem=s_send.at[axis, k - 1], recv_sem=s_recv.at[axis, k - 1],
                device_id=along(axis, k)[0], device_id_type=MESH)
            copy.start()
            copies.append(copy)
        return copies

    def total_small(axis):
        return (small_all[axis, 0] + small_all[axis, 1]) + (small_all[axis, 2] + small_all[axis, 3])

    turned[...] = h1[...].T
    for j, part in enumerate((dq, dk, dv)):

        def multiply(i, carry, j=j, part=part):
            yy, core = lax.div(i, 2), lax.rem(i, 2)
            rows = pl.ds(pl.multiple_of(i * 128, 128), 128)
            grads[j, yy, core] = jnp.dot(
                turned[rows, :], part[...], preferred_element_type=jnp.float32
            ).astype(jnp.bfloat16)
            return carry

        lax.fori_loop(0, 8, multiply, 0)
        reducer.cross(j).start()

    for copy in to_columns:
        copy.wait_recv()
    to_owners = []
    for k in range(1, owners):
        copy = pltpu.make_async_remote_copy(
            src_ref=by_column.at[:, shards[k][1]], dst_ref=by_owner.at[store],
            send_sem=b_send.at[k], recv_sem=b_recv.at[k], device_id=shards[k], device_id_type=MESH)
        copy.start()
        to_owners.append(copy)
    by_owner[store] = by_column[:, store]

    tiny.wait()
    small_all[0, here[0]] = small[...] + small_core[...]
    tiny_copies = spread_small(0)
    for j in range(PIECES):
        reducer.add_cores(j)
    for copy in tiny_copies:
        copy.wait()
    small_all[1, here[1]] = total_small(0)
    tiny_copies = spread_small(1)
    for copy in to_owners:
        copy.wait_recv()

    entries = lists.shape[1]
    pairs = owners // lists.shape[0]

    def place(i, carry):
        base = i * 256
        total = jnp.zeros((256, 128), jnp.float32)
        for a in range(lists.shape[0]):
            shape = (256, entries)
            hit = jnp.broadcast_to(lists[a : a + 1, :], shape) == lax.broadcasted_iota(jnp.int32, shape, 0) + base
            total = total + jnp.dot(
                jnp.where(hit, 1.0, 0.0).astype(jnp.bfloat16),
                by_owner[pairs * a : pairs * (a + 1)].reshape(entries, 128),
                preferred_element_type=jnp.float32,
            )
        o_table[pl.ds(pl.multiple_of(base, 256), 256), :] = total.astype(jnp.bfloat16)
        return carry

    blocks = o_table.shape[0] // 256
    first = blocks // 4
    lax.fori_loop(0, first, place, 0)
    for j in range(PIECES):
        reducer.add(0, j)
    for copy in tiny_copies:
        copy.wait()
    small_all[2, here[2]] = total_small(1)
    tiny_copies = spread_small(2)
    lax.fori_loop(first, first + blocks // 2, place, 0)
    for j in range(PIECES):
        reducer.add(1, j)
    lax.fori_loop(first + blocks // 2, blocks, place, 0)
    for copy in tiny_copies:
        copy.wait()
    o_small[...] = total_small(2)
    for j in range(PIECES):
        o_qkv[:, j * 1024 : j * 1024 + 1024] = reducer.result(j)
    reducer.close()
    for copy in to_columns + to_owners:
        copy.wait_send()


def finish(slot_grads, h1, dq, dk, dv, lists, small, rows):
    bf16, f32 = jnp.bfloat16, jnp.float32
    groups, owners = slot_grads.shape[:2]
    vmem = pl.BlockSpec(memory_space=pltpu.VMEM)
    dma = pltpu.SemaphoreType.DMA
    return pl.pallas_call(
        finish_kernel,
        name="finish",
        out_shape=(
            jax.ShapeDtypeStruct((8, 3072), bf16),
            jax.ShapeDtypeStruct(small.shape, f32),
            jax.ShapeDtypeStruct((rows, 128), bf16),
        ),
        in_specs=[vmem] * 7,
        out_specs=[vmem] * 3,
        scratch_shapes=[
            pltpu.VMEM(slot_grads.shape, bf16),
            pltpu.VMEM((owners, groups) + slot_grads.shape[2:], bf16),
            pltpu.VMEM((h1.shape[1], h1.shape[0]), bf16),
            pltpu.VMEM((PIECES, 4, 2, 128, 1024), bf16),
            pltpu.VMEM(small.shape, f32),
            pltpu.VMEM((3, 4) + small.shape, f32),
        ]
        + Reducer.scratch()
        + [dma, dma, dma((3, 3)), dma((3, 3)), dma((groups,)), dma((groups,)), dma((owners,)), dma((owners,))],
        compiler_params=pltpu.CompilerParams(
            collective_id=0, has_side_effects=True, vmem_limit_bytes=48 * 1024 * 1024
        ),
    )(slot_grads, h1, dq, dk, dv, lists, small)


def body(
    node_table,
    touched,
    member_slot,
    distances,
    cotangent,
    w_qkv,
    w_out,
    w_up,
    w_down,
    gains,
    bias_table,
):
    bf16, f32 = jnp.bfloat16, jnp.float32
    shard_rows, width = node_table.shape
    owners, cap = touched.shape[1:]
    egos, count = member_slot.shape
    tokens = egos * count
    dot = lambda a, b: jnp.dot(a, b, preferred_element_type=f32)
    back = lambda a, b: lax.dot_general(a, b, (((1,), (1,)), ((), ())), preferred_element_type=f32)
    weight = lambda a, b: lax.dot_general(
        a, b, (((0,), (0,)), ((), ())), preferred_element_type=f32
    ).astype(bf16)

    x, lists, bias = fetch(node_table, touched, member_slot, distances, bias_table)
    x = x.astype(f32)
    dout = cotangent.reshape(tokens, width)

    h1, x_hat, x_rstd = layer_normalize(x, gains[0])
    h1 = h1.astype(bf16)
    qkv = dot(h1, w_qkv).astype(bf16)
    attended, probs = attention_forward(qkv, bias)
    y = x + dot(attended, w_out)
    h2, y_hat, y_rstd = layer_normalize(y, gains[1])
    h2 = h2.astype(bf16)
    act, slope = gelu_parts(dot(h2, w_up))
    act = act.astype(bf16)
    layer_out = (y + dot(act, w_down)).astype(bf16)

    du = (back(dout, w_down) * slope).astype(bf16)
    dy, gain_two = layer_normalize_backward(back(du, w_up), gains[1], y_hat, y_rstd)
    dy = dout.astype(f32) + dy
    dyb = dy.astype(bf16)
    dattn = back(dyb, w_out).astype(bf16)
    dq, dk, dv, grad_bias, (sum_down, sum_up, sum_out) = attention_backward(
        qkv, dattn, probs, distances, (weight(act, dout), weight(h2, du), weight(attended, dyb))
    )
    dh1 = (
        back(dq, w_qkv[:, :width])
        + back(dk, w_qkv[:, width : 2 * width])
        + back(dv, w_qkv[:, 2 * width :])
    )
    dx, gain_one = layer_normalize_backward(dh1, gains[0], x_hat, x_rstd)
    dx = dy + dx

    padded = -(-cap // 16) * 16
    member = member_slot + (padded - cap) * lax.div(member_slot, cap)
    slot_grads = slot_gradients(member, dx, owners * padded).reshape(-1, owners, padded, 128)
    entries = lists[:, :, :padded].transpose(1, 0, 2).reshape(owners // 2, -1)
    small = jnp.concatenate(
        [gain_one.reshape(8, 128), gain_two.reshape(8, 128), grad_bias.reshape(8, 128)]
    )
    sum_qkv, small, grad_table = finish(slot_grads, h1, dq, dk, dv, entries, small, shard_rows)
    return (
        layer_out.reshape(egos, count, width),
        grad_table,
        sum_qkv,
        sum_out,
        sum_up,
        sum_down,
        small[:16].reshape(2, width),
        small[16:].reshape(32, 32),
    )


def solution(mesh):
    in_specs = (
        P("store", None),
        P(("dp", "store"), None, None),
        P(("dp", "store"), None),
        P(("dp", "store"), None, None),
        P(("dp", "store"), None, None),
        P(),
        P(),
        P(),
        P(),
        P(),
        P(),
    )
    out_specs = (
        P(("dp", "store"), None, None),
        P("store", "dp"),
        P(("dp", "store"), None),
        P(("dp", "store"), None),
        P(("dp", "store"), None),
        P(("dp", "store"), None),
        P(),
        P(),
    )
    return jax.shard_map(body, mesh=mesh, in_specs=in_specs, out_specs=out_specs, check_vma=False)
```

```python
import math

import jax
import jax.numpy as jnp
from jax import lax
from jax.experimental import pallas as pl
from jax.experimental.pallas import tpu as pltpu
from jax.sharding import PartitionSpec as P

EPS = 1e-05
ROOT_HALF = 1.0 / math.sqrt(2.0)
ROOT_TWO_PI = 1.0 / math.sqrt(2.0 * math.pi)


def layer_normalize(value, gain):
    mean = jnp.mean(value, -1, keepdims=True)
    centred = value - mean
    rstd = lax.rsqrt(jnp.mean(centred * centred, -1, keepdims=True) + EPS)
    vhat = centred * rstd
    return (vhat * gain, vhat, rstd)


def layer_normalize_backward(grad, gain, vhat, rstd):
    scaled = grad * gain
    first = jnp.mean(scaled, -1, keepdims=True)
    second = jnp.mean(scaled * vhat, -1, keepdims=True)
    return (rstd * (scaled - first - vhat * second), jnp.sum(grad * vhat, 0))


def gelu_parts(upper):
    normal_cdf = 0.5 * (1.0 + jax.scipy.special.erf(upper * ROOT_HALF))
    activation_slope = normal_cdf + upper * jnp.exp(-0.5 * upper * upper) * ROOT_TWO_PI
    return (upper * normal_cdf, activation_slope)


MESH = pl.DeviceIdType.MESH
ORDERS = ((0, 1, 2), (1, 2, 0), (2, 0, 1))
PIECES = 3


def coordinates():
    dp, store = lax.axis_index("dp"), lax.axis_index("store")
    return lax.div(dp, 2), lax.rem(dp, 2), lax.div(store, 4), lax.rem(store, 4)


def peer(y, core, x, z):
    return (y * 2 + core, x * 4 + z)


def along(axis, offset):
    y, core, x, z = coordinates()
    place = [y, x, z]
    place[axis] = lax.rem(place[axis] + offset, 4)
    return peer(place[0], core, place[1], place[2]), place[axis]


def other_core():
    y, core, x, z = coordinates()
    return peer(y, 1 - core, x, z)


def signal_meet(devices):
    barrier = pltpu.get_barrier_semaphore()
    for device in devices:
        pl.semaphore_signal(barrier, inc=1, device_id=device, device_id_type=MESH)


def wait_meet(devices):
    pl.semaphore_wait(pltpu.get_barrier_semaphore(), len(devices))


class Reducer:
    SCRATCH = (
        (PIECES, 4, 128, 1024), (PIECES, 4, 4, 4, 16, 512), (PIECES, 3, 4, 4, 16, 512), (PIECES, 4, 4, 16, 512),
        (PIECES, 3, 4, 16, 512), (PIECES, 4, 16, 512), (PIECES, 3, 16, 512),
    )
    SEMAPHORES = ((PIECES,), (PIECES,), (3, PIECES, 3), (3, PIECES, 3))

    @classmethod
    def scratch(cls):
        return [pltpu.VMEM(s, jnp.bfloat16) for s in cls.SCRATCH] + [
            pltpu.SemaphoreType.DMA(s) for s in cls.SEMAPHORES
        ]

    def __init__(self, refs, given, kept):
        (self.got, part0, recv0, part1, recv1, part2, recv2,
         self.core_send, self.core_recv, self.send, self.recv) = refs
        self.parts, self.landing = (part0, part1, part2), (recv0, recv1, recv2)
        self.given, self.kept = given, kept
        y, self.core, x, z = coordinates()
        self.here = (y, x, z)

    def cross(self, j):
        return pltpu.make_async_remote_copy(
            src_ref=self.given(j), dst_ref=self.got.at[j],
            send_sem=self.core_send.at[j], recv_sem=self.core_recv.at[j],
            device_id=other_core(), device_id_type=MESH)

    def spread(self, stage, j):
        order = ORDERS[j]
        axis = order[stage]
        where = [a for a in (0, 1, 2) if a not in order[:stage]].index(axis)
        copies = []
        for k in (1, 2, 3):
            device, place = along(axis, k)
            block = (j,) + (slice(None),) * where + (place,)
            copies.append(
                pltpu.make_async_remote_copy(
                    src_ref=self.parts[stage].at[block], dst_ref=self.landing[stage].at[j, k - 1],
                    send_sem=self.send.at[stage, j, k - 1], recv_sem=self.recv.at[stage, j, k - 1],
                    device_id=device, device_id_type=MESH)
            )
        return copies

    def launch(self, stage, j):
        for copy in self.spread(stage, j):
            copy.start()

    def add_cores(self, j):
        self.cross(j).wait_recv()

        def step(i, carry):
            yy, xx = lax.div(i, 4), lax.rem(i, 4)
            rows = pl.ds(pl.multiple_of(xx * 32, 32), 32)
            total = self.kept(j, yy, rows).astype(jnp.float32) + self.got[j, yy, rows, :].astype(jnp.float32)
            for zz in range(4):
                mine = total[8 * zz : 8 * zz + 8]
                self.parts[0][j, yy, xx, zz] = jnp.concatenate(
                    [mine[:, :512], mine[:, 512:]], 0
                ).astype(jnp.bfloat16)
            return carry

        lax.fori_loop(0, 16, step, 0)
        self.launch(0, j)

    def total(self, stage, j, block):
        order = ORDERS[j]
        where = [a for a in (0, 1, 2) if a not in order[:stage]].index(order[stage])
        index = list(block)
        index.insert(where, self.here[order[stage]])
        total = self.parts[stage][(j,) + tuple(index)].astype(jnp.float32)
        for k in range(3):
            total = total + self.landing[stage][(j, k) + tuple(block)].astype(jnp.float32)
        return total

    def add(self, stage, j):
        for copy in self.spread(stage, j):
            copy.wait_recv()

        def step(i, carry):
            block = (lax.div(i, 4), lax.rem(i, 4)) if stage == 0 else (i,)
            self.parts[stage + 1][(j,) + block] = self.total(stage, j, block).astype(jnp.bfloat16)
            return carry

        lax.fori_loop(0, 16 if stage == 0 else 4, step, 0)
        self.launch(stage + 1, j)

    def result(self, j):
        for copy in self.spread(2, j):
            copy.wait_recv()
        total = self.total(2, j, ())
        return jnp.concatenate([total[:8], total[8:]], 1).astype(jnp.bfloat16)

    def close(self):
        for j in range(PIECES):
            self.cross(j).wait_send()
            for stage in range(3):
                for copy in self.spread(stage, j):
                    copy.wait_send()


def torus_peers():
    return [other_core()] + [along(a, k)[0] for a in range(3) for k in (1, 2, 3)]


def halves(g):
    return g.reshape(4, 2, 128, g.shape[1])


LISTED = 128


def fetch_kernel(
    touched, members, table_hbm, spd, lookup,
    x_out, lists_out, bias_hbm,
    table, asked, lists, chosen, outgoing, slots, bias,
    table_sem, ask_send, ask_recv, list_send, list_recv, row_send, row_recv, bias_sem,
):
    dp, store = lax.axis_index("dp"), lax.axis_index("store")
    shards, groups = asked.shape[0], lists.shape[0]
    rows, width = table.shape
    cap = slots.shape[1] // 2
    half = width // 2
    egos, heads, count, _ = bias.shape
    turn = lambda here, k, size: lax.rem(here + k, size)
    owners = [(dp, turn(store, k, shards)) for k in range(shards)]
    copies_of_shard = [(turn(dp, k, groups), store) for k in range(groups)]

    load = pltpu.make_async_copy(table_hbm, table, table_sem)
    load.start()
    barrier = pltpu.get_barrier_semaphore()
    for device in owners[1:] + copies_of_shard[1:]:
        pl.semaphore_signal(barrier, inc=1, device_id=device, device_id_type=MESH)
    pl.semaphore_wait(barrier, shards + groups - 2)

    requests = []
    for k in range(1, shards):
        copy = pltpu.make_async_remote_copy(
            src_ref=touched.at[owners[k][1]], dst_ref=asked.at[store],
            send_sem=ask_send.at[k], recv_sem=ask_recv.at[k],
            device_id=owners[k], device_id_type=MESH)
        copy.start()
        requests.append(copy)
    asked[store] = touched[store]

    bias_copies = []

    def look_up(ego, first, many):
        def step(n, carry):
            at = pl.ds(pl.multiple_of(n * 8, 8), 8)
            for a in range(0, count, 128):
                distance = spd[ego, at, a : a + 128]
                for h in range(first, first + many):
                    row = jnp.broadcast_to(lookup[h : h + 1, :], (8, 128))
                    bias[ego, h, at, a : a + 128] = jnp.take_along_axis(
                        row, distance, axis=1, mode="promise_in_bounds"
                    )
            return carry

        lax.fori_loop(0, count // 8, step, 0, unroll=2)
        part = pl.ds(first, many)
        copy = pltpu.make_async_copy(
            bias.at[ego, part], bias_hbm.at[ego, part], bias_sem.at[len(bias_copies)])
        copy.start()
        bias_copies.append(copy)

    look_up(0, 0, 8)
    for copy in requests:
        copy.wait_recv()
    shared = []
    for k in range(1, groups):
        copy = pltpu.make_async_remote_copy(
            src_ref=asked, dst_ref=lists.at[dp],
            send_sem=list_send.at[k], recv_sem=list_recv.at[k],
            device_id=copies_of_shard[k], device_id_type=MESH)
        copy.start()
        shared.append(copy)
    lists[dp] = asked[...]

    order = list(range(1, shards)) + [0]
    turned = jnp.concatenate(
        [asked[owners[k][1]] for k in order] + [jnp.full((LISTED - shards, LISTED), -1, jnp.int32)], 0
    ).T
    for p in range(0, shards, 2):
        pair = jnp.concatenate([turned[:cap, p : p + 1], turned[:cap, p + 1 : p + 2]], 0)
        shape = (2 * cap, rows)
        hit = jnp.broadcast_to(pair, shape) == lax.broadcasted_iota(jnp.int32, shape, 1)
        chosen[p * cap : (p + 2) * cap, :] = jnp.where(hit, 1.0, 0.0).astype(jnp.bfloat16)
    load.wait()
    sent = []
    for first in range(0, shards, 4):
        picks = chosen[first * cap : (first + 4) * cap, :]
        left = jnp.dot(picks, table[:, :half], preferred_element_type=jnp.float32)
        right = jnp.dot(picks, table[:, half:], preferred_element_type=jnp.float32)
        for i in range(4):
            k = order[first + i]
            mine = slice(i * cap, i * cap + cap)
            block = jnp.concatenate([left[mine], right[mine]], 0).astype(jnp.bfloat16)
            if k == 0:
                slots[store] = block
                continue
            outgoing[k] = block
            copy = pltpu.make_async_remote_copy(
                src_ref=outgoing.at[k], dst_ref=slots.at[store],
                send_sem=row_send.at[k], recv_sem=row_recv.at[k],
                device_id=owners[k], device_id_type=MESH)
            copy.start()
            sent.append(copy)

    look_up(0, 8, heads - 8)
    look_up(1, 0, heads)
    for copy in sent:
        copy.wait_recv()
    tokens = members.shape[0]
    shape = (tokens, shards * 2 * cap)
    held = slots[...].reshape(shards * 2 * cap, half)
    places = lax.broadcasted_iota(jnp.int32, shape, 1)
    for part in range(2):
        hit = jnp.broadcast_to(members[...] + part * cap, shape) == places
        x_out[:, part * half : part * half + half] = jnp.dot(
            jnp.where(hit, 1.0, 0.0).astype(jnp.bfloat16), held, preferred_element_type=jnp.float32
        ).astype(x_out.dtype)
    for copy in shared:
        copy.wait()
    lists_out[...] = lists[...]
    for copy in requests + sent:
        copy.wait_send()
    for copy in bias_copies:
        copy.wait()


def fetch(node_table, touched, member_slot, spd, table):
    bf16, f32, i32 = jnp.bfloat16, jnp.float32, jnp.int32
    _, shards, cap = touched.shape
    groups = lax.axis_size("dp")
    egos, count = member_slot.shape
    heads = table.shape[1]
    rows, width = node_table.shape
    lookup = jnp.pad((table * LOG2E).T, ((0, 0), (0, 128 - table.shape[0])))
    listed = jnp.pad(
        touched.reshape(shards, 1, cap), ((0, 0), (0, 0), (0, LISTED - cap)), constant_values=-1
    )
    members = (member_slot + cap * lax.div(member_slot, cap)).reshape(egos * count, 1)
    hbm = pl.BlockSpec(memory_space=pl.ANY)
    vmem = pl.BlockSpec(memory_space=pltpu.VMEM)
    dma = pltpu.SemaphoreType.DMA
    x, lists, bias = pl.pallas_call(
        fetch_kernel,
        name="fetch",
        out_shape=(
            jax.ShapeDtypeStruct((egos * count, width), bf16),
            jax.ShapeDtypeStruct((groups, shards, 1, LISTED), i32),
            jax.ShapeDtypeStruct((egos, heads, count, count), f32),
        ),
        in_specs=[vmem, vmem, hbm, vmem, vmem],
        out_specs=(vmem, vmem, hbm),
        scratch_shapes=[
            pltpu.VMEM((rows, width), bf16),
            pltpu.VMEM((shards, 1, LISTED), i32),
            pltpu.VMEM((groups, shards, 1, LISTED), i32),
            pltpu.VMEM((shards * cap, rows), bf16),
            pltpu.VMEM((shards, 2 * cap, width // 2), bf16),
            pltpu.VMEM((shards, 2 * cap, width // 2), bf16),
            pltpu.VMEM((egos, heads, count, count), f32),
            dma,
            dma((shards,)),
            dma((shards,)),
            dma((groups,)),
            dma((groups,)),
            dma((shards,)),
            dma((shards,)),
            dma((3,)),
        ],
        compiler_params=pltpu.CompilerParams(
            collective_id=1, has_side_effects=True, vmem_limit_bytes=48 * 1024 * 1024
        ),
    )(listed, members, node_table, spd, lookup)
    return x, lists[:, :, 0, :], bias


GROUP = 8
LOG2E = math.log2(math.e)


def head_mask(rows, width, head):
    lanes = lax.broadcasted_iota(jnp.int32, (rows, width), 1)
    return lax.div(lanes, width // GROUP) == head


def only_head(value, head):
    return jnp.where(head_mask(value.shape[0], value.shape[1], head), value, jnp.zeros((), value.dtype))


def attend_kernel(q_ref, k_ref, v_ref, bias_ref, mixed_ref, probs_ref):
    count = q_ref.shape[0]
    head_width = q_ref.shape[1] // GROUP
    scale = LOG2E * head_width ** (-0.5)
    chunk = 32
    q, k, v = q_ref[...], k_ref[...], v_ref[...]
    mixed = jnp.zeros(q.shape, jnp.float32)
    for j in range(GROUP):
        raw = lax.dot_general(
            q, only_head(k, j), (((1,), (1,)), ((), ())), preferred_element_type=jnp.float32
        )
        parts = []
        for c in range(count // chunk):
            rows = slice(c * chunk, c * chunk + chunk)
            logits = raw[rows] * scale + bias_ref[0, j, rows, :]
            power = jnp.exp2(logits - jnp.max(logits, -1, keepdims=True))
            probs = power * (1.0 / jnp.sum(power, -1, keepdims=True))
            probs_ref[0, j, rows, :] = probs
            parts.append(probs.astype(jnp.bfloat16))
        mixed = mixed + jnp.dot(
            jnp.concatenate(parts, 0), only_head(v, j), preferred_element_type=jnp.float32
        )
    mixed_ref[...] = mixed.astype(mixed_ref.dtype)


def attend_back_kernel(
    q_ref, k_ref, v_ref, dattn_ref, probs_ref, spd_ref, g_down, g_up, g_out,
    dq_ref, dk_ref, dv_ref, bias_ref, o_down, o_up, o_out, slopes, onehot, corner, own, own_sem, *rest,
):
    ego, group = pl.program_id(0), pl.program_id(1)
    step = ego * pl.num_programs(1) + group
    sources, sums = (g_down, g_up, g_out), (o_down, o_up, o_out)
    core = lax.rem(lax.axis_index("dp"), 2)
    reducer = Reducer(
        rest, lambda j: sources[j].at[:, 1 - core], lambda j, yy, rows: own[j, yy, rows, :]
    )
    keep = lambda j: pltpu.make_async_copy(sources[j].at[:, core], own.at[j], own_sem.at[j])

    @pl.when(step == 0)
    def _():
        signal_meet(torus_peers())
        for j in range(PIECES):
            keep(j).start()

    @pl.when(step == 1)
    def _():
        wait_meet(torus_peers())
        for j in range(PIECES):
            reducer.cross(j).start()

    @pl.when(step == 3)
    def _():
        for j in range(PIECES):
            keep(j).wait()
            reducer.add_cores(j)

    @pl.when(step == 5)
    def _():
        for j in range(PIECES):
            reducer.add(0, j)

    @pl.when(step == 6)
    def _():
        for j in range(PIECES):
            reducer.add(1, j)

    @pl.when(step == 7)
    def _():
        for j in range(PIECES):
            sums[j][...] = reducer.result(j)
        reducer.close()

    count, width = q_ref.shape
    scale = (width // GROUP) ** (-0.5)
    buckets = 32
    chunk = 32
    q, k, v, dattn = q_ref[...], k_ref[...], v_ref[...], dattn_ref[...]

    @pl.when(group == 0)
    def _():
        def fill(n, carry):
            row = jnp.broadcast_to(spd_ref[0, pl.ds(n, 1), :], (buckets, count))
            hit = row == lax.broadcasted_iota(jnp.int32, (buckets, count), 0)
            onehot[pl.ds(pl.multiple_of(n * buckets, buckets), buckets), :] = jnp.where(hit, 1.0, 0.0).astype(jnp.bfloat16)
            return carry

        lax.fori_loop(0, count, fill, 0, unroll=8)

    dq = jnp.zeros((count, width), jnp.float32)
    dk = jnp.zeros((count, width), jnp.float32)
    dv = jnp.zeros((count, width), jnp.float32)
    over_rows = (((0,), (0,)), ((), ()))
    for j in range(GROUP):
        dprobs = lax.dot_general(
            dattn, only_head(v, j), (((1,), (1,)), ((), ())), preferred_element_type=jnp.float32
        )
        slope_parts, prob_parts = [], []
        for c in range(count // chunk):
            rows = slice(c * chunk, c * chunk + chunk)
            probs = probs_ref[0, j, rows, :]
            part = dprobs[rows]
            slope = probs * (part - jnp.sum(part * probs, -1, keepdims=True))
            for a in range(count // 128):
                slopes[group * (count // 128) + a, pl.ds(c * chunk * GROUP + j, chunk, stride=GROUP), :] = slope[:, a * 128 : a * 128 + 128]
            slope_parts.append((slope * scale).astype(jnp.bfloat16))
            prob_parts.append(probs.astype(jnp.bfloat16))
        slope_b = jnp.concatenate(slope_parts, 0)
        probs_b = jnp.concatenate(prob_parts, 0)
        dq = dq + jnp.dot(slope_b, only_head(k, j), preferred_element_type=jnp.float32)
        dk = dk + lax.dot_general(slope_b, only_head(q, j), over_rows, preferred_element_type=jnp.float32)
        dv = dv + lax.dot_general(probs_b, only_head(dattn, j), over_rows, preferred_element_type=jnp.float32)
    dq_ref[...] = dq.astype(dq_ref.dtype)
    dk_ref[...] = dk.astype(dk_ref.dtype)
    dv_ref[...] = dv.astype(dv_ref.dtype)

    @pl.when(group == pl.num_programs(1) - 1)
    def _():
        halves = count // 128
        groups = slopes.shape[0] // halves
        corner[...] = jnp.zeros_like(corner)

        def collect(i, carry):
            total = corner[...]
            for n in range(4):
                first = pl.multiple_of((i * 4 + n) * 8 * GROUP, 8 * GROUP)
                rows = pl.ds(first, 8 * GROUP)
                left = jnp.concatenate(
                    [
                        jnp.concatenate([slopes[g * halves + a, rows, :] for a in range(halves)], 1)
                        for g in range(groups)
                    ],
                    0,
                ).astype(jnp.bfloat16)
                first = pl.multiple_of((i * 4 + n) * 8 * buckets, 8 * buckets)
                right = onehot[pl.ds(first, 8 * buckets), :]
                total = total + lax.dot_general(
                    left, right, (((1,), (1,)), ((), ())), preferred_element_type=jnp.float32
                )
            corner[...] = total
            return carry

        lax.fori_loop(0, count // 32, collect, 0)
        shape = corner.shape
        node_row = lax.rem(lax.div(lax.broadcasted_iota(jnp.int32, shape, 0), GROUP), 8)
        node_col = lax.div(lax.broadcasted_iota(jnp.int32, shape, 1), buckets)
        kept = jnp.where(node_row == node_col, corner[...], 0.0)
        tall = []
        for g in range(groups):
            heads = kept[g * 8 * GROUP : g * 8 * GROUP + GROUP]
            for n in range(1, 8):
                heads = heads + kept[(g * 8 + n) * GROUP : (g * 8 + n) * GROUP + GROUP]
            tall.append(heads)
        bias_ref[0] = jnp.concatenate(tall, 0)


def attention_specs(count, width, heads):
    wide = width // heads * GROUP
    groups = heads // GROUP
    column = lambda part: pl.BlockSpec((count, wide), lambda e, g, part=part: (e, part * groups + g))
    probs = pl.BlockSpec((1, GROUP, count, count), lambda e, g: (e, g, 0, 0))
    spd = pl.BlockSpec((1, count, count), lambda e, g: (e, 0, 0))
    return column, probs, spd, groups


def attention_forward(qkv, bias):
    egos, heads, count, _ = bias.shape
    width = qkv.shape[1] // 3
    column, probs, _, groups = attention_specs(count, width, heads)
    return pl.pallas_call(
        attend_kernel,
        name="attend",
        grid=(egos, groups),
        out_shape=(
            jax.ShapeDtypeStruct((egos * count, width), jnp.bfloat16),
            jax.ShapeDtypeStruct((egos, heads, count, count), jnp.float32),
        ),
        in_specs=[column(0), column(1), column(2), probs],
        out_specs=(column(0), probs),
        compiler_params=pltpu.CompilerParams(vmem_limit_bytes=40 * 1024 * 1024),
    )(qkv, qkv, qkv, bias)


def attention_backward(qkv, dattn, probs, spd, gradients):
    egos, heads, count, _ = probs.shape
    width = qkv.shape[1] // 3
    column, probs_spec, spd_spec, groups = attention_specs(count, width, heads)
    flat = jax.ShapeDtypeStruct((egos * count, width), jnp.bfloat16)
    summed = jax.ShapeDtypeStruct((8, 1024), jnp.bfloat16)
    whole = pl.BlockSpec((8, 1024), lambda e, g: (0, 0))
    dq, dk, dv, bias, *sums = pl.pallas_call(
        attend_back_kernel,
        name="attend_back",
        grid=(egos, groups),
        out_shape=(flat, flat, flat, jax.ShapeDtypeStruct((egos, heads, 256), jnp.float32)) + (summed,) * 3,
        in_specs=[column(0), column(1), column(2), column(0), probs_spec, spd_spec]
        + [pl.BlockSpec(memory_space=pl.ANY)] * PIECES,
        out_specs=(column(0), column(0), column(0), pl.BlockSpec((1, heads, 256), lambda e, g: (e, 0, 0)))
        + (whole,) * 3,
        scratch_shapes=[
            pltpu.VMEM((groups * (count // 128), count * GROUP, 128), jnp.float32),
            pltpu.VMEM((count * 32, count), jnp.bfloat16),
            pltpu.VMEM((groups * 8 * GROUP, 256), jnp.float32),
            pltpu.VMEM((PIECES, 4, 128, 1024), jnp.bfloat16),
            pltpu.SemaphoreType.DMA((PIECES,)),
        ]
        + Reducer.scratch(),
        compiler_params=pltpu.CompilerParams(
            collective_id=2, has_side_effects=True, vmem_limit_bytes=48 * 1024 * 1024
        ),
    )(qkv, qkv, qkv, dattn, probs, spd, *[halves(g) for g in gradients])
    return dq, dk, dv, bias.reshape(egos, heads, 8, 32).sum((0, 2)).T, sums


CHUNKS = 4


def finish_kernel(
    h1, dq, dk, dv, x, dy, gain, members, lists, small, w_hbm,
    o_qkv, o_small, o_table,
    weights, turned, grads, dh1, high, low, gain_sum, slot_grads, by_column, by_owner, placed,
    mine, small_core, small_all, *rest,
):
    dp, store = lax.axis_index("dp"), lax.axis_index("store")
    core = lax.rem(dp, 2)
    reducer = Reducer(
        rest[:-9],
        lambda j: grads.at[j, :, 1 - core],
        lambda j, yy, rows: grads[j, yy, core, rows, :],
    )
    w_sem, sc_send, sc_recv, s_send, s_recv, a_send, a_recv, b_send, b_recv = rest[-9:]
    groups, owners, padded, _ = by_column.shape
    per = owners // CHUNKS
    tokens, width = x.shape
    columns = [(lax.rem(dp + k, groups), store) for k in range(groups)]
    shards = [(dp, lax.rem(store + k, owners)) for k in range(owners)]
    here = reducer.here
    signal_meet(columns[1:] + shards[1:])
    load = pltpu.make_async_copy(w_hbm, weights, w_sem)
    load.start()

    turned[...] = h1[...].T
    for j, part in enumerate((dq, dk, dv)):

        def multiply(i, carry, j=j, part=part):
            rows = pl.ds(pl.multiple_of(i * 256, 256), 256)
            block = jnp.dot(turned[rows, :], part[...], preferred_element_type=jnp.float32).astype(jnp.bfloat16)
            grads[j, i, 0] = block[:128]
            grads[j, i, 1] = block[128:]
            return carry

        lax.fori_loop(0, 4, multiply, 0)
        if j == 0:
            wait_meet(columns[1:] + shards[1:])
            load.wait()
        reducer.cross(j).start()

    def back(i, carry):
        rows = pl.ds(pl.multiple_of(i * 256, 256), 256)
        total = jnp.zeros((tokens, 256), jnp.float32)
        for j, part in enumerate((dq, dk, dv)):
            total = total + lax.dot_general(
                part[...], weights[rows, j * width : j * width + width], (((1,), (1,)), ((), ())),
                preferred_element_type=jnp.float32)
        dh1[i] = total
        return carry

    lax.fori_loop(0, 2, back, 0)
    reducer.add_cores(0)
    lax.fori_loop(2, 4, back, 0)
    reducer.add_cores(1)
    reducer.add_cores(2)
    gain_sum[...] = jnp.zeros_like(gain_sum)

    def norm_back(i, carry):
        rows = pl.ds(pl.multiple_of(i * 32, 32), 32)
        centred = x[rows, :].astype(jnp.float32)
        centred = centred - jnp.mean(centred, -1, keepdims=True)
        rstd = lax.rsqrt(jnp.mean(centred * centred, -1, keepdims=True) + EPS)
        vhat = centred * rstd
        grad = jnp.concatenate([dh1[n, rows, :] for n in range(4)], 1)
        product = grad * vhat
        gain_sum[...] += product[:8] + product[8:16] + product[16:24] + product[24:]
        scaled = grad * gain[...]
        first = jnp.mean(scaled, -1, keepdims=True)
        second = jnp.mean(scaled * vhat, -1, keepdims=True)
        dx = dy[rows, :] + rstd * (scaled - first - vhat * second)
        top = dx.astype(jnp.bfloat16)
        high[rows, :] = top
        low[rows, :] = (dx - top.astype(jnp.float32)).astype(jnp.bfloat16)
        return carry

    lax.fori_loop(0, tokens // 32, norm_back, 0, unroll=2)

    to_columns = []
    for i in range(CHUNKS):
        block = (per * padded, tokens)
        hit = jnp.broadcast_to(members[...], block) == lax.broadcasted_iota(jnp.int32, block, 0) + i * per * padded
        chosen = jnp.where(hit, 1.0, 0.0).astype(jnp.bfloat16)
        total = jnp.dot(chosen, high[...], preferred_element_type=jnp.float32) + jnp.dot(
            chosen, low[...], preferred_element_type=jnp.float32
        )
        for c in range(groups):
            slot_grads[c, i * per : i * per + per] = (
                total[:, c * 128 : c * 128 + 128].reshape(per, padded, 128).astype(jnp.bfloat16)
            )
        some = pl.ds(i * per, per)
        copies = []
        for k in range(1, groups):
            copy = pltpu.make_async_remote_copy(
                src_ref=slot_grads.at[columns[k][0], some], dst_ref=by_column.at[dp, some],
                send_sem=a_send.at[i, k], recv_sem=a_recv.at[i, k], device_id=columns[k], device_id_type=MESH)
            copy.start()
            copies.append(copy)
        by_column[dp, some] = slot_grads[dp, some]
        to_columns.append(copies)

    sums = gain_sum[...]
    sums = sums[:4] + sums[4:]
    sums = sums[:2] + sums[2:]
    sums = sums[:1] + sums[1:]
    mine[...] = small[...]
    for n in range(8):
        mine[n : n + 1, :] = sums[:, n * 128 : n * 128 + 128]
    tiny = pltpu.make_async_remote_copy(
        src_ref=mine, dst_ref=small_core, send_sem=sc_send, recv_sem=sc_recv,
        device_id=other_core(), device_id_type=MESH)
    tiny.start()

    def spread_small(axis):
        copies = []
        for k in (1, 2, 3):
            copy = pltpu.make_async_remote_copy(
                src_ref=small_all.at[axis, here[axis]], dst_ref=small_all.at[axis, here[axis]],
                send_sem=s_send.at[axis, k - 1], recv_sem=s_recv.at[axis, k - 1],
                device_id=along(axis, k)[0], device_id_type=MESH)
            copy.start()
            copies.append(copy)
        return copies

    def total_small(axis):
        return (small_all[axis, 0] + small_all[axis, 1]) + (small_all[axis, 2] + small_all[axis, 3])

    for j in range(PIECES):
        reducer.add(0, j)
    to_owners = []
    for i in range(CHUNKS):
        for copy in to_columns[i]:
            copy.wait_recv()
        for k in range(i * per, i * per + per):
            if k == 0:
                by_owner[0] = by_column[:, 0]
                continue
            copy = pltpu.make_async_remote_copy(
                src_ref=by_column.at[:, k], dst_ref=by_owner.at[k],
                send_sem=b_send.at[k], recv_sem=b_recv.at[k], device_id=shards[k], device_id_type=MESH)
            copy.start()
            to_owners.append(copy)
        if i == 0:
            tiny.wait()
            small_all[0, here[0]] = mine[...] + small_core[...]
            tiny_copies = spread_small(0)
    for j in range(PIECES):
        reducer.add(1, j)
    for axis in (1, 2):
        for copy in tiny_copies:
            copy.wait()
        small_all[axis, here[axis]] = total_small(axis - 1)
        tiny_copies = spread_small(axis)

    entries = 2 * groups * padded
    for k in range(0, owners, 2):
        for copy in to_owners[max(k - 1, 0) : k + 1]:
            copy.wait_recv()
        senders = [lax.rem(store + owners - k - n, owners) for n in range(2)]
        wanted = jnp.concatenate([lists[pl.ds(s, 1), :] for s in senders], 1)
        arrived = by_owner[k : k + 2].reshape(entries, 128)

        def place(i, carry, k=k, wanted=wanted, arrived=arrived):
            block = (512, entries)
            rows = pl.ds(pl.multiple_of(i * 512, 512), 512)
            hit = jnp.broadcast_to(wanted, block) == lax.broadcasted_iota(jnp.int32, block, 0) + i * 512
            total = jnp.dot(
                jnp.where(hit, 1.0, 0.0).astype(jnp.bfloat16), arrived, preferred_element_type=jnp.float32
            )
            if k > 0:
                total = total + placed[rows, :]
            if k < owners - 2:
                placed[rows, :] = total
            else:
                o_table[rows, :] = total.astype(jnp.bfloat16)
            return carry

        lax.fori_loop(0, o_table.shape[0] // 512, place, 0)

    for copy in tiny_copies:
        copy.wait()
    o_small[...] = total_small(2)
    for j in range(PIECES):
        o_qkv[:, j * 1024 : j * 1024 + 1024] = reducer.result(j)
    reducer.close()
    for copies in to_columns + [to_owners]:
        for copy in copies:
            copy.wait_send()


def finish(h1, dq, dk, dv, x, dy, gain, member_slot, lists, small, w_qkv, rows, cap):
    bf16, f32 = jnp.bfloat16, jnp.float32
    groups, owners, _ = lists.shape
    tokens, width = x.shape
    padded = -(-cap // 16) * 16
    owner = lax.div(member_slot, cap)
    turn = lax.rem(owner + owners - lax.axis_index("store"), owners)
    members = (turn * padded + member_slot - owner * cap).reshape(1, tokens)
    entries = lists[:, :, :padded].transpose(1, 0, 2).reshape(owners, groups * padded)
    vmem = pl.BlockSpec(memory_space=pltpu.VMEM)
    dma = pltpu.SemaphoreType.DMA
    return pl.pallas_call(
        finish_kernel,
        name="finish",
        out_shape=(
            jax.ShapeDtypeStruct((8, 3 * width), bf16),
            jax.ShapeDtypeStruct(small.shape, f32),
            jax.ShapeDtypeStruct((rows, 128), bf16),
        ),
        in_specs=[vmem] * 10 + [pl.BlockSpec(memory_space=pl.ANY)],
        out_specs=[vmem] * 3,
        scratch_shapes=[
            pltpu.VMEM(w_qkv.shape, bf16),
            pltpu.VMEM((width, tokens), bf16),
            pltpu.VMEM((PIECES, 4, 2, 128, 1024), bf16),
            pltpu.VMEM((4, tokens, 256), f32),
            pltpu.VMEM((tokens, width), bf16),
            pltpu.VMEM((tokens, width), bf16),
            pltpu.VMEM((8, width), f32),
            pltpu.VMEM((groups, owners, padded, 128), bf16),
            pltpu.VMEM((groups, owners, padded, 128), bf16),
            pltpu.VMEM((owners, groups, padded, 128), bf16),
            pltpu.VMEM((rows, 128), f32),
            pltpu.VMEM(small.shape, f32),
            pltpu.VMEM(small.shape, f32),
            pltpu.VMEM((3, 4) + small.shape, f32),
        ]
        + Reducer.scratch()
        + [dma, dma, dma, dma((3, 3)), dma((3, 3)), dma((CHUNKS, groups)), dma((CHUNKS, groups)), dma((owners,)), dma((owners,))],
        compiler_params=pltpu.CompilerParams(
            collective_id=0, has_side_effects=True, vmem_limit_bytes=54 * 1024 * 1024
        ),
    )(h1, dq, dk, dv, x, dy, gain, members, entries, small, w_qkv)


def body(
    node_table,
    touched,
    member_slot,
    distances,
    cotangent,
    w_qkv,
    w_out,
    w_up,
    w_down,
    gains,
    bias_table,
):
    bf16, f32 = jnp.bfloat16, jnp.float32
    shard_rows, width = node_table.shape
    owners, cap = touched.shape[1:]
    egos, count = member_slot.shape
    tokens = egos * count
    dot = lambda a, b: jnp.dot(a, b, preferred_element_type=f32)
    back = lambda a, b: lax.dot_general(a, b, (((1,), (1,)), ((), ())), preferred_element_type=f32)
    weight = lambda a, b: lax.dot_general(
        a, b, (((0,), (0,)), ((), ())), preferred_element_type=f32
    ).astype(bf16)

    x, lists, bias = fetch(node_table, touched, member_slot, distances, bias_table)
    x_rows, x = x, x.astype(f32)
    dout = cotangent.reshape(tokens, width)

    h1, _, _ = layer_normalize(x, gains[0])
    h1 = h1.astype(bf16)
    qkv = dot(h1, w_qkv).astype(bf16)
    attended, probs = attention_forward(qkv, bias)
    y = x + dot(attended, w_out)
    h2, y_hat, y_rstd = layer_normalize(y, gains[1])
    h2 = h2.astype(bf16)
    act, slope = gelu_parts(dot(h2, w_up))
    act = act.astype(bf16)
    layer_out = (y + dot(act, w_down)).astype(bf16)

    du = (back(dout, w_down) * slope).astype(bf16)
    dy, gain_two = layer_normalize_backward(back(du, w_up), gains[1], y_hat, y_rstd)
    dy = dout.astype(f32) + dy
    dyb = dy.astype(bf16)
    dattn = back(dyb, w_out).astype(bf16)
    dq, dk, dv, grad_bias, (sum_down, sum_up, sum_out) = attention_backward(
        qkv, dattn, probs, distances, (weight(act, dout), weight(h2, du), weight(attended, dyb))
    )
    small = jnp.concatenate(
        [jnp.zeros((8, 128), f32), gain_two.reshape(8, 128), grad_bias.reshape(8, 128)]
    )
    sum_qkv, small, grad_table = finish(
        h1, dq, dk, dv, x_rows, dy, gains[:1], member_slot, lists, small, w_qkv, shard_rows, cap
    )
    return (
        layer_out.reshape(egos, count, width),
        grad_table,
        sum_qkv,
        sum_out,
        sum_up,
        sum_down,
        small[:16].reshape(2, width),
        small[16:].reshape(32, 32),
    )


def solution(mesh):
    in_specs = (
        P("store", None),
        P(("dp", "store"), None, None),
        P(("dp", "store"), None),
        P(("dp", "store"), None, None),
        P(("dp", "store"), None, None),
        P(),
        P(),
        P(),
        P(),
        P(),
        P(),
    )
    out_specs = (
        P(("dp", "store"), None, None),
        P("store", "dp"),
        P(("dp", "store"), None),
        P(("dp", "store"), None),
        P(("dp", "store"), None),
        P(("dp", "store"), None),
        P(),
        P(),
    )
    return jax.shard_map(body, mesh=mesh, in_specs=in_specs, out_specs=out_specs, check_vma=False)
```

```python
import math

import jax
import jax.numpy as jnp
from jax import lax
from jax.experimental import pallas as pl
from jax.experimental.pallas import tpu as pltpu
from jax.sharding import PartitionSpec as P

MESH = pl.DeviceIdType.MESH
ORDERS = ((0, 1, 2), (1, 2, 0), (2, 0, 1))
PIECES = 6


EPS = 1e-05
ROOT_HALF = 1.0 / math.sqrt(2.0)
ROOT_TWO_PI = 1.0 / math.sqrt(2.0 * math.pi)


def layer_normalize(value, gain):
    mean = jnp.mean(value, -1, keepdims=True)
    centred = value - mean
    rstd = lax.rsqrt(jnp.mean(centred * centred, -1, keepdims=True) + EPS)
    vhat = centred * rstd
    return (vhat * gain, vhat, rstd)


def layer_normalize_backward(grad, gain, vhat, rstd):
    scaled = grad * gain
    first = jnp.mean(scaled, -1, keepdims=True)
    second = jnp.mean(scaled * vhat, -1, keepdims=True)
    return (rstd * (scaled - first - vhat * second), jnp.sum(grad * vhat, 0))


def gelu_parts(upper):
    normal_cdf = 0.5 * (1.0 + jax.scipy.special.erf(upper * ROOT_HALF))
    activation_slope = normal_cdf + upper * jnp.exp(-0.5 * upper * upper) * ROOT_TWO_PI
    return (upper * normal_cdf, activation_slope)


LISTED = 128


def fetch_kernel(
    touched, members, table_hbm, spd, lookup,
    x_out, lists_out, bias_hbm,
    table, asked, lists, chosen, outgoing, slots, bias,
    table_sem, ask_send, ask_recv, list_send, list_recv, row_send, row_recv, bias_sem,
):
    dp, store = lax.axis_index("dp"), lax.axis_index("store")
    shards, groups = asked.shape[0], lists.shape[0]
    rows, width = table.shape
    cap = slots.shape[1] // 2
    half = width // 2
    egos, heads, count, _ = bias.shape
    turn = lambda here, k, size: lax.rem(here + k, size)
    owners = [(dp, turn(store, k, shards)) for k in range(shards)]
    copies_of_shard = [(turn(dp, k, groups), store) for k in range(groups)]

    load = pltpu.make_async_copy(table_hbm, table, table_sem)
    load.start()
    barrier = pltpu.get_barrier_semaphore()
    for device in owners[1:] + copies_of_shard[1:]:
        pl.semaphore_signal(barrier, inc=1, device_id=device, device_id_type=MESH)
    pl.semaphore_wait(barrier, shards + groups - 2)

    requests = []
    for k in range(1, shards):
        copy = pltpu.make_async_remote_copy(
            src_ref=touched.at[owners[k][1]], dst_ref=asked.at[store],
            send_sem=ask_send.at[k], recv_sem=ask_recv.at[k],
            device_id=owners[k], device_id_type=MESH)
        copy.start()
        requests.append(copy)
    asked[store] = touched[store]

    bias_copies = []

    def look_up(ego, first, many):
        def step(n, carry):
            at = pl.ds(pl.multiple_of(n * 8, 8), 8)
            for a in range(0, count, 128):
                distance = spd[ego, at, a : a + 128]
                for h in range(first, first + many):
                    row = jnp.broadcast_to(lookup[h : h + 1, :], (8, 128))
                    bias[ego, h, at, a : a + 128] = jnp.take_along_axis(
                        row, distance, axis=1, mode="promise_in_bounds"
                    )
            return carry

        lax.fori_loop(0, count // 8, step, 0, unroll=2)
        part = pl.ds(first, many)
        copy = pltpu.make_async_copy(
            bias.at[ego, part], bias_hbm.at[ego, part], bias_sem.at[len(bias_copies)])
        copy.start()
        bias_copies.append(copy)

    look_up(0, 0, 8)
    for copy in requests:
        copy.wait_recv()
    shared = []
    for k in range(1, groups):
        copy = pltpu.make_async_remote_copy(
            src_ref=asked, dst_ref=lists.at[dp],
            send_sem=list_send.at[k], recv_sem=list_recv.at[k],
            device_id=copies_of_shard[k], device_id_type=MESH)
        copy.start()
        shared.append(copy)
    lists[dp] = asked[...]

    order = list(range(1, shards)) + [0]
    turned = jnp.concatenate(
        [asked[owners[k][1]] for k in order] + [jnp.full((LISTED - shards, LISTED), -1, jnp.int32)], 0
    ).T
    for p in range(0, shards, 2):
        pair = jnp.concatenate([turned[:cap, p : p + 1], turned[:cap, p + 1 : p + 2]], 0)
        shape = (2 * cap, rows)
        hit = jnp.broadcast_to(pair, shape) == lax.broadcasted_iota(jnp.int32, shape, 1)
        chosen[p * cap : (p + 2) * cap, :] = jnp.where(hit, 1.0, 0.0).astype(jnp.bfloat16)
    load.wait()
    sent = []
    for first in range(0, shards, 4):
        picks = chosen[first * cap : (first + 4) * cap, :]
        left = jnp.dot(picks, table[:, :half], preferred_element_type=jnp.float32)
        right = jnp.dot(picks, table[:, half:], preferred_element_type=jnp.float32)
        for i in range(4):
            k = order[first + i]
            mine = slice(i * cap, i * cap + cap)
            block = jnp.concatenate([left[mine], right[mine]], 0).astype(jnp.bfloat16)
            if k == 0:
                slots[store] = block
                continue
            outgoing[k] = block
            copy = pltpu.make_async_remote_copy(
                src_ref=outgoing.at[k], dst_ref=slots.at[store],
                send_sem=row_send.at[k], recv_sem=row_recv.at[k],
                device_id=owners[k], device_id_type=MESH)
            copy.start()
            sent.append(copy)

    look_up(0, 8, heads - 8)
    look_up(1, 0, heads)
    for copy in sent:
        copy.wait_recv()
    tokens = members.shape[0]
    shape = (tokens, shards * 2 * cap)
    held = slots[...].reshape(shards * 2 * cap, half)
    places = lax.broadcasted_iota(jnp.int32, shape, 1)
    for part in range(2):
        hit = jnp.broadcast_to(members[...] + part * cap, shape) == places
        x_out[:, part * half : part * half + half] = jnp.dot(
            jnp.where(hit, 1.0, 0.0).astype(jnp.bfloat16), held, preferred_element_type=jnp.float32
        ).astype(x_out.dtype)
    for copy in shared:
        copy.wait()
    lists_out[...] = lists[...]
    for copy in requests + sent:
        copy.wait_send()
    for copy in bias_copies:
        copy.wait()


def fetch(node_table, touched, member_slot, spd, table):
    bf16, f32, i32 = jnp.bfloat16, jnp.float32, jnp.int32
    _, shards, cap = touched.shape
    groups = lax.axis_size("dp")
    egos, count = member_slot.shape
    heads = table.shape[1]
    rows, width = node_table.shape
    lookup = jnp.pad((table * LOG2E).T, ((0, 0), (0, 128 - table.shape[0])))
    listed = jnp.pad(
        touched.reshape(shards, 1, cap), ((0, 0), (0, 0), (0, LISTED - cap)), constant_values=-1
    )
    members = (member_slot + cap * lax.div(member_slot, cap)).reshape(egos * count, 1)
    hbm = pl.BlockSpec(memory_space=pl.ANY)
    vmem = pl.BlockSpec(memory_space=pltpu.VMEM)
    dma = pltpu.SemaphoreType.DMA
    x, lists, bias = pl.pallas_call(
        fetch_kernel,
        name="fetch",
        out_shape=(
            jax.ShapeDtypeStruct((egos * count, width), bf16),
            jax.ShapeDtypeStruct((groups, shards, 1, LISTED), i32),
            jax.ShapeDtypeStruct((egos, heads, count, count), f32),
        ),
        in_specs=[vmem, vmem, hbm, vmem, vmem],
        out_specs=(vmem, vmem, hbm),
        scratch_shapes=[
            pltpu.VMEM((rows, width), bf16),
            pltpu.VMEM((shards, 1, LISTED), i32),
            pltpu.VMEM((groups, shards, 1, LISTED), i32),
            pltpu.VMEM((shards * cap, rows), bf16),
            pltpu.VMEM((shards, 2 * cap, width // 2), bf16),
            pltpu.VMEM((shards, 2 * cap, width // 2), bf16),
            pltpu.VMEM((egos, heads, count, count), f32),
            dma,
            dma((shards,)),
            dma((shards,)),
            dma((groups,)),
            dma((groups,)),
            dma((shards,)),
            dma((shards,)),
            dma((3,)),
        ],
        compiler_params=pltpu.CompilerParams(
            collective_id=1, has_side_effects=True, vmem_limit_bytes=48 * 1024 * 1024
        ),
    )(listed, members, node_table, spd, lookup)
    return x, lists[:, :, 0, :cap].reshape(-1), bias


GROUP = 8
LOG2E = math.log2(math.e)


def head_mask(rows, width, head):
    lanes = lax.broadcasted_iota(jnp.int32, (rows, width), 1)
    return lax.div(lanes, width // GROUP) == head


def only_head(value, head):
    return jnp.where(head_mask(value.shape[0], value.shape[1], head), value, jnp.zeros((), value.dtype))


def attend_kernel(q_ref, k_ref, v_ref, bias_ref, mixed_ref, probs_ref):
    count = q_ref.shape[0]
    head_width = q_ref.shape[1] // GROUP
    scale = LOG2E * head_width ** (-0.5)
    chunk = 32
    q, k, v = q_ref[...], k_ref[...], v_ref[...]
    mixed = jnp.zeros(q.shape, jnp.float32)
    for j in range(GROUP):
        raw = lax.dot_general(
            q, only_head(k, j), (((1,), (1,)), ((), ())), preferred_element_type=jnp.float32
        )
        parts = []
        for c in range(count // chunk):
            rows = slice(c * chunk, c * chunk + chunk)
            logits = raw[rows] * scale + bias_ref[0, j, rows, :]
            power = jnp.exp2(logits - jnp.max(logits, -1, keepdims=True))
            probs = power * (1.0 / jnp.sum(power, -1, keepdims=True))
            probs_ref[0, j, rows, :] = probs
            parts.append(probs.astype(jnp.bfloat16))
        mixed = mixed + jnp.dot(
            jnp.concatenate(parts, 0), only_head(v, j), preferred_element_type=jnp.float32
        )
    mixed_ref[...] = mixed.astype(mixed_ref.dtype)


def attend_back_kernel(
    q_ref, k_ref, v_ref, dattn_ref, probs_ref, spd_ref,
    dq_ref, dk_ref, dv_ref, bias_ref, slopes, onehot, corner,
):
    ego, group = pl.program_id(0), pl.program_id(1)
    count, width = q_ref.shape
    scale = (width // GROUP) ** (-0.5)
    buckets = 32
    chunk = 32
    q, k, v, dattn = q_ref[...], k_ref[...], v_ref[...], dattn_ref[...]

    @pl.when(group == 0)
    def _():
        def fill(n, carry):
            row = jnp.broadcast_to(spd_ref[0, pl.ds(n, 1), :], (buckets, count))
            hit = row == lax.broadcasted_iota(jnp.int32, (buckets, count), 0)
            onehot[pl.ds(pl.multiple_of(n * buckets, buckets), buckets), :] = jnp.where(hit, 1.0, 0.0).astype(jnp.bfloat16)
            return carry

        lax.fori_loop(0, count, fill, 0, unroll=8)

    dq = jnp.zeros((count, width), jnp.float32)
    dk = jnp.zeros((count, width), jnp.float32)
    dv = jnp.zeros((count, width), jnp.float32)
    over_rows = (((0,), (0,)), ((), ()))
    for j in range(GROUP):
        dprobs = lax.dot_general(
            dattn, only_head(v, j), (((1,), (1,)), ((), ())), preferred_element_type=jnp.float32
        )
        slope_parts, prob_parts = [], []
        for c in range(count // chunk):
            rows = slice(c * chunk, c * chunk + chunk)
            probs = probs_ref[0, j, rows, :]
            part = dprobs[rows]
            slope = probs * (part - jnp.sum(part * probs, -1, keepdims=True))
            for a in range(count // 128):
                slopes[group * (count // 128) + a, pl.ds(c * chunk * GROUP + j, chunk, stride=GROUP), :] = slope[:, a * 128 : a * 128 + 128]
            slope_parts.append((slope * scale).astype(jnp.bfloat16))
            prob_parts.append(probs.astype(jnp.bfloat16))
        slope_b = jnp.concatenate(slope_parts, 0)
        probs_b = jnp.concatenate(prob_parts, 0)
        dq = dq + jnp.dot(slope_b, only_head(k, j), preferred_element_type=jnp.float32)
        dk = dk + lax.dot_general(slope_b, only_head(q, j), over_rows, preferred_element_type=jnp.float32)
        dv = dv + lax.dot_general(probs_b, only_head(dattn, j), over_rows, preferred_element_type=jnp.float32)
    dq_ref[...] = dq.astype(dq_ref.dtype)
    dk_ref[...] = dk.astype(dk_ref.dtype)
    dv_ref[...] = dv.astype(dv_ref.dtype)

    @pl.when(group == pl.num_programs(1) - 1)
    def _():
        halves = count // 128
        groups = slopes.shape[0] // halves
        corner[...] = jnp.zeros_like(corner)

        def collect(i, carry):
            total = corner[...]
            for n in range(4):
                first = pl.multiple_of((i * 4 + n) * 8 * GROUP, 8 * GROUP)
                rows = pl.ds(first, 8 * GROUP)
                left = jnp.concatenate(
                    [
                        jnp.concatenate([slopes[g * halves + a, rows, :] for a in range(halves)], 1)
                        for g in range(groups)
                    ],
                    0,
                ).astype(jnp.bfloat16)
                first = pl.multiple_of((i * 4 + n) * 8 * buckets, 8 * buckets)
                right = onehot[pl.ds(first, 8 * buckets), :]
                total = total + lax.dot_general(
                    left, right, (((1,), (1,)), ((), ())), preferred_element_type=jnp.float32
                )
            corner[...] = total
            return carry

        lax.fori_loop(0, count // 32, collect, 0)
        shape = corner.shape
        node_row = lax.rem(lax.div(lax.broadcasted_iota(jnp.int32, shape, 0), GROUP), 8)
        node_col = lax.div(lax.broadcasted_iota(jnp.int32, shape, 1), buckets)
        kept = jnp.where(node_row == node_col, corner[...], 0.0)
        tall = []
        for g in range(groups):
            heads = kept[g * 8 * GROUP : g * 8 * GROUP + GROUP]
            for n in range(1, 8):
                heads = heads + kept[(g * 8 + n) * GROUP : (g * 8 + n) * GROUP + GROUP]
            tall.append(heads)
        bias_ref[0] = jnp.concatenate(tall, 0)


def attention_specs(count, width, heads):
    wide = width // heads * GROUP
    groups = heads // GROUP
    column = lambda part: pl.BlockSpec((count, wide), lambda e, g, part=part: (e, part * groups + g))
    probs = pl.BlockSpec((1, GROUP, count, count), lambda e, g: (e, g, 0, 0))
    spd = pl.BlockSpec((1, count, count), lambda e, g: (e, 0, 0))
    return column, probs, spd, groups


def attention_forward(qkv, bias):
    egos, heads, count, _ = bias.shape
    width = qkv.shape[1] // 3
    column, probs, _, groups = attention_specs(count, width, heads)
    return pl.pallas_call(
        attend_kernel,
        name="attend",
        grid=(egos, groups),
        out_shape=(
            jax.ShapeDtypeStruct((egos * count, width), jnp.bfloat16),
            jax.ShapeDtypeStruct((egos, heads, count, count), jnp.float32),
        ),
        in_specs=[column(0), column(1), column(2), probs],
        out_specs=(column(0), probs),
        compiler_params=pltpu.CompilerParams(vmem_limit_bytes=40 * 1024 * 1024),
    )(qkv, qkv, qkv, bias)


def attention_backward(qkv, dattn, probs, spd):
    egos, heads, count, _ = probs.shape
    width = qkv.shape[1] // 3
    column, probs_spec, spd_spec, groups = attention_specs(count, width, heads)
    flat = jax.ShapeDtypeStruct((egos * count, width), jnp.bfloat16)
    dq, dk, dv, bias = pl.pallas_call(
        attend_back_kernel,
        name="attend_back",
        grid=(egos, groups),
        out_shape=(flat, flat, flat, jax.ShapeDtypeStruct((egos, heads, 256), jnp.float32)),
        in_specs=[column(0), column(1), column(2), column(0), probs_spec, spd_spec],
        out_specs=(column(0), column(0), column(0), pl.BlockSpec((1, heads, 256), lambda e, g: (e, 0, 0))),
        scratch_shapes=[
            pltpu.VMEM((groups * (count // 128), count * GROUP, 128), jnp.float32),
            pltpu.VMEM((count * 32, count), jnp.bfloat16),
            pltpu.VMEM((groups * 8 * GROUP, 256), jnp.float32),
        ],
        compiler_params=pltpu.CompilerParams(vmem_limit_bytes=48 * 1024 * 1024),
    )(qkv, qkv, qkv, dattn, probs, spd)
    return dq, dk, dv, bias.reshape(egos, heads, 8, 32).sum((0, 2)).T


def slot_kernel(member_ref, dx_ref, out_ref):
    slots, tokens = out_ref.shape[1], dx_ref.shape[0]
    shape = (slots, tokens)
    hit = jnp.broadcast_to(member_ref[...], shape) == lax.broadcasted_iota(jnp.int32, shape, 0)
    placed = jnp.where(hit, 1.0, 0.0).astype(jnp.bfloat16)
    dx = dx_ref[...]
    high = dx.astype(jnp.bfloat16)
    low = (dx - high.astype(jnp.float32)).astype(jnp.bfloat16)
    total = jnp.dot(placed, high, preferred_element_type=jnp.float32) + jnp.dot(
        placed, low, preferred_element_type=jnp.float32
    )
    for c in range(out_ref.shape[0]):
        out_ref[c] = total[:, c * 128 : c * 128 + 128].astype(out_ref.dtype)


def slot_gradients(member_slot, dx, slots):
    tokens, width = dx.shape
    return pl.pallas_call(
        slot_kernel,
        name="slot_gradients",
        grid=(width // 256,),
        out_shape=jax.ShapeDtypeStruct((width // 128, slots, 128), jnp.bfloat16),
        in_specs=[pl.BlockSpec((1, tokens), lambda i: (0, 0)), pl.BlockSpec((tokens, 256), lambda i: (0, i))],
        out_specs=pl.BlockSpec((2, slots, 128), lambda i: (i, 0, 0)),
        compiler_params=pltpu.CompilerParams(vmem_limit_bytes=40 * 1024 * 1024),
    )(member_slot.reshape(1, tokens), dx)


def coordinates():
    dp, store = lax.axis_index("dp"), lax.axis_index("store")
    return lax.div(dp, 2), lax.rem(dp, 2), lax.div(store, 4), lax.rem(store, 4)


def peer(y, core, x, z):
    return (y * 2 + core, x * 4 + z)


def along(axis, offset):
    y, core, x, z = coordinates()
    place = [y, x, z]
    place[axis] = lax.rem(place[axis] + offset, 4)
    return peer(place[0], core, place[1], place[2]), place[axis]


def reduce_kernel(
    g_down, g_up, g_out, g_q, g_k, g_v, small, lists, returned,
    o_qkv, o_out, o_up, o_down, o_small, o_table,
    own, got, part0, low0, high0, left0, right0, part1, low1, high1, left1, right1, part2, low2, high2, left2, right2,
    small_core, small_all,
    own_sem, core_send, core_recv, send, recv, sc_send, sc_recv, s_send, s_recv,
):
    y, core, x, z = coordinates()
    here = (y, x, z)
    other = peer(y, 1 - core, x, z)
    everyone = [other] + [along(a, k)[0] for a in range(3) for k in (1, 2, 3)]

    barrier = pltpu.get_barrier_semaphore()
    for device in everyone:
        pl.semaphore_signal(barrier, inc=1, device_id=device, device_id_type=MESH)
    pl.semaphore_wait(barrier, len(everyone))

    sources = [g_down, g_up, g_out, g_q, g_k, g_v]
    outs = [o_down, o_up, o_out] + [o_qkv] * 3
    columns = [0, 0, 0, 0, 1024, 2048]
    sends = []

    local, cross = [], []
    tiny = pltpu.make_async_remote_copy(
        src_ref=small, dst_ref=small_core, send_sem=sc_send, recv_sem=sc_recv,
        device_id=other, device_id_type=MESH)
    tiny.start()
    for j in range(PIECES):
        remote = pltpu.make_async_remote_copy(
            src_ref=sources[j].at[:, 1 - core], dst_ref=got.at[j],
            send_sem=core_send.at[j], recv_sem=core_recv.at[j],
            device_id=other, device_id_type=MESH)
        remote.start()
        cross.append(remote)
        keep = pltpu.make_async_copy(sources[j].at[:, core], own.at[j], own_sem.at[j])
        keep.start()
        local.append(keep)

    tiny.wait()

    def spread_small(axis):
        copies = []
        for k in (1, 2, 3):
            device, _ = along(axis, k)
            copy = pltpu.make_async_remote_copy(
                src_ref=small_all.at[axis, here[axis]], dst_ref=small_all.at[axis, here[axis]],
                send_sem=s_send.at[axis, k - 1], recv_sem=s_recv.at[axis, k - 1],
                device_id=device, device_id_type=MESH)
            copy.start()
            copies.append(copy)
        return copies

    def total_small(axis):
        return (small_all[axis, 0] + small_all[axis, 1]) + (small_all[axis, 2] + small_all[axis, 3])

    small_all[0, here[0]] = small[...] + small_core[...]
    tiny_copies = spread_small(0)

    parts = (part0, part1, part2)
    landing = ((low0, high0, left0, right0), (low1, high1, left1, right1), (low2, high2, left2, right2))

    def block_of(j, stage, rest, place):
        order = ORDERS[j % 3]
        where = [a for a in (0, 1, 2) if a not in order[:stage]].index(order[stage])
        index = list(rest)
        index.insert(where, place)
        return (j,) + tuple(index)

    def ring(j, stage):
        axis = ORDERS[j % 3][stage]
        return [along(axis, k) for k in (0, 1, 2, 3)]

    def push(j, stage, kind, block, device):
        copy = pltpu.make_async_remote_copy(
            src_ref=parts[stage].at[block], dst_ref=landing[stage][kind].at[j],
            send_sem=send.at[stage, j, kind], recv_sem=recv.at[stage, j, kind],
            device_id=device, device_id_type=MESH)
        copy.start()
        return copy

    everything = lambda stage: (slice(None),) * (2 - stage)
    rows_lanes = lambda half: (slice(None), pl.ds(half * 256, 256))
    flight = {}

    def begin(j, stage):
        places = ring(j, stage)
        block = block_of(j, stage, everything(stage), places[2][1])
        flight[j] = [
            push(j, stage, 0, block + rows_lanes(0), places[1][0]),
            push(j, stage, 1, block + rows_lanes(1), places[3][0]),
        ]

    def each(stage, step):
        if stage == 2:
            step(())
        else:
            def body(i, carry):
                step((lax.div(i, 4), lax.rem(i, 4)) if stage == 0 else (i,))
                return carry

            lax.fori_loop(0, 16 if stage == 0 else 4, body, 0)

    def middle(j, stage):
        places = ring(j, stage)
        for copy in flight[j]:
            copy.wait_recv()
        sends.extend(flight[j])

        def step(rest):
            for half, place in ((0, places[1][1]), (1, places[3][1])):
                at = block_of(j, stage, rest, place) + (slice(None), slice(half * 256, half * 256 + 256))
                total = parts[stage][at].astype(jnp.float32) + landing[stage][half][(j,) + rest].astype(jnp.float32)
                parts[stage][at] = total.astype(jnp.bfloat16)

        each(stage, step)
        flight[j] = [
            push(j, stage, 2, block_of(j, stage, everything(stage), places[1][1]), places[1][0]),
            push(j, stage, 3, block_of(j, stage, everything(stage), places[3][1]), places[3][0]),
        ]

    def end(j, stage, store):
        places = ring(j, stage)
        for copy in flight[j]:
            copy.wait_recv()
        sends.extend(flight[j])

        def step(rest):
            total = parts[stage][block_of(j, stage, rest, places[0][1])].astype(jnp.float32)
            for kind in (2, 3):
                total = total + landing[stage][kind][(j,) + rest].astype(jnp.float32)
            store(rest, total)

        each(stage, step)

    entries = lists.shape[1]

    def place(i, carry):
        base = i * 256
        total = jnp.zeros((256, 128), jnp.float32)
        for a in range(lists.shape[0]):
            block = (256, entries)
            hit = jnp.broadcast_to(lists[a : a + 1, :], block) == lax.broadcasted_iota(jnp.int32, block, 0) + base
            total = total + jnp.dot(
                jnp.where(hit, 1.0, 0.0).astype(jnp.bfloat16), returned[a * entries : a * entries + entries, :],
                preferred_element_type=jnp.float32,
            )
        o_table[pl.ds(pl.multiple_of(base, 256), 256), :] = total.astype(jnp.bfloat16)
        return carry

    for j in range(PIECES):
        local[j].wait()
        cross[j].wait_recv()

        def add_cores(i, carry, j=j):
            yy, xx = lax.div(i, 4), lax.rem(i, 4)
            rows = pl.ds(pl.multiple_of(xx * 32, 32), 32)
            total = own[j, yy, rows, :].astype(jnp.float32) + got[j, yy, rows, :].astype(jnp.float32)
            for zz in range(4):
                mine = total[8 * zz : 8 * zz + 8]
                part0[j, yy, xx, zz] = jnp.concatenate([mine[:, :512], mine[:, 512:]], 0).astype(jnp.bfloat16)
            return carry

        lax.fori_loop(0, 16, add_cores, 0)
        begin(j, 0)

    def small_step(axis):
        for copy in tiny_copies:
            copy.wait()
        small_all[axis, here[axis]] = total_small(axis - 1)
        return spread_small(axis)

    blocks = o_table.shape[0] // 256
    lax.fori_loop(0, blocks // 4, place, 0)
    for j in range(PIECES):
        middle(j, 0)
    tiny_copies = small_step(1)
    lax.fori_loop(blocks // 4, blocks - blocks // 4, place, 0)

    for stage in (0, 1):
        for j in range(PIECES):

            def keep(rest, total, j=j, stage=stage):
                parts[stage + 1][(j,) + rest] = total.astype(jnp.bfloat16)

            end(j, stage, keep)
            begin(j, stage + 1)
        if stage == 0:
            tiny_copies = small_step(2)
            lax.fori_loop(blocks - blocks // 4, blocks, place, 0)
        for j in range(PIECES):
            middle(j, stage + 1)
    for copy in tiny_copies:
        copy.wait()
    o_small[...] = total_small(2)

    for j in range(PIECES):

        def write(rest, total, j=j):
            joined = jnp.concatenate([total[:8], total[8:]], 1).astype(jnp.bfloat16)
            outs[j][:, columns[j] : columns[j] + 1024] = joined

        end(j, 2, write)

    for copy in cross + sends:
        copy.wait_send()


def reduce_gradients(gradients, small, lists, returned, rows):
    bf16, f32 = jnp.bfloat16, jnp.float32
    hbm = pl.BlockSpec(memory_space=pl.ANY)
    vmem = pl.BlockSpec(memory_space=pltpu.VMEM)
    dma = pltpu.SemaphoreType.DMA
    split = lambda g: g.reshape(4, 2, 128, g.shape[1])
    return pl.pallas_call(
        reduce_kernel,
        name="reduce_gradients",
        out_shape=(
            jax.ShapeDtypeStruct((8, 3072), bf16),
            jax.ShapeDtypeStruct((8, 1024), bf16),
            jax.ShapeDtypeStruct((8, 1024), bf16),
            jax.ShapeDtypeStruct((8, 1024), bf16),
            jax.ShapeDtypeStruct(small.shape, f32),
            jax.ShapeDtypeStruct((rows, 128), bf16),
        ),
        in_specs=[hbm] * PIECES + [vmem] * 3,
        out_specs=[vmem] * 6,
        scratch_shapes=[
            pltpu.VMEM((PIECES, 4, 128, 1024), bf16),
            pltpu.VMEM((PIECES, 4, 128, 1024), bf16),
            pltpu.VMEM((PIECES, 4, 4, 4, 16, 512), bf16),
            pltpu.VMEM((PIECES, 4, 4, 16, 256), bf16),
            pltpu.VMEM((PIECES, 4, 4, 16, 256), bf16),
            pltpu.VMEM((PIECES, 4, 4, 16, 512), bf16),
            pltpu.VMEM((PIECES, 4, 4, 16, 512), bf16),
            pltpu.VMEM((PIECES, 4, 4, 16, 512), bf16),
            pltpu.VMEM((PIECES, 4, 16, 256), bf16),
            pltpu.VMEM((PIECES, 4, 16, 256), bf16),
            pltpu.VMEM((PIECES, 4, 16, 512), bf16),
            pltpu.VMEM((PIECES, 4, 16, 512), bf16),
            pltpu.VMEM((PIECES, 4, 16, 512), bf16),
            pltpu.VMEM((PIECES, 16, 256), bf16),
            pltpu.VMEM((PIECES, 16, 256), bf16),
            pltpu.VMEM((PIECES, 16, 512), bf16),
            pltpu.VMEM((PIECES, 16, 512), bf16),
            pltpu.VMEM(small.shape, f32),
            pltpu.VMEM((3, 4) + small.shape, f32),
            dma((PIECES,)),
            dma((PIECES,)),
            dma((PIECES,)),
            dma((3, PIECES, 4)),
            dma((3, PIECES, 4)),
            dma,
            dma,
            dma((3, 3)),
            dma((3, 3)),
        ],
        compiler_params=pltpu.CompilerParams(
            collective_id=0, has_side_effects=True, vmem_limit_bytes=48 * 1024 * 1024
        ),
    )(*[split(g) for g in gradients], small, lists, returned)


def body(
    node_table,
    touched,
    member_slot,
    distances,
    cotangent,
    w_qkv,
    w_out,
    w_up,
    w_down,
    gains,
    bias_table,
):
    bf16, f32 = jnp.bfloat16, jnp.float32
    both = ("dp", "store")
    shard_rows, width = node_table.shape
    owners, cap = touched.shape[1:]
    egos, count = member_slot.shape
    tokens, slots_held = egos * count, owners * cap
    dot = lambda a, b: jnp.dot(a, b, preferred_element_type=f32)
    back = lambda a, b: lax.dot_general(a, b, (((1,), (1,)), ((), ())), preferred_element_type=f32)
    weight = lambda a, b: lax.dot_general(
        a, b, (((0,), (0,)), ((), ())), preferred_element_type=f32
    ).astype(bf16)

    x, lists, bias = fetch(node_table, touched, member_slot, distances, bias_table)
    x = x.astype(f32)
    dout = cotangent.reshape(tokens, width)

    h1, x_hat, x_rstd = layer_normalize(x, gains[0])
    h1 = h1.astype(bf16)
    qkv = dot(h1, w_qkv).astype(bf16)
    attended, probs = attention_forward(qkv, bias)
    y = x + dot(attended, w_out)
    h2, y_hat, y_rstd = layer_normalize(y, gains[1])
    h2 = h2.astype(bf16)
    act, slope = gelu_parts(dot(h2, w_up))
    act = act.astype(bf16)
    layer_out = (y + dot(act, w_down)).astype(bf16)

    du = (back(dout, w_down) * slope).astype(bf16)
    dy, gain_two = layer_normalize_backward(back(du, w_up), gains[1], y_hat, y_rstd)
    dy = dout.astype(f32) + dy
    dyb = dy.astype(bf16)
    dattn = back(dyb, w_out).astype(bf16)
    dq, dk, dv, grad_bias = attention_backward(qkv, dattn, probs, distances)
    dh1 = (
        back(dq, w_qkv[:, :width])
        + back(dk, w_qkv[:, width : 2 * width])
        + back(dv, w_qkv[:, 2 * width :])
    )
    dx, gain_one = layer_normalize_backward(dh1, gains[0], x_hat, x_rstd)
    dx = dy + dx

    slot_grads = slot_gradients(member_slot, dx, slots_held)
    returned = lax.all_to_all(
        slot_grads.reshape(-1, cap, 128), both, split_axis=0, concat_axis=0, tiled=True
    )
    gradients = (
        weight(act, dout), weight(h2, du), weight(attended, dyb),
        weight(h1, dq), weight(h1, dk), weight(h1, dv),
    )
    small = jnp.concatenate(
        [gain_one.reshape(8, 128), gain_two.reshape(8, 128), grad_bias.reshape(8, 128)]
    )
    sum_qkv, sum_out, sum_up, sum_down, small, grad_table = reduce_gradients(
        gradients, small, lists.reshape(-1, 1024), returned.reshape(-1, 128), shard_rows
    )
    return (
        layer_out.reshape(egos, count, width),
        grad_table,
        sum_qkv,
        sum_out,
        sum_up,
        sum_down,
        small[:16].reshape(2, width),
        small[16:].reshape(32, 32),
    )


def solution(mesh):
    in_specs = (
        P("store", None),
        P(("dp", "store"), None, None),
        P(("dp", "store"), None),
        P(("dp", "store"), None, None),
        P(("dp", "store"), None, None),
        P(),
        P(),
        P(),
        P(),
        P(),
        P(),
    )
    out_specs = (
        P(("dp", "store"), None, None),
        P("store", "dp"),
        P(("dp", "store"), None),
        P(("dp", "store"), None),
        P(("dp", "store"), None),
        P(("dp", "store"), None),
        P(),
        P(),
    )
    return jax.shard_map(body, mesh=mesh, in_specs=in_specs, out_specs=out_specs, check_vma=False)
```

```python
import math

import jax
import jax.numpy as jnp
from jax import lax
from jax.experimental import pallas as pl
from jax.experimental.pallas import tpu as pltpu
from jax.sharding import PartitionSpec as P

MESH = pl.DeviceIdType.MESH
ORDERS = ((0, 1, 2), (1, 2, 0), (2, 0, 1))
PIECES = 6


EPS = 1e-05
ROOT_HALF = 1.0 / math.sqrt(2.0)
ROOT_TWO_PI = 1.0 / math.sqrt(2.0 * math.pi)


def layer_normalize(value, gain):
    mean = jnp.mean(value, -1, keepdims=True)
    centred = value - mean
    rstd = lax.rsqrt(jnp.mean(centred * centred, -1, keepdims=True) + EPS)
    vhat = centred * rstd
    return (vhat * gain, vhat, rstd)


def layer_normalize_backward(grad, gain, vhat, rstd):
    scaled = grad * gain
    first = jnp.mean(scaled, -1, keepdims=True)
    second = jnp.mean(scaled * vhat, -1, keepdims=True)
    return (rstd * (scaled - first - vhat * second), jnp.sum(grad * vhat, 0))


def gelu_parts(upper):
    normal_cdf = 0.5 * (1.0 + jax.scipy.special.erf(upper * ROOT_HALF))
    activation_slope = normal_cdf + upper * jnp.exp(-0.5 * upper * upper) * ROOT_TWO_PI
    return (upper * normal_cdf, activation_slope)


LISTED = 128


def fetch_kernel(
    touched_in, member_slot, table_hbm, spd_hbm, bias_table,
    x_out, lists_out, bias_hbm,
    table, spd, touched, lookup, asked, lists, chosen, outgoing, slots, bias,
    table_sem, spd_sem, ask_send, ask_recv, list_send, list_recv, row_send, row_recv, bias_sem,
):
    dp, store = lax.axis_index("dp"), lax.axis_index("store")
    shards, groups = asked.shape[0], lists.shape[0]
    rows, width = table.shape
    cap = slots.shape[1] // 2
    half = width // 2
    egos, heads, count, _ = bias.shape
    turn = lambda here, k, size: lax.rem(here + k, size)
    owners = [(dp, turn(store, k, shards)) for k in range(shards)]
    copies_of_shard = [(turn(dp, k, groups), store) for k in range(groups)]

    load = pltpu.make_async_copy(table_hbm, table, table_sem)
    load.start()
    load_spd = pltpu.make_async_copy(spd_hbm, spd, spd_sem)
    load_spd.start()
    barrier = pltpu.get_barrier_semaphore()
    for device in owners[1:] + copies_of_shard[1:]:
        pl.semaphore_signal(barrier, inc=1, device_id=device, device_id_type=MESH)
    wide = jnp.concatenate([touched_in[0], jnp.full((shards, LISTED - cap), -1, jnp.int32)], 1)
    for k in range(shards):
        touched[k] = wide[k : k + 1]
    buckets = bias_table.shape[0]
    square = jnp.concatenate(
        [bias_table[...] * LOG2E, jnp.zeros((buckets, LISTED - heads), jnp.float32)], 1
    )
    square = jnp.concatenate([square, jnp.zeros((LISTED - buckets, LISTED), jnp.float32)], 0)
    lookup[...] = square.T[:heads]
    pl.semaphore_wait(barrier, shards + groups - 2)

    requests = []
    for k in range(1, shards):
        copy = pltpu.make_async_remote_copy(
            src_ref=touched.at[owners[k][1]], dst_ref=asked.at[store],
            send_sem=ask_send.at[k], recv_sem=ask_recv.at[k],
            device_id=owners[k], device_id_type=MESH)
        copy.start()
        requests.append(copy)
    asked[store] = touched[store]

    many = 8
    parts = heads // many

    def bias_copy(index):
        ego, part = lax.div(index, parts), pl.ds(lax.rem(index, parts) * many, many)
        return pltpu.make_async_copy(bias.at[ego, part], bias_hbm.at[ego, part], bias_sem.at[index])

    def look_up(index, carry):
        ego, first = lax.div(index, parts), lax.rem(index, parts) * many
        tables = [jnp.broadcast_to(lookup[pl.ds(first + h, 1), :], (8, 128)) for h in range(many)]

        def step(n, carry):
            at = pl.ds(pl.multiple_of(n * 8, 8), 8)
            for a in range(0, count, 128):
                distance = spd[ego, at, a : a + 128]
                for h in range(many):
                    bias[ego, first + h, at, a : a + 128] = jnp.take_along_axis(
                        tables[h], distance, axis=1, mode="promise_in_bounds"
                    )
            return carry

        lax.fori_loop(0, count // 8, step, 0, unroll=2)
        bias_copy(index).start()
        return carry

    load_spd.wait()
    lax.fori_loop(0, 1, look_up, 0)
    for copy in requests:
        copy.wait_recv()
    shared = []
    for k in range(1, groups):
        copy = pltpu.make_async_remote_copy(
            src_ref=asked, dst_ref=lists.at[dp],
            send_sem=list_send.at[k], recv_sem=list_recv.at[k],
            device_id=copies_of_shard[k], device_id_type=MESH)
        copy.start()
        shared.append(copy)
    lists[dp] = asked[...]

    order = list(range(1, shards)) + [0]
    turned = jnp.concatenate(
        [asked[owners[k][1]] for k in order] + [jnp.full((LISTED - shards, LISTED), -1, jnp.int32)], 0
    ).T
    for p in range(0, shards, 2):
        pair = jnp.concatenate([turned[:cap, p : p + 1], turned[:cap, p + 1 : p + 2]], 0)
        shape = (2 * cap, rows)
        hit = jnp.broadcast_to(pair, shape) == lax.broadcasted_iota(jnp.int32, shape, 1)
        chosen[p * cap : (p + 2) * cap, :] = jnp.where(hit, 1.0, 0.0).astype(jnp.bfloat16)
    load.wait()
    sent = []
    for first in range(0, shards, 4):
        picks = chosen[first * cap : (first + 4) * cap, :]
        left = jnp.dot(picks, table[:, :half], preferred_element_type=jnp.float32)
        right = jnp.dot(picks, table[:, half:], preferred_element_type=jnp.float32)
        for i in range(4):
            k = order[first + i]
            mine = slice(i * cap, i * cap + cap)
            block = jnp.concatenate([left[mine], right[mine]], 0).astype(jnp.bfloat16)
            if k == 0:
                slots[store] = block
                continue
            outgoing[k] = block
            copy = pltpu.make_async_remote_copy(
                src_ref=outgoing.at[k], dst_ref=slots.at[store],
                send_sem=row_send.at[k], recv_sem=row_recv.at[k],
                device_id=owners[k], device_id_type=MESH)
            copy.start()
            sent.append(copy)

    lax.fori_loop(1, egos * parts, look_up, 0)
    for copy in sent:
        copy.wait_recv()
    held = slots[...].reshape(shards * 2 * cap, half)
    member = member_slot[...]
    member = (member + cap * lax.div(member, cap)).astype(jnp.float32)
    member = jnp.concatenate([member, jnp.zeros((8 - egos, count), jnp.float32)], 0).T.astype(jnp.int32)
    shape = (count, shards * 2 * cap)
    places = lax.broadcasted_iota(jnp.int32, shape, 1)
    for part in range(2):
        for ego in range(egos):
            hit = jnp.broadcast_to(member[:, ego : ego + 1] + part * cap, shape) == places
            x_out[ego * count : ego * count + count, part * half : part * half + half] = jnp.dot(
                jnp.where(hit, 1.0, 0.0).astype(jnp.bfloat16), held, preferred_element_type=jnp.float32
            ).astype(x_out.dtype)
    for copy in shared:
        copy.wait()
    lists_out[...] = lists[...]
    for copy in requests + sent:
        copy.wait_send()
    for index in range(egos * parts):
        bias_copy(index).wait()


def fetch(node_table, touched, member_slot, spd, table):
    bf16, f32, i32 = jnp.bfloat16, jnp.float32, jnp.int32
    _, shards, cap = touched.shape
    groups = lax.axis_size("dp")
    egos, count = member_slot.shape
    heads = table.shape[1]
    rows, width = node_table.shape
    hbm = pl.BlockSpec(memory_space=pl.ANY)
    vmem = pl.BlockSpec(memory_space=pltpu.VMEM)
    dma = pltpu.SemaphoreType.DMA
    x, lists, bias = pl.pallas_call(
        fetch_kernel,
        name="fetch",
        out_shape=(
            jax.ShapeDtypeStruct((egos * count, width), bf16),
            jax.ShapeDtypeStruct((groups, shards, 1, LISTED), i32),
            jax.ShapeDtypeStruct((egos, heads, count, count), f32),
        ),
        in_specs=[vmem, vmem, hbm, hbm, vmem],
        out_specs=(vmem, vmem, hbm),
        scratch_shapes=[
            pltpu.VMEM((rows, width), bf16),
            pltpu.VMEM(spd.shape, i32),
            pltpu.VMEM((shards, 1, LISTED), i32),
            pltpu.VMEM((heads, LISTED), f32),
            pltpu.VMEM((shards, 1, LISTED), i32),
            pltpu.VMEM((groups, shards, 1, LISTED), i32),
            pltpu.VMEM((shards * cap, rows), bf16),
            pltpu.VMEM((shards, 2 * cap, width // 2), bf16),
            pltpu.VMEM((shards, 2 * cap, width // 2), bf16),
            pltpu.VMEM((egos, heads, count, count), f32),
            dma,
            dma,
            dma((shards,)),
            dma((shards,)),
            dma((groups,)),
            dma((groups,)),
            dma((shards,)),
            dma((shards,)),
            dma((egos * heads // 8,)),
        ],
        compiler_params=pltpu.CompilerParams(
            collective_id=1, has_side_effects=True, vmem_limit_bytes=48 * 1024 * 1024
        ),
    )(touched, member_slot, node_table, spd, table)
    return x, lists[:, :, 0, :cap].reshape(-1), bias


GROUP = 8
LOG2E = math.log2(math.e)


def head_mask(rows, width, head):
    lanes = lax.broadcasted_iota(jnp.int32, (rows, width), 1)
    return lax.div(lanes, width // GROUP) == head


def only_head(value, head):
    return jnp.where(head_mask(value.shape[0], value.shape[1], head), value, jnp.zeros((), value.dtype))


def attend_kernel(q_ref, k_ref, v_ref, bias_ref, mixed_ref, probs_ref):
    count = q_ref.shape[0]
    head_width = q_ref.shape[1] // GROUP
    scale = LOG2E * head_width ** (-0.5)
    chunk = 32
    q, k, v = q_ref[...], k_ref[...], v_ref[...]
    mixed = jnp.zeros(q.shape, jnp.float32)
    for j in range(GROUP):
        raw = lax.dot_general(
            q, only_head(k, j), (((1,), (1,)), ((), ())), preferred_element_type=jnp.float32
        )
        parts = []
        for c in range(count // chunk):
            rows = slice(c * chunk, c * chunk + chunk)
            logits = raw[rows] * scale + bias_ref[0, j, rows, :]
            power = jnp.exp2(logits - jnp.max(logits, -1, keepdims=True))
            probs = power * (1.0 / jnp.sum(power, -1, keepdims=True))
            probs_ref[0, j, rows, :] = probs
            parts.append(probs.astype(jnp.bfloat16))
        mixed = mixed + jnp.dot(
            jnp.concatenate(parts, 0), only_head(v, j), preferred_element_type=jnp.float32
        )
    mixed_ref[...] = mixed.astype(mixed_ref.dtype)


def attend_back_kernel(
    q_ref, k_ref, v_ref, dattn_ref, probs_ref, spd_ref,
    dq_ref, dk_ref, dv_ref, bias_ref, slopes, onehot, corner,
):
    ego, group = pl.program_id(0), pl.program_id(1)
    count, width = q_ref.shape
    scale = (width // GROUP) ** (-0.5)
    buckets = 32
    chunk = 32
    q, k, v, dattn = q_ref[...], k_ref[...], v_ref[...], dattn_ref[...]

    @pl.when(group == 0)
    def _():
        def fill(n, carry):
            row = jnp.broadcast_to(spd_ref[0, pl.ds(n, 1), :], (buckets, count))
            hit = row == lax.broadcasted_iota(jnp.int32, (buckets, count), 0)
            onehot[pl.ds(pl.multiple_of(n * buckets, buckets), buckets), :] = jnp.where(hit, 1.0, 0.0).astype(jnp.bfloat16)
            return carry

        lax.fori_loop(0, count, fill, 0, unroll=4)

    dq = jnp.zeros((count, width), jnp.float32)
    dk = jnp.zeros((count, width), jnp.float32)
    dv = jnp.zeros((count, width), jnp.float32)
    over_rows = (((0,), (0,)), ((), ()))
    for j in range(GROUP):
        dprobs = lax.dot_general(
            dattn, only_head(v, j), (((1,), (1,)), ((), ())), preferred_element_type=jnp.float32
        )
        slope_parts, prob_parts = [], []
        for c in range(count // chunk):
            rows = slice(c * chunk, c * chunk + chunk)
            probs = probs_ref[0, j, rows, :]
            part = dprobs[rows]
            slope = probs * (part - jnp.sum(part * probs, -1, keepdims=True))
            for a in range(count // 128):
                slopes[group * (count // 128) + a, pl.ds(c * chunk * GROUP + j, chunk, stride=GROUP), :] = slope[:, a * 128 : a * 128 + 128]
            slope_parts.append((slope * scale).astype(jnp.bfloat16))
            prob_parts.append(probs.astype(jnp.bfloat16))
        slope_b = jnp.concatenate(slope_parts, 0)
        probs_b = jnp.concatenate(prob_parts, 0)
        dq = dq + jnp.dot(slope_b, only_head(k, j), preferred_element_type=jnp.float32)
        dk = dk + lax.dot_general(slope_b, only_head(q, j), over_rows, preferred_element_type=jnp.float32)
        dv = dv + lax.dot_general(probs_b, only_head(dattn, j), over_rows, preferred_element_type=jnp.float32)
    dq_ref[...] = dq.astype(dq_ref.dtype)
    dk_ref[...] = dk.astype(dk_ref.dtype)
    dv_ref[...] = dv.astype(dv_ref.dtype)

    @pl.when(group == pl.num_programs(1) - 1)
    def _():
        halves = count // 128
        groups = slopes.shape[0] // halves
        corner[...] = jnp.zeros_like(corner)

        def collect(i, carry):
            total = corner[...]
            for n in range(4):
                first = pl.multiple_of((i * 4 + n) * 8 * GROUP, 8 * GROUP)
                rows = pl.ds(first, 8 * GROUP)
                left = jnp.concatenate(
                    [
                        jnp.concatenate([slopes[g * halves + a, rows, :] for a in range(halves)], 1)
                        for g in range(groups)
                    ],
                    0,
                ).astype(jnp.bfloat16)
                first = pl.multiple_of((i * 4 + n) * 8 * buckets, 8 * buckets)
                right = onehot[pl.ds(first, 8 * buckets), :]
                total = total + lax.dot_general(
                    left, right, (((1,), (1,)), ((), ())), preferred_element_type=jnp.float32
                )
            corner[...] = total
            return carry

        lax.fori_loop(0, count // 32, collect, 0)
        shape = corner.shape
        node_row = lax.rem(lax.div(lax.broadcasted_iota(jnp.int32, shape, 0), GROUP), 8)
        node_col = lax.div(lax.broadcasted_iota(jnp.int32, shape, 1), buckets)
        kept = jnp.where(node_row == node_col, corner[...], 0.0)
        tall = []
        for g in range(groups):
            heads = kept[g * 8 * GROUP : g * 8 * GROUP + GROUP]
            for n in range(1, 8):
                heads = heads + kept[(g * 8 + n) * GROUP : (g * 8 + n) * GROUP + GROUP]
            tall.append(heads)
        bias_ref[0] = jnp.concatenate(tall, 0)


def attention_specs(count, width, heads):
    wide = width // heads * GROUP
    groups = heads // GROUP
    column = lambda part: pl.BlockSpec((count, wide), lambda e, g, part=part: (e, part * groups + g))
    probs = pl.BlockSpec((1, GROUP, count, count), lambda e, g: (e, g, 0, 0))
    spd = pl.BlockSpec((1, count, count), lambda e, g: (e, 0, 0))
    return column, probs, spd, groups


def attention_forward(qkv, bias):
    egos, heads, count, _ = bias.shape
    width = qkv.shape[1] // 3
    column, probs, _, groups = attention_specs(count, width, heads)
    return pl.pallas_call(
        attend_kernel,
        name="attend",
        grid=(egos, groups),
        out_shape=(
            jax.ShapeDtypeStruct((egos * count, width), jnp.bfloat16),
            jax.ShapeDtypeStruct((egos, heads, count, count), jnp.float32),
        ),
        in_specs=[column(0), column(1), column(2), probs],
        out_specs=(column(0), probs),
        compiler_params=pltpu.CompilerParams(vmem_limit_bytes=40 * 1024 * 1024),
    )(qkv, qkv, qkv, bias)


def attention_backward(qkv, dattn, probs, spd):
    egos, heads, count, _ = probs.shape
    width = qkv.shape[1] // 3
    column, probs_spec, spd_spec, groups = attention_specs(count, width, heads)
    flat = jax.ShapeDtypeStruct((egos * count, width), jnp.bfloat16)
    dq, dk, dv, bias = pl.pallas_call(
        attend_back_kernel,
        name="attend_back",
        grid=(egos, groups),
        out_shape=(flat, flat, flat, jax.ShapeDtypeStruct((egos, heads, 256), jnp.float32)),
        in_specs=[column(0), column(1), column(2), column(0), probs_spec, spd_spec],
        out_specs=(column(0), column(0), column(0), pl.BlockSpec((1, heads, 256), lambda e, g: (e, 0, 0))),
        scratch_shapes=[
            pltpu.VMEM((groups * (count // 128), count * GROUP, 128), jnp.float32),
            pltpu.VMEM((count * 32, count), jnp.bfloat16),
            pltpu.VMEM((groups * 8 * GROUP, 256), jnp.float32),
        ],
        compiler_params=pltpu.CompilerParams(vmem_limit_bytes=48 * 1024 * 1024),
    )(qkv, qkv, qkv, dattn, probs, spd)
    return dq, dk, dv, bias.reshape(egos, heads, 8, 32).sum((0, 2)).T


def slot_kernel(member_ref, dx_ref, out_ref):
    slots, tokens = out_ref.shape[1], dx_ref.shape[0]
    shape = (slots, tokens)
    hit = jnp.broadcast_to(member_ref[...], shape) == lax.broadcasted_iota(jnp.int32, shape, 0)
    placed = jnp.where(hit, 1.0, 0.0).astype(jnp.bfloat16)
    dx = dx_ref[...]
    high = dx.astype(jnp.bfloat16)
    low = (dx - high.astype(jnp.float32)).astype(jnp.bfloat16)
    total = jnp.dot(placed, high, preferred_element_type=jnp.float32) + jnp.dot(
        placed, low, preferred_element_type=jnp.float32
    )
    for c in range(out_ref.shape[0]):
        out_ref[c] = total[:, c * 128 : c * 128 + 128].astype(out_ref.dtype)


def slot_gradients(member_slot, dx, slots):
    tokens, width = dx.shape
    return pl.pallas_call(
        slot_kernel,
        name="slot_gradients",
        grid=(width // 256,),
        out_shape=jax.ShapeDtypeStruct((width // 128, slots, 128), jnp.bfloat16),
        in_specs=[pl.BlockSpec((1, tokens), lambda i: (0, 0)), pl.BlockSpec((tokens, 256), lambda i: (0, i))],
        out_specs=pl.BlockSpec((2, slots, 128), lambda i: (i, 0, 0)),
        compiler_params=pltpu.CompilerParams(vmem_limit_bytes=40 * 1024 * 1024),
    )(member_slot.reshape(1, tokens), dx)


def place_kernel(lists_ref, grads_ref, out_ref):
    block, entries = out_ref.shape[0], lists_ref.shape[1]
    base = pl.program_id(0) * block
    total = jnp.zeros(out_ref.shape, jnp.float32)
    step = 1024
    for a in range(0, entries, step):
        shape = (block, step)
        hit = jnp.broadcast_to(lists_ref[:, a : a + step], shape) == lax.broadcasted_iota(jnp.int32, shape, 0) + base
        total = total + jnp.dot(
            jnp.where(hit, 1.0, 0.0).astype(jnp.bfloat16), grads_ref[a : a + step], preferred_element_type=jnp.float32
        )
    out_ref[...] = total.astype(out_ref.dtype)


def place_gradients(lists, grads, rows):
    entries, width = grads.shape
    return pl.pallas_call(
        place_kernel,
        name="place_gradients",
        grid=(rows // 256,),
        out_shape=jax.ShapeDtypeStruct((rows, width), jnp.bfloat16),
        in_specs=[pl.BlockSpec((1, entries), lambda i: (0, 0)), pl.BlockSpec((entries, width), lambda i: (0, 0))],
        out_specs=pl.BlockSpec((256, width), lambda i: (i, 0)),
        compiler_params=pltpu.CompilerParams(vmem_limit_bytes=40 * 1024 * 1024),
    )(lists.reshape(1, entries), grads)


def coordinates():
    dp, store = lax.axis_index("dp"), lax.axis_index("store")
    return lax.div(dp, 2), lax.rem(dp, 2), lax.div(store, 4), lax.rem(store, 4)


def peer(y, core, x, z):
    return (y * 2 + core, x * 4 + z)


def along(axis, offset):
    y, core, x, z = coordinates()
    place = [y, x, z]
    place[axis] = lax.rem(place[axis] + offset, 4)
    return peer(place[0], core, place[1], place[2]), place[axis]


def reduce_kernel(
    g_down, g_up, g_out, g_q, g_k, g_v, small,
    o_qkv, o_out, o_up, o_down, o_small,
    own, got, part0, low0, high0, left0, right0, part1, low1, high1, left1, right1, part2, low2, high2, left2, right2,
    small_core, small_all,
    own_sem, core_send, core_recv, send, recv, sc_send, sc_recv, s_send, s_recv,
):
    y, core, x, z = coordinates()
    here = (y, x, z)
    other = peer(y, 1 - core, x, z)
    everyone = [other] + [along(a, k)[0] for a in range(3) for k in (1, 2, 3)]

    barrier = pltpu.get_barrier_semaphore()
    for device in everyone:
        pl.semaphore_signal(barrier, inc=1, device_id=device, device_id_type=MESH)
    pl.semaphore_wait(barrier, len(everyone))

    sources = [g_down, g_up, g_out, g_q, g_k, g_v]
    outs = [o_down, o_up, o_out] + [o_qkv] * 3
    columns = [0, 0, 0, 0, 1024, 2048]
    sends = []

    local, cross = [], []
    tiny = pltpu.make_async_remote_copy(
        src_ref=small, dst_ref=small_core, send_sem=sc_send, recv_sem=sc_recv,
        device_id=other, device_id_type=MESH)
    tiny.start()
    for j in range(PIECES):
        remote = pltpu.make_async_remote_copy(
            src_ref=sources[j].at[:, 1 - core], dst_ref=got.at[j],
            send_sem=core_send.at[j], recv_sem=core_recv.at[j],
            device_id=other, device_id_type=MESH)
        remote.start()
        cross.append(remote)
        keep = pltpu.make_async_copy(sources[j].at[:, core], own.at[j], own_sem.at[j])
        keep.start()
        local.append(keep)

    tiny.wait()

    def spread_small(axis):
        copies = []
        for k in (1, 2, 3):
            device, _ = along(axis, k)
            copy = pltpu.make_async_remote_copy(
                src_ref=small_all.at[axis, here[axis]], dst_ref=small_all.at[axis, here[axis]],
                send_sem=s_send.at[axis, k - 1], recv_sem=s_recv.at[axis, k - 1],
                device_id=device, device_id_type=MESH)
            copy.start()
            copies.append(copy)
        return copies

    def total_small(axis):
        return (small_all[axis, 0] + small_all[axis, 1]) + (small_all[axis, 2] + small_all[axis, 3])

    small_all[0, here[0]] = small[...] + small_core[...]
    tiny_copies = spread_small(0)

    parts = (part0, part1, part2)
    landing = ((low0, high0, left0, right0), (low1, high1, left1, right1), (low2, high2, left2, right2))

    def block_of(j, stage, rest, place):
        order = ORDERS[j % 3]
        where = [a for a in (0, 1, 2) if a not in order[:stage]].index(order[stage])
        index = list(rest)
        index.insert(where, place)
        return (j,) + tuple(index)

    def ring(j, stage):
        axis = ORDERS[j % 3][stage]
        return [along(axis, k) for k in (0, 1, 2, 3)]

    def push(j, stage, kind, block, device):
        copy = pltpu.make_async_remote_copy(
            src_ref=parts[stage].at[block], dst_ref=landing[stage][kind].at[j],
            send_sem=send.at[stage, j, kind], recv_sem=recv.at[stage, j, kind],
            device_id=device, device_id_type=MESH)
        copy.start()
        return copy

    everything = lambda stage: (slice(None),) * (2 - stage)
    rows_lanes = lambda half: (slice(None), pl.ds(half * 256, 256))
    flight = {}

    def begin(j, stage):
        places = ring(j, stage)
        block = block_of(j, stage, everything(stage), places[2][1])
        flight[j] = [
            push(j, stage, 0, block + rows_lanes(0), places[1][0]),
            push(j, stage, 1, block + rows_lanes(1), places[3][0]),
        ]

    def each(stage, step):
        if stage == 2:
            step(())
        else:
            def body(i, carry):
                step((lax.div(i, 4), lax.rem(i, 4)) if stage == 0 else (i,))
                return carry

            lax.fori_loop(0, 16 if stage == 0 else 4, body, 0)

    def middle(j, stage):
        places = ring(j, stage)
        for copy in flight[j]:
            copy.wait_recv()
        sends.extend(flight[j])

        def step(rest):
            for half, place in ((0, places[1][1]), (1, places[3][1])):
                at = block_of(j, stage, rest, place) + (slice(None), slice(half * 256, half * 256 + 256))
                total = parts[stage][at].astype(jnp.float32) + landing[stage][half][(j,) + rest].astype(jnp.float32)
                parts[stage][at] = total.astype(jnp.bfloat16)

        each(stage, step)
        flight[j] = [
            push(j, stage, 2, block_of(j, stage, everything(stage), places[1][1]), places[1][0]),
            push(j, stage, 3, block_of(j, stage, everything(stage), places[3][1]), places[3][0]),
        ]

    def end(j, stage, store):
        places = ring(j, stage)
        for copy in flight[j]:
            copy.wait_recv()
        sends.extend(flight[j])

        def step(rest):
            total = parts[stage][block_of(j, stage, rest, places[0][1])].astype(jnp.float32)
            for kind in (2, 3):
                total = total + landing[stage][kind][(j,) + rest].astype(jnp.float32)
            store(rest, total)

        each(stage, step)

    for j in range(PIECES):
        local[j].wait()
        cross[j].wait_recv()

        def add_cores(i, carry, j=j):
            yy, xx = lax.div(i, 4), lax.rem(i, 4)
            rows = pl.ds(pl.multiple_of(xx * 32, 32), 32)
            total = own[j, yy, rows, :].astype(jnp.float32) + got[j, yy, rows, :].astype(jnp.float32)
            for zz in range(4):
                mine = total[8 * zz : 8 * zz + 8]
                part0[j, yy, xx, zz] = jnp.concatenate([mine[:, :512], mine[:, 512:]], 0).astype(jnp.bfloat16)
            return carry

        lax.fori_loop(0, 16, add_cores, 0)
        begin(j, 0)

    def small_step(axis):
        for copy in tiny_copies:
            copy.wait()
        small_all[axis, here[axis]] = total_small(axis - 1)
        return spread_small(axis)

    for j in range(PIECES):
        middle(j, 0)
    tiny_copies = small_step(1)

    for stage in (0, 1):
        for j in range(PIECES):

            def keep(rest, total, j=j, stage=stage):
                parts[stage + 1][(j,) + rest] = total.astype(jnp.bfloat16)

            end(j, stage, keep)
            begin(j, stage + 1)
        if stage == 0:
            tiny_copies = small_step(2)
        for j in range(PIECES):
            middle(j, stage + 1)
    for copy in tiny_copies:
        copy.wait()
    o_small[...] = total_small(2)

    for j in range(PIECES):

        def write(rest, total, j=j):
            joined = jnp.concatenate([total[:8], total[8:]], 1).astype(jnp.bfloat16)
            outs[j][:, columns[j] : columns[j] + 1024] = joined

        end(j, 2, write)

    for copy in cross + sends:
        copy.wait_send()


def reduce_gradients(gradients, small):
    bf16, f32 = jnp.bfloat16, jnp.float32
    hbm = pl.BlockSpec(memory_space=pl.ANY)
    vmem = pl.BlockSpec(memory_space=pltpu.VMEM)
    dma = pltpu.SemaphoreType.DMA
    split = lambda g: g.reshape(4, 2, 128, g.shape[1])
    return pl.pallas_call(
        reduce_kernel,
        name="reduce_gradients",
        out_shape=(
            jax.ShapeDtypeStruct((8, 3072), bf16),
            jax.ShapeDtypeStruct((8, 1024), bf16),
            jax.ShapeDtypeStruct((8, 1024), bf16),
            jax.ShapeDtypeStruct((8, 1024), bf16),
            jax.ShapeDtypeStruct(small.shape, f32),
        ),
        in_specs=[hbm] * PIECES + [vmem],
        out_specs=[vmem] * 5,
        scratch_shapes=[
            pltpu.VMEM((PIECES, 4, 128, 1024), bf16),
            pltpu.VMEM((PIECES, 4, 128, 1024), bf16),
            pltpu.VMEM((PIECES, 4, 4, 4, 16, 512), bf16),
            pltpu.VMEM((PIECES, 4, 4, 16, 256), bf16),
            pltpu.VMEM((PIECES, 4, 4, 16, 256), bf16),
            pltpu.VMEM((PIECES, 4, 4, 16, 512), bf16),
            pltpu.VMEM((PIECES, 4, 4, 16, 512), bf16),
            pltpu.VMEM((PIECES, 4, 4, 16, 512), bf16),
            pltpu.VMEM((PIECES, 4, 16, 256), bf16),
            pltpu.VMEM((PIECES, 4, 16, 256), bf16),
            pltpu.VMEM((PIECES, 4, 16, 512), bf16),
            pltpu.VMEM((PIECES, 4, 16, 512), bf16),
            pltpu.VMEM((PIECES, 4, 16, 512), bf16),
            pltpu.VMEM((PIECES, 16, 256), bf16),
            pltpu.VMEM((PIECES, 16, 256), bf16),
            pltpu.VMEM((PIECES, 16, 512), bf16),
            pltpu.VMEM((PIECES, 16, 512), bf16),
            pltpu.VMEM(small.shape, f32),
            pltpu.VMEM((3, 4) + small.shape, f32),
            dma((PIECES,)),
            dma((PIECES,)),
            dma((PIECES,)),
            dma((3, PIECES, 4)),
            dma((3, PIECES, 4)),
            dma,
            dma,
            dma((3, 3)),
            dma((3, 3)),
        ],
        compiler_params=pltpu.CompilerParams(
            collective_id=0, has_side_effects=True, vmem_limit_bytes=48 * 1024 * 1024
        ),
    )(*[split(g) for g in gradients], small)


def body(
    node_table,
    touched,
    member_slot,
    distances,
    cotangent,
    w_qkv,
    w_out,
    w_up,
    w_down,
    gains,
    bias_table,
):
    bf16, f32 = jnp.bfloat16, jnp.float32
    both = ("dp", "store")
    shard_rows, width = node_table.shape
    owners, cap = touched.shape[1:]
    egos, count = member_slot.shape
    tokens, slots_held = egos * count, owners * cap
    dot = lambda a, b: jnp.dot(a, b, preferred_element_type=f32)
    back = lambda a, b: lax.dot_general(a, b, (((1,), (1,)), ((), ())), preferred_element_type=f32)
    weight = lambda a, b: lax.dot_general(
        a, b, (((0,), (0,)), ((), ())), preferred_element_type=f32
    ).astype(bf16)

    x, lists, bias = fetch(node_table, touched, member_slot, distances, bias_table)
    x = x.astype(f32)
    dout = cotangent.reshape(tokens, width)

    h1, x_hat, x_rstd = layer_normalize(x, gains[0])
    h1 = h1.astype(bf16)
    qkv = dot(h1, w_qkv).astype(bf16)
    attended, probs = attention_forward(qkv, bias)
    y = x + dot(attended, w_out)
    h2, y_hat, y_rstd = layer_normalize(y, gains[1])
    h2 = h2.astype(bf16)
    act, slope = gelu_parts(dot(h2, w_up))
    act = act.astype(bf16)
    layer_out = (y + dot(act, w_down)).astype(bf16)

    du = (back(dout, w_down) * slope).astype(bf16)
    dy, gain_two = layer_normalize_backward(back(du, w_up), gains[1], y_hat, y_rstd)
    dy = dout.astype(f32) + dy
    dyb = dy.astype(bf16)
    dattn = back(dyb, w_out).astype(bf16)
    dq, dk, dv, grad_bias = attention_backward(qkv, dattn, probs, distances)
    dh1 = (
        back(dq, w_qkv[:, :width])
        + back(dk, w_qkv[:, width : 2 * width])
        + back(dv, w_qkv[:, 2 * width :])
    )
    dx, gain_one = layer_normalize_backward(dh1, gains[0], x_hat, x_rstd)
    dx = dy + dx

    slot_grads = slot_gradients(member_slot, dx, slots_held)
    returned = lax.all_to_all(
        slot_grads.reshape(-1, cap, 128), both, split_axis=0, concat_axis=0, tiled=True
    )
    gradients = (
        weight(act, dout), weight(h2, du), weight(attended, dyb),
        weight(h1, dq), weight(h1, dk), weight(h1, dv),
    )
    small = jnp.concatenate(
        [gain_one.reshape(8, 128), gain_two.reshape(8, 128), grad_bias.reshape(8, 128)]
    )
    sum_qkv, sum_out, sum_up, sum_down, small = reduce_gradients(gradients, small)
    grad_table = place_gradients(lists, returned.reshape(-1, 128), shard_rows)
    return (
        layer_out.reshape(egos, count, width),
        grad_table,
        sum_qkv,
        sum_out,
        sum_up,
        sum_down,
        small[:16].reshape(2, width),
        small[16:].reshape(32, 32),
    )


def solution(mesh):
    in_specs = (
        P("store", None),
        P(("dp", "store"), None, None),
        P(("dp", "store"), None),
        P(("dp", "store"), None, None),
        P(("dp", "store"), None, None),
        P(),
        P(),
        P(),
        P(),
        P(),
        P(),
    )
    out_specs = (
        P(("dp", "store"), None, None),
        P("store", "dp"),
        P(("dp", "store"), None),
        P(("dp", "store"), None),
        P(("dp", "store"), None),
        P(("dp", "store"), None),
        P(),
        P(),
    )
    return jax.shard_map(body, mesh=mesh, in_specs=in_specs, out_specs=out_specs, check_vma=False)
```

```python
import math

import jax
import jax.numpy as jnp
from jax import lax
from jax.experimental import pallas as pl
from jax.experimental.pallas import tpu as pltpu
from jax.sharding import PartitionSpec as P

MESH = pl.DeviceIdType.MESH
ORDERS = ((0, 1, 2), (1, 2, 0), (2, 0, 1))
PIECES = 6


EPS = 1e-05
ROOT_HALF = 1.0 / math.sqrt(2.0)
ROOT_TWO_PI = 1.0 / math.sqrt(2.0 * math.pi)


def layer_normalize(value, gain):
    mean = jnp.mean(value, -1, keepdims=True)
    centred = value - mean
    rstd = lax.rsqrt(jnp.mean(centred * centred, -1, keepdims=True) + EPS)
    vhat = centred * rstd
    return (vhat * gain, vhat, rstd)


def layer_normalize_backward(grad, gain, vhat, rstd):
    scaled = grad * gain
    first = jnp.mean(scaled, -1, keepdims=True)
    second = jnp.mean(scaled * vhat, -1, keepdims=True)
    return (rstd * (scaled - first - vhat * second), jnp.sum(grad * vhat, 0))


def gelu_parts(upper):
    normal_cdf = 0.5 * (1.0 + jax.scipy.special.erf(upper * ROOT_HALF))
    activation_slope = normal_cdf + upper * jnp.exp(-0.5 * upper * upper) * ROOT_TWO_PI
    return (upper * normal_cdf, activation_slope)


LISTED = 128


def fetch_kernel(
    touched, members, table_hbm, spd, lookup,
    x_out, lists_out, bias_hbm,
    table, asked, lists, chosen, outgoing, slots, bias,
    table_sem, ask_send, ask_recv, list_send, list_recv, row_send, row_recv, bias_sem,
):
    dp, store = lax.axis_index("dp"), lax.axis_index("store")
    shards, groups = asked.shape[0], lists.shape[0]
    rows, width = table.shape
    cap = slots.shape[1] // 2
    half = width // 2
    egos, heads, count, _ = bias.shape
    turn = lambda here, k, size: lax.rem(here + k, size)
    owners = [(dp, turn(store, k, shards)) for k in range(shards)]
    copies_of_shard = [(turn(dp, k, groups), store) for k in range(groups)]

    load = pltpu.make_async_copy(table_hbm, table, table_sem)
    load.start()
    barrier = pltpu.get_barrier_semaphore()
    for device in owners[1:] + copies_of_shard[1:]:
        pl.semaphore_signal(barrier, inc=1, device_id=device, device_id_type=MESH)
    pl.semaphore_wait(barrier, shards + groups - 2)

    requests = []
    for k in range(1, shards):
        copy = pltpu.make_async_remote_copy(
            src_ref=touched.at[owners[k][1]], dst_ref=asked.at[store],
            send_sem=ask_send.at[k], recv_sem=ask_recv.at[k],
            device_id=owners[k], device_id_type=MESH)
        copy.start()
        requests.append(copy)
    asked[store] = touched[store]

    bias_copies = []

    def look_up(ego, first, many):
        def step(n, carry):
            at = pl.ds(pl.multiple_of(n * 8, 8), 8)
            for a in range(0, count, 128):
                distance = spd[ego, at, a : a + 128]
                for h in range(first, first + many):
                    row = jnp.broadcast_to(lookup[h : h + 1, :], (8, 128))
                    bias[ego, h, at, a : a + 128] = jnp.take_along_axis(
                        row, distance, axis=1, mode="promise_in_bounds"
                    )
            return carry

        lax.fori_loop(0, count // 8, step, 0, unroll=2)
        part = pl.ds(first, many)
        copy = pltpu.make_async_copy(
            bias.at[ego, part], bias_hbm.at[ego, part], bias_sem.at[len(bias_copies)])
        copy.start()
        bias_copies.append(copy)

    look_up(0, 0, 8)
    for copy in requests:
        copy.wait_recv()
    shared = []
    for k in range(1, groups):
        copy = pltpu.make_async_remote_copy(
            src_ref=asked, dst_ref=lists.at[dp],
            send_sem=list_send.at[k], recv_sem=list_recv.at[k],
            device_id=copies_of_shard[k], device_id_type=MESH)
        copy.start()
        shared.append(copy)
    lists[dp] = asked[...]

    order = list(range(1, shards)) + [0]
    turned = jnp.concatenate(
        [asked[owners[k][1]] for k in order] + [jnp.full((LISTED - shards, LISTED), -1, jnp.int32)], 0
    ).T
    for p in range(0, shards, 2):
        pair = jnp.concatenate([turned[:cap, p : p + 1], turned[:cap, p + 1 : p + 2]], 0)
        shape = (2 * cap, rows)
        hit = jnp.broadcast_to(pair, shape) == lax.broadcasted_iota(jnp.int32, shape, 1)
        chosen[p * cap : (p + 2) * cap, :] = jnp.where(hit, 1.0, 0.0).astype(jnp.bfloat16)
    load.wait()
    sent = []
    for first in range(0, shards, 4):
        picks = chosen[first * cap : (first + 4) * cap, :]
        left = jnp.dot(picks, table[:, :half], preferred_element_type=jnp.float32)
        right = jnp.dot(picks, table[:, half:], preferred_element_type=jnp.float32)
        for i in range(4):
            k = order[first + i]
            mine = slice(i * cap, i * cap + cap)
            block = jnp.concatenate([left[mine], right[mine]], 0).astype(jnp.bfloat16)
            if k == 0:
                slots[store] = block
                continue
            outgoing[k] = block
            copy = pltpu.make_async_remote_copy(
                src_ref=outgoing.at[k], dst_ref=slots.at[store],
                send_sem=row_send.at[k], recv_sem=row_recv.at[k],
                device_id=owners[k], device_id_type=MESH)
            copy.start()
            sent.append(copy)

    look_up(0, 8, heads - 8)
    look_up(1, 0, heads)
    for copy in sent:
        copy.wait_recv()
    tokens = members.shape[0]
    shape = (tokens, shards * 2 * cap)
    held = slots[...].reshape(shards * 2 * cap, half)
    places = lax.broadcasted_iota(jnp.int32, shape, 1)
    for part in range(2):
        hit = jnp.broadcast_to(members[...] + part * cap, shape) == places
        x_out[:, part * half : part * half + half] = jnp.dot(
            jnp.where(hit, 1.0, 0.0).astype(jnp.bfloat16), held, preferred_element_type=jnp.float32
        ).astype(x_out.dtype)
    for copy in shared:
        copy.wait()
    lists_out[...] = lists[...]
    for copy in requests + sent:
        copy.wait_send()
    for copy in bias_copies:
        copy.wait()


def fetch(node_table, touched, member_slot, spd, table):
    bf16, f32, i32 = jnp.bfloat16, jnp.float32, jnp.int32
    _, shards, cap = touched.shape
    groups = lax.axis_size("dp")
    egos, count = member_slot.shape
    heads = table.shape[1]
    rows, width = node_table.shape
    lookup = jnp.pad((table * LOG2E).T, ((0, 0), (0, 128 - table.shape[0])))
    listed = jnp.pad(
        touched.reshape(shards, 1, cap), ((0, 0), (0, 0), (0, LISTED - cap)), constant_values=-1
    )
    members = (member_slot + cap * lax.div(member_slot, cap)).reshape(egos * count, 1)
    hbm = pl.BlockSpec(memory_space=pl.ANY)
    vmem = pl.BlockSpec(memory_space=pltpu.VMEM)
    dma = pltpu.SemaphoreType.DMA
    x, lists, bias = pl.pallas_call(
        fetch_kernel,
        name="fetch",
        out_shape=(
            jax.ShapeDtypeStruct((egos * count, width), bf16),
            jax.ShapeDtypeStruct((groups, shards, 1, LISTED), i32),
            jax.ShapeDtypeStruct((egos, heads, count, count), f32),
        ),
        in_specs=[vmem, vmem, hbm, vmem, vmem],
        out_specs=(vmem, vmem, hbm),
        scratch_shapes=[
            pltpu.VMEM((rows, width), bf16),
            pltpu.VMEM((shards, 1, LISTED), i32),
            pltpu.VMEM((groups, shards, 1, LISTED), i32),
            pltpu.VMEM((shards * cap, rows), bf16),
            pltpu.VMEM((shards, 2 * cap, width // 2), bf16),
            pltpu.VMEM((shards, 2 * cap, width // 2), bf16),
            pltpu.VMEM((egos, heads, count, count), f32),
            dma,
            dma((shards,)),
            dma((shards,)),
            dma((groups,)),
            dma((groups,)),
            dma((shards,)),
            dma((shards,)),
            dma((3,)),
        ],
        compiler_params=pltpu.CompilerParams(
            collective_id=1, has_side_effects=True, vmem_limit_bytes=36 * 1024 * 1024
        ),
    )(listed, members, node_table, spd, lookup)
    return x, lists[:, :, 0, :cap].reshape(-1), bias


GROUP = 8
LOG2E = math.log2(math.e)


def head_mask(rows, width, head):
    lanes = lax.broadcasted_iota(jnp.int32, (rows, width), 1)
    return lax.div(lanes, width // GROUP) == head


def only_head(value, head):
    return jnp.where(head_mask(value.shape[0], value.shape[1], head), value, jnp.zeros((), value.dtype))


def attend_kernel(q_ref, k_ref, v_ref, bias_ref, mixed_ref, probs_ref):
    count = q_ref.shape[0]
    head_width = q_ref.shape[1] // GROUP
    scale = LOG2E * head_width ** (-0.5)
    chunk = 32
    q, k, v = q_ref[...], k_ref[...], v_ref[...]
    mixed = jnp.zeros(q.shape, jnp.float32)
    for j in range(GROUP):
        raw = lax.dot_general(
            q, only_head(k, j), (((1,), (1,)), ((), ())), preferred_element_type=jnp.float32
        )
        parts = []
        for c in range(count // chunk):
            rows = slice(c * chunk, c * chunk + chunk)
            logits = raw[rows] * scale + bias_ref[0, j, rows, :]
            power = jnp.exp2(logits - jnp.max(logits, -1, keepdims=True))
            probs = power * (1.0 / jnp.sum(power, -1, keepdims=True))
            probs_ref[0, j, rows, :] = probs
            parts.append(probs.astype(jnp.bfloat16))
        mixed = mixed + jnp.dot(
            jnp.concatenate(parts, 0), only_head(v, j), preferred_element_type=jnp.float32
        )
    mixed_ref[...] = mixed.astype(mixed_ref.dtype)


def attend_back_kernel(
    q_ref, k_ref, v_ref, dattn_ref, probs_ref, spd_ref,
    dq_ref, dk_ref, dv_ref, bias_ref, slopes, onehot, corner,
):
    ego, group = pl.program_id(0), pl.program_id(1)
    count, width = q_ref.shape
    scale = (width // GROUP) ** (-0.5)
    buckets = 32
    chunk = 32
    q, k, v, dattn = q_ref[...], k_ref[...], v_ref[...], dattn_ref[...]

    @pl.when(group == 0)
    def _():
        def fill(n, carry):
            row = jnp.broadcast_to(spd_ref[0, pl.ds(n, 1), :], (buckets, count))
            hit = row == lax.broadcasted_iota(jnp.int32, (buckets, count), 0)
            onehot[pl.ds(pl.multiple_of(n * buckets, buckets), buckets), :] = jnp.where(hit, 1.0, 0.0).astype(jnp.bfloat16)
            return carry

        lax.fori_loop(0, count, fill, 0, unroll=8)

    dq = jnp.zeros((count, width), jnp.float32)
    dk = jnp.zeros((count, width), jnp.float32)
    dv = jnp.zeros((count, width), jnp.float32)
    over_rows = (((0,), (0,)), ((), ()))
    for j in range(GROUP):
        dprobs = lax.dot_general(
            dattn, only_head(v, j), (((1,), (1,)), ((), ())), preferred_element_type=jnp.float32
        )
        slope_parts, prob_parts = [], []
        for c in range(count // chunk):
            rows = slice(c * chunk, c * chunk + chunk)
            probs = probs_ref[0, j, rows, :]
            part = dprobs[rows]
            slope = probs * (part - jnp.sum(part * probs, -1, keepdims=True))
            for a in range(count // 128):
                slopes[group * (count // 128) + a, pl.ds(c * chunk * GROUP + j, chunk, stride=GROUP), :] = slope[:, a * 128 : a * 128 + 128]
            slope_parts.append((slope * scale).astype(jnp.bfloat16))
            prob_parts.append(probs.astype(jnp.bfloat16))
        slope_b = jnp.concatenate(slope_parts, 0)
        probs_b = jnp.concatenate(prob_parts, 0)
        dq = dq + jnp.dot(slope_b, only_head(k, j), preferred_element_type=jnp.float32)
        dk = dk + lax.dot_general(slope_b, only_head(q, j), over_rows, preferred_element_type=jnp.float32)
        dv = dv + lax.dot_general(probs_b, only_head(dattn, j), over_rows, preferred_element_type=jnp.float32)
    dq_ref[...] = dq.astype(dq_ref.dtype)
    dk_ref[...] = dk.astype(dk_ref.dtype)
    dv_ref[...] = dv.astype(dv_ref.dtype)

    @pl.when(group == pl.num_programs(1) - 1)
    def _():
        halves = count // 128
        groups = slopes.shape[0] // halves
        corner[...] = jnp.zeros_like(corner)

        def collect(i, carry):
            total = corner[...]
            for n in range(4):
                first = pl.multiple_of((i * 4 + n) * 8 * GROUP, 8 * GROUP)
                rows = pl.ds(first, 8 * GROUP)
                left = jnp.concatenate(
                    [
                        jnp.concatenate([slopes[g * halves + a, rows, :] for a in range(halves)], 1)
                        for g in range(groups)
                    ],
                    0,
                ).astype(jnp.bfloat16)
                first = pl.multiple_of((i * 4 + n) * 8 * buckets, 8 * buckets)
                right = onehot[pl.ds(first, 8 * buckets), :]
                total = total + lax.dot_general(
                    left, right, (((1,), (1,)), ((), ())), preferred_element_type=jnp.float32
                )
            corner[...] = total
            return carry

        lax.fori_loop(0, count // 32, collect, 0)
        shape = corner.shape
        node_row = lax.rem(lax.div(lax.broadcasted_iota(jnp.int32, shape, 0), GROUP), 8)
        node_col = lax.div(lax.broadcasted_iota(jnp.int32, shape, 1), buckets)
        kept = jnp.where(node_row == node_col, corner[...], 0.0)
        tall = []
        for g in range(groups):
            heads = kept[g * 8 * GROUP : g * 8 * GROUP + GROUP]
            for n in range(1, 8):
                heads = heads + kept[(g * 8 + n) * GROUP : (g * 8 + n) * GROUP + GROUP]
            tall.append(heads)
        bias_ref[0] = jnp.concatenate(tall, 0)


def attention_specs(count, width, heads):
    wide = width // heads * GROUP
    groups = heads // GROUP
    column = lambda part: pl.BlockSpec((count, wide), lambda e, g, part=part: (e, part * groups + g))
    probs = pl.BlockSpec((1, GROUP, count, count), lambda e, g: (e, g, 0, 0))
    spd = pl.BlockSpec((1, count, count), lambda e, g: (e, 0, 0))
    return column, probs, spd, groups


def attention_forward(qkv, bias):
    egos, heads, count, _ = bias.shape
    width = qkv.shape[1] // 3
    column, probs, _, groups = attention_specs(count, width, heads)
    return pl.pallas_call(
        attend_kernel,
        name="attend",
        grid=(egos, groups),
        out_shape=(
            jax.ShapeDtypeStruct((egos * count, width), jnp.bfloat16),
            jax.ShapeDtypeStruct((egos, heads, count, count), jnp.float32),
        ),
        in_specs=[column(0), column(1), column(2), probs],
        out_specs=(column(0), probs),
        compiler_params=pltpu.CompilerParams(vmem_limit_bytes=16 * 1024 * 1024),
    )(qkv, qkv, qkv, bias)


def attention_backward(qkv, dattn, probs, spd):
    egos, heads, count, _ = probs.shape
    width = qkv.shape[1] // 3
    column, probs_spec, spd_spec, groups = attention_specs(count, width, heads)
    flat = jax.ShapeDtypeStruct((egos * count, width), jnp.bfloat16)
    dq, dk, dv, bias = pl.pallas_call(
        attend_back_kernel,
        name="attend_back",
        grid=(egos, groups),
        out_shape=(flat, flat, flat, jax.ShapeDtypeStruct((egos, heads, 256), jnp.float32)),
        in_specs=[column(0), column(1), column(2), column(0), probs_spec, spd_spec],
        out_specs=(column(0), column(0), column(0), pl.BlockSpec((1, heads, 256), lambda e, g: (e, 0, 0))),
        scratch_shapes=[
            pltpu.VMEM((groups * (count // 128), count * GROUP, 128), jnp.float32),
            pltpu.VMEM((count * 32, count), jnp.bfloat16),
            pltpu.VMEM((groups * 8 * GROUP, 256), jnp.float32),
        ],
        compiler_params=pltpu.CompilerParams(vmem_limit_bytes=26 * 1024 * 1024),
    )(qkv, qkv, qkv, dattn, probs, spd)
    return dq, dk, dv, bias.reshape(egos, heads, 8, 32).sum((0, 2)).T


def slot_kernel(member_ref, dx_ref, out_ref):
    slots, tokens = out_ref.shape[1], dx_ref.shape[0]
    shape = (slots, tokens)
    hit = jnp.broadcast_to(member_ref[...], shape) == lax.broadcasted_iota(jnp.int32, shape, 0)
    placed = jnp.where(hit, 1.0, 0.0).astype(jnp.bfloat16)
    dx = dx_ref[...]
    high = dx.astype(jnp.bfloat16)
    low = (dx - high.astype(jnp.float32)).astype(jnp.bfloat16)
    total = jnp.dot(placed, high, preferred_element_type=jnp.float32) + jnp.dot(
        placed, low, preferred_element_type=jnp.float32
    )
    for c in range(out_ref.shape[0]):
        out_ref[c] = total[:, c * 128 : c * 128 + 128].astype(out_ref.dtype)


def slot_gradients(member_slot, dx, slots):
    tokens, width = dx.shape
    return pl.pallas_call(
        slot_kernel,
        name="slot_gradients",
        grid=(width // 256,),
        out_shape=jax.ShapeDtypeStruct((width // 128, slots, 128), jnp.bfloat16),
        in_specs=[pl.BlockSpec((1, tokens), lambda i: (0, 0)), pl.BlockSpec((tokens, 256), lambda i: (0, i))],
        out_specs=pl.BlockSpec((2, slots, 128), lambda i: (i, 0, 0)),
        compiler_params=pltpu.CompilerParams(vmem_limit_bytes=12 * 1024 * 1024),
    )(member_slot.reshape(1, tokens), dx)


def place_kernel(lists_ref, grads_ref, out_ref):
    block, entries = out_ref.shape[0], lists_ref.shape[1]
    base = pl.program_id(0) * block
    total = jnp.zeros(out_ref.shape, jnp.float32)
    step = 1024
    for a in range(0, entries, step):
        shape = (block, step)
        hit = jnp.broadcast_to(lists_ref[:, a : a + step], shape) == lax.broadcasted_iota(jnp.int32, shape, 0) + base
        total = total + jnp.dot(
            jnp.where(hit, 1.0, 0.0).astype(jnp.bfloat16), grads_ref[a : a + step], preferred_element_type=jnp.float32
        )
    out_ref[...] = total.astype(out_ref.dtype)


def place_gradients(lists, grads, rows):
    entries, width = grads.shape
    return pl.pallas_call(
        place_kernel,
        name="place_gradients",
        grid=(rows // 512,),
        out_shape=jax.ShapeDtypeStruct((rows, width), jnp.bfloat16),
        in_specs=[pl.BlockSpec((1, entries), lambda i: (0, 0)), pl.BlockSpec((entries, width), lambda i: (0, 0))],
        out_specs=pl.BlockSpec((512, width), lambda i: (i, 0)),
        compiler_params=pltpu.CompilerParams(vmem_limit_bytes=12 * 1024 * 1024),
    )(lists.reshape(1, entries), grads)


def coordinates():
    dp, store = lax.axis_index("dp"), lax.axis_index("store")
    return lax.div(dp, 2), lax.rem(dp, 2), lax.div(store, 4), lax.rem(store, 4)


def peer(y, core, x, z):
    return (y * 2 + core, x * 4 + z)


def along(axis, offset):
    y, core, x, z = coordinates()
    place = [y, x, z]
    place[axis] = lax.rem(place[axis] + offset, 4)
    return peer(place[0], core, place[1], place[2]), place[axis]


def reduce_kernel(
    g_down, g_up, g_out, g_q, g_k, g_v, small,
    o_qkv, o_out, o_up, o_down, o_small,
    own, got, part0, recv0, part1, recv1, part2, recv2, small_core, small_all,
    own_sem, core_send, core_recv, send, recv, sc_send, sc_recv, s_send, s_recv,
):
    y, core, x, z = coordinates()
    here = (y, x, z)
    other = peer(y, 1 - core, x, z)
    everyone = [other] + [along(a, k)[0] for a in range(3) for k in (1, 2, 3)]

    barrier = pltpu.get_barrier_semaphore()
    for device in everyone:
        pl.semaphore_signal(barrier, inc=1, device_id=device, device_id_type=MESH)
    pl.semaphore_wait(barrier, len(everyone))

    sources = [g_down, g_up, g_out, g_q, g_k, g_v]
    outs = [o_down, o_up, o_out] + [o_qkv] * 3
    columns = [0, 0, 0, 0, 1024, 2048]
    sends = []

    local, cross = [], []
    tiny = pltpu.make_async_remote_copy(
        src_ref=small, dst_ref=small_core, send_sem=sc_send, recv_sem=sc_recv,
        device_id=other, device_id_type=MESH)
    tiny.start()
    for j in range(PIECES):
        remote = pltpu.make_async_remote_copy(
            src_ref=sources[j].at[:, 1 - core], dst_ref=got.at[j],
            send_sem=core_send.at[j], recv_sem=core_recv.at[j],
            device_id=other, device_id_type=MESH)
        remote.start()
        cross.append(remote)
        keep = pltpu.make_async_copy(sources[j].at[:, core], own.at[j], own_sem.at[j])
        keep.start()
        local.append(keep)

    tiny.wait()

    def spread_small(axis):
        copies = []
        for k in (1, 2, 3):
            device, _ = along(axis, k)
            copy = pltpu.make_async_remote_copy(
                src_ref=small_all.at[axis, here[axis]], dst_ref=small_all.at[axis, here[axis]],
                send_sem=s_send.at[axis, k - 1], recv_sem=s_recv.at[axis, k - 1],
                device_id=device, device_id_type=MESH)
            copy.start()
            copies.append(copy)
        return copies

    def total_small(axis):
        return (small_all[axis, 0] + small_all[axis, 1]) + (small_all[axis, 2] + small_all[axis, 3])

    small_all[0, here[0]] = small[...] + small_core[...]
    tiny_copies = spread_small(0)

    def scatter(j, stage, part):
        order = ORDERS[j % 3]
        axis = order[stage]
        left = [a for a in (0, 1, 2) if a not in order[:stage]]
        where = left.index(axis)
        landing = (recv0, recv1, recv2)[stage]
        copies = []
        for k in (1, 2, 3):
            device, place = along(axis, k)
            block = (j,) + (slice(None),) * where + (place,)
            copy = pltpu.make_async_remote_copy(
                src_ref=part.at[block], dst_ref=landing.at[j, k - 1],
                send_sem=send.at[stage, j, k - 1], recv_sem=recv.at[stage, j, k - 1],
                device_id=device, device_id_type=MESH)
            copy.start()
            copies.append(copy)
        return copies

    flight = [None] * PIECES
    for j in range(PIECES):
        local[j].wait()
        cross[j].wait_recv()

        def add_cores(i, carry, j=j):
            yy, xx = lax.div(i, 4), lax.rem(i, 4)
            rows = pl.ds(pl.multiple_of(xx * 32, 32), 32)
            total = own[j, yy, rows, :].astype(jnp.float32) + got[j, yy, rows, :].astype(jnp.float32)
            for zz in range(4):
                mine = total[8 * zz : 8 * zz + 8]
                part0[j, yy, xx, zz] = jnp.concatenate([mine[:, :512], mine[:, 512:]], 0).astype(jnp.bfloat16)
            return carry

        lax.fori_loop(0, 16, add_cores, 0)
        flight[j] = scatter(j, 0, part0)

    for copy in tiny_copies:
        copy.wait()
    small_all[1, here[1]] = total_small(0)
    tiny_copies = spread_small(1)

    for j in range(PIECES):
        for copy in flight[j]:
            copy.wait_recv()
        sends += flight[j]
        axis = ORDERS[j % 3][0]

        def add_first(i, carry, j=j, axis=axis):
            a, b = lax.div(i, 4), lax.rem(i, 4)
            block = [a, b]
            block.insert(axis, here[axis])
            total = part0[(j,) + tuple(block)].astype(jnp.float32)
            for k in range(3):
                total = total + recv0[j, k, a, b].astype(jnp.float32)
            part1[j, a, b] = total.astype(jnp.bfloat16)
            return carry

        lax.fori_loop(0, 16, add_first, 0)
        flight[j] = scatter(j, 1, part1)

    for copy in tiny_copies:
        copy.wait()
    small_all[2, here[2]] = total_small(1)
    tiny_copies = spread_small(2)

    for j in range(PIECES):
        for copy in flight[j]:
            copy.wait_recv()
        sends += flight[j]
        order = ORDERS[j % 3]
        where = [a for a in (0, 1, 2) if a != order[0]].index(order[1])

        def add_second(i, carry, j=j, axis=order[1], where=where):
            block = [i]
            block.insert(where, here[axis])
            total = part1[(j,) + tuple(block)].astype(jnp.float32)
            for k in range(3):
                total = total + recv1[j, k, i].astype(jnp.float32)
            part2[j, i] = total.astype(jnp.bfloat16)
            return carry

        lax.fori_loop(0, 4, add_second, 0)
        flight[j] = scatter(j, 2, part2)

    for copy in tiny_copies:
        copy.wait()
    o_small[...] = total_small(2)

    for j in range(PIECES):
        for copy in flight[j]:
            copy.wait_recv()
        sends += flight[j]
        axis = ORDERS[j % 3][2]
        total = part2[j, here[axis]].astype(jnp.float32)
        for k in range(3):
            total = total + recv2[j, k].astype(jnp.float32)
        joined = jnp.concatenate([total[:8], total[8:]], 1).astype(jnp.bfloat16)
        outs[j][:, columns[j] : columns[j] + 1024] = joined

    for copy in cross + sends:
        copy.wait_send()


def reduce_gradients(gradients, small):
    bf16, f32 = jnp.bfloat16, jnp.float32
    hbm = pl.BlockSpec(memory_space=pl.ANY)
    vmem = pl.BlockSpec(memory_space=pltpu.VMEM)
    dma = pltpu.SemaphoreType.DMA
    split = lambda g: g.reshape(4, 2, 128, g.shape[1])
    return pl.pallas_call(
        reduce_kernel,
        name="reduce_gradients",
        out_shape=(
            jax.ShapeDtypeStruct((8, 3072), bf16),
            jax.ShapeDtypeStruct((8, 1024), bf16),
            jax.ShapeDtypeStruct((8, 1024), bf16),
            jax.ShapeDtypeStruct((8, 1024), bf16),
            jax.ShapeDtypeStruct(small.shape, f32),
        ),
        in_specs=[hbm] * PIECES + [vmem],
        out_specs=[vmem] * 5,
        scratch_shapes=[
            pltpu.VMEM((PIECES, 4, 128, 1024), bf16),
            pltpu.VMEM((PIECES, 4, 128, 1024), bf16),
            pltpu.VMEM((PIECES, 4, 4, 4, 16, 512), bf16),
            pltpu.VMEM((PIECES, 3, 4, 4, 16, 512), bf16),
            pltpu.VMEM((PIECES, 4, 4, 16, 512), bf16),
            pltpu.VMEM((PIECES, 3, 4, 16, 512), bf16),
            pltpu.VMEM((PIECES, 4, 16, 512), bf16),
            pltpu.VMEM((PIECES, 3, 16, 512), bf16),
            pltpu.VMEM(small.shape, f32),
            pltpu.VMEM((3, 4) + small.shape, f32),
            dma((PIECES,)),
            dma((PIECES,)),
            dma((PIECES,)),
            dma((3, PIECES, 3)),
            dma((3, PIECES, 3)),
            dma,
            dma,
            dma((3, 3)),
            dma((3, 3)),
        ],
        compiler_params=pltpu.CompilerParams(
            collective_id=0, has_side_effects=True, vmem_limit_bytes=30 * 1024 * 1024
        ),
    )(*[split(g) for g in gradients], small)


def body(
    node_table,
    touched,
    member_slot,
    distances,
    cotangent,
    w_qkv,
    w_out,
    w_up,
    w_down,
    gains,
    bias_table,
):
    bf16, f32 = jnp.bfloat16, jnp.float32
    both = ("dp", "store")
    shard_rows, width = node_table.shape
    owners, cap = touched.shape[1:]
    egos, count = member_slot.shape
    tokens, slots_held = egos * count, owners * cap
    dot = lambda a, b: jnp.dot(a, b, preferred_element_type=f32)
    back = lambda a, b: lax.dot_general(a, b, (((1,), (1,)), ((), ())), preferred_element_type=f32)
    weight = lambda a, b: lax.dot_general(
        a, b, (((0,), (0,)), ((), ())), preferred_element_type=f32
    ).astype(bf16)

    x, lists, bias = fetch(node_table, touched, member_slot, distances, bias_table)
    x = x.astype(f32)
    dout = cotangent.reshape(tokens, width)

    h1, x_hat, x_rstd = layer_normalize(x, gains[0])
    h1 = h1.astype(bf16)
    qkv = dot(h1, w_qkv).astype(bf16)
    attended, probs = attention_forward(qkv, bias)
    y = x + dot(attended, w_out)
    h2, y_hat, y_rstd = layer_normalize(y, gains[1])
    h2 = h2.astype(bf16)
    act, slope = gelu_parts(dot(h2, w_up))
    act = act.astype(bf16)
    layer_out = (y + dot(act, w_down)).astype(bf16)

    du = (back(dout, w_down) * slope).astype(bf16)
    dy, gain_two = layer_normalize_backward(back(du, w_up), gains[1], y_hat, y_rstd)
    dy = dout.astype(f32) + dy
    dyb = dy.astype(bf16)
    dattn = back(dyb, w_out).astype(bf16)
    dq, dk, dv, grad_bias = attention_backward(qkv, dattn, probs, distances)
    dh1 = (
        back(dq, w_qkv[:, :width])
        + back(dk, w_qkv[:, width : 2 * width])
        + back(dv, w_qkv[:, 2 * width :])
    )
    dx, gain_one = layer_normalize_backward(dh1, gains[0], x_hat, x_rstd)
    dx = dy + dx

    slot_grads = slot_gradients(member_slot, dx, slots_held)
    returned = lax.all_to_all(
        slot_grads.reshape(-1, cap, 128), both, split_axis=0, concat_axis=0, tiled=True
    )
    gradients = (
        weight(act, dout), weight(h2, du), weight(attended, dyb),
        weight(h1, dq), weight(h1, dk), weight(h1, dv),
    )
    small = jnp.concatenate(
        [gain_one.reshape(8, 128), gain_two.reshape(8, 128), grad_bias.reshape(8, 128)]
    )
    sum_qkv, sum_out, sum_up, sum_down, small = reduce_gradients(gradients, small)
    grad_table = place_gradients(lists, returned.reshape(-1, 128), shard_rows)
    return (
        layer_out.reshape(egos, count, width),
        grad_table,
        sum_qkv,
        sum_out,
        sum_up,
        sum_down,
        small[:16].reshape(2, width),
        small[16:].reshape(32, 32),
    )


def solution(mesh):
    in_specs = (
        P("store", None),
        P(("dp", "store"), None, None),
        P(("dp", "store"), None),
        P(("dp", "store"), None, None),
        P(("dp", "store"), None, None),
        P(),
        P(),
        P(),
        P(),
        P(),
        P(),
    )
    out_specs = (
        P(("dp", "store"), None, None),
        P("store", "dp"),
        P(("dp", "store"), None),
        P(("dp", "store"), None),
        P(("dp", "store"), None),
        P(("dp", "store"), None),
        P(),
        P(),
    )
    return jax.shard_map(body, mesh=mesh, in_specs=in_specs, out_specs=out_specs, check_vma=False)
```

```python
import math

import jax
import jax.numpy as jnp
from jax import lax
from jax.experimental import pallas as pl
from jax.experimental.pallas import tpu as pltpu
from jax.sharding import PartitionSpec as P

MESH = pl.DeviceIdType.MESH
ORDERS = ((0, 1, 2), (1, 2, 0), (2, 0, 1))
PIECES = 6


EPS = 1e-05
ROOT_HALF = 1.0 / math.sqrt(2.0)
ROOT_TWO_PI = 1.0 / math.sqrt(2.0 * math.pi)


def layer_normalize(value, gain):
    mean = jnp.mean(value, -1, keepdims=True)
    centred = value - mean
    rstd = lax.rsqrt(jnp.mean(centred * centred, -1, keepdims=True) + EPS)
    vhat = centred * rstd
    return (vhat * gain, vhat, rstd)


def layer_normalize_backward(grad, gain, vhat, rstd):
    scaled = grad * gain
    first = jnp.mean(scaled, -1, keepdims=True)
    second = jnp.mean(scaled * vhat, -1, keepdims=True)
    return (rstd * (scaled - first - vhat * second), jnp.sum(grad * vhat, 0))


def gelu_parts(upper):
    normal_cdf = 0.5 * (1.0 + jax.scipy.special.erf(upper * ROOT_HALF))
    activation_slope = normal_cdf + upper * jnp.exp(-0.5 * upper * upper) * ROOT_TWO_PI
    return (upper * normal_cdf, activation_slope)


LISTED = 128


def fetch_kernel(
    touched, members, table_hbm, spd, lookup,
    x_out, lists_out, bias_hbm,
    table, asked, lists, chosen, outgoing, slots, bias,
    table_sem, ask_send, ask_recv, list_send, list_recv, row_send, row_recv, bias_sem,
):
    dp, store = lax.axis_index("dp"), lax.axis_index("store")
    shards, groups = asked.shape[0], lists.shape[0]
    rows, width = table.shape
    cap = slots.shape[1] // 2
    half = width // 2
    egos, heads, count, _ = bias.shape
    turn = lambda here, k, size: lax.rem(here + k, size)
    owners = [(dp, turn(store, k, shards)) for k in range(shards)]
    copies_of_shard = [(turn(dp, k, groups), store) for k in range(groups)]

    load = pltpu.make_async_copy(table_hbm, table, table_sem)
    load.start()
    barrier = pltpu.get_barrier_semaphore()
    for device in owners[1:] + copies_of_shard[1:]:
        pl.semaphore_signal(barrier, inc=1, device_id=device, device_id_type=MESH)
    pl.semaphore_wait(barrier, shards + groups - 2)

    requests = []
    for k in range(1, shards):
        copy = pltpu.make_async_remote_copy(
            src_ref=touched.at[owners[k][1]], dst_ref=asked.at[store],
            send_sem=ask_send.at[k], recv_sem=ask_recv.at[k],
            device_id=owners[k], device_id_type=MESH)
        copy.start()
        requests.append(copy)
    asked[store] = touched[store]

    bias_copies = []

    def look_up(ego, first, many):
        def step(n, carry):
            at = pl.ds(pl.multiple_of(n * 8, 8), 8)
            for a in range(0, count, 128):
                distance = spd[ego, at, a : a + 128]
                for h in range(first, first + many):
                    row = jnp.broadcast_to(lookup[h : h + 1, :], (8, 128))
                    bias[ego, h, at, a : a + 128] = jnp.take_along_axis(
                        row, distance, axis=1, mode="promise_in_bounds"
                    )
            return carry

        lax.fori_loop(0, count // 8, step, 0, unroll=2)
        part = pl.ds(first, many)
        copy = pltpu.make_async_copy(
            bias.at[ego, part], bias_hbm.at[ego, part], bias_sem.at[len(bias_copies)])
        copy.start()
        bias_copies.append(copy)

    look_up(0, 0, 8)
    for copy in requests:
        copy.wait_recv()
    shared = []
    for k in range(1, groups):
        copy = pltpu.make_async_remote_copy(
            src_ref=asked, dst_ref=lists.at[dp],
            send_sem=list_send.at[k], recv_sem=list_recv.at[k],
            device_id=copies_of_shard[k], device_id_type=MESH)
        copy.start()
        shared.append(copy)
    lists[dp] = asked[...]

    order = list(range(1, shards)) + [0]
    turned = jnp.concatenate(
        [asked[owners[k][1]] for k in order] + [jnp.full((LISTED - shards, LISTED), -1, jnp.int32)], 0
    ).T
    for p in range(0, shards, 2):
        pair = jnp.concatenate([turned[:cap, p : p + 1], turned[:cap, p + 1 : p + 2]], 0)
        shape = (2 * cap, rows)
        hit = jnp.broadcast_to(pair, shape) == lax.broadcasted_iota(jnp.int32, shape, 1)
        chosen[p * cap : (p + 2) * cap, :] = jnp.where(hit, 1.0, 0.0).astype(jnp.bfloat16)
    load.wait()
    sent = []
    for first in range(0, shards, 4):
        picks = chosen[first * cap : (first + 4) * cap, :]
        left = jnp.dot(picks, table[:, :half], preferred_element_type=jnp.float32)
        right = jnp.dot(picks, table[:, half:], preferred_element_type=jnp.float32)
        for i in range(4):
            k = order[first + i]
            mine = slice(i * cap, i * cap + cap)
            block = jnp.concatenate([left[mine], right[mine]], 0).astype(jnp.bfloat16)
            if k == 0:
                slots[store] = block
                continue
            outgoing[k] = block
            copy = pltpu.make_async_remote_copy(
                src_ref=outgoing.at[k], dst_ref=slots.at[store],
                send_sem=row_send.at[k], recv_sem=row_recv.at[k],
                device_id=owners[k], device_id_type=MESH)
            copy.start()
            sent.append(copy)

    look_up(0, 8, heads - 8)
    look_up(1, 0, heads)
    for copy in sent:
        copy.wait_recv()
    tokens = members.shape[0]
    shape = (tokens, shards * 2 * cap)
    held = slots[...].reshape(shards * 2 * cap, half)
    places = lax.broadcasted_iota(jnp.int32, shape, 1)
    for part in range(2):
        hit = jnp.broadcast_to(members[...] + part * cap, shape) == places
        x_out[:, part * half : part * half + half] = jnp.dot(
            jnp.where(hit, 1.0, 0.0).astype(jnp.bfloat16), held, preferred_element_type=jnp.float32
        ).astype(x_out.dtype)
    for copy in shared:
        copy.wait()
    lists_out[...] = lists[...]
    for copy in requests + sent:
        copy.wait_send()
    for copy in bias_copies:
        copy.wait()


def fetch(node_table, touched, member_slot, spd, table):
    bf16, f32, i32 = jnp.bfloat16, jnp.float32, jnp.int32
    _, shards, cap = touched.shape
    groups = lax.axis_size("dp")
    egos, count = member_slot.shape
    heads = table.shape[1]
    rows, width = node_table.shape
    lookup = jnp.pad((table * LOG2E).T, ((0, 0), (0, 128 - table.shape[0])))
    listed = jnp.pad(
        touched.reshape(shards, 1, cap), ((0, 0), (0, 0), (0, LISTED - cap)), constant_values=-1
    )
    members = (member_slot + cap * lax.div(member_slot, cap)).reshape(egos * count, 1)
    hbm = pl.BlockSpec(memory_space=pl.ANY)
    vmem = pl.BlockSpec(memory_space=pltpu.VMEM)
    dma = pltpu.SemaphoreType.DMA
    x, lists, bias = pl.pallas_call(
        fetch_kernel,
        name="fetch",
        out_shape=(
            jax.ShapeDtypeStruct((egos * count, width), bf16),
            jax.ShapeDtypeStruct((groups, shards, 1, LISTED), i32),
            jax.ShapeDtypeStruct((egos, heads, count, count), f32),
        ),
        in_specs=[vmem, vmem, hbm, vmem, vmem],
        out_specs=(vmem, vmem, hbm),
        scratch_shapes=[
            pltpu.VMEM((rows, width), bf16),
            pltpu.VMEM((shards, 1, LISTED), i32),
            pltpu.VMEM((groups, shards, 1, LISTED), i32),
            pltpu.VMEM((shards * cap, rows), bf16),
            pltpu.VMEM((shards, 2 * cap, width // 2), bf16),
            pltpu.VMEM((shards, 2 * cap, width // 2), bf16),
            pltpu.VMEM((egos, heads, count, count), f32),
            dma,
            dma((shards,)),
            dma((shards,)),
            dma((groups,)),
            dma((groups,)),
            dma((shards,)),
            dma((shards,)),
            dma((3,)),
        ],
        compiler_params=pltpu.CompilerParams(
            collective_id=1, has_side_effects=True, vmem_limit_bytes=48 * 1024 * 1024
        ),
    )(listed, members, node_table, spd, lookup)
    return x, lists[:, :, 0, :cap].reshape(-1), bias


GROUP = 8
LOG2E = math.log2(math.e)


def head_mask(rows, width, head):
    lanes = lax.broadcasted_iota(jnp.int32, (rows, width), 1)
    return lax.div(lanes, width // GROUP) == head


def only_head(value, head):
    return jnp.where(head_mask(value.shape[0], value.shape[1], head), value, jnp.zeros((), value.dtype))


def attend_kernel(q_ref, k_ref, v_ref, bias_ref, mixed_ref, probs_ref):
    count = q_ref.shape[0]
    head_width = q_ref.shape[1] // GROUP
    scale = LOG2E * head_width ** (-0.5)
    chunk = 32
    q, k, v = q_ref[...], k_ref[...], v_ref[...]
    mixed = jnp.zeros(q.shape, jnp.float32)
    for j in range(GROUP):
        raw = lax.dot_general(
            q, only_head(k, j), (((1,), (1,)), ((), ())), preferred_element_type=jnp.float32
        )
        parts = []
        for c in range(count // chunk):
            rows = slice(c * chunk, c * chunk + chunk)
            logits = raw[rows] * scale + bias_ref[0, j, rows, :]
            power = jnp.exp2(logits - jnp.max(logits, -1, keepdims=True))
            probs = power * (1.0 / jnp.sum(power, -1, keepdims=True))
            probs_ref[0, j, rows, :] = probs
            parts.append(probs.astype(jnp.bfloat16))
        mixed = mixed + jnp.dot(
            jnp.concatenate(parts, 0), only_head(v, j), preferred_element_type=jnp.float32
        )
    mixed_ref[...] = mixed.astype(mixed_ref.dtype)


def attend_back_kernel(
    q_ref, k_ref, v_ref, dattn_ref, probs_ref, spd_ref,
    dq_ref, dk_ref, dv_ref, bias_ref, slopes, onehot, corner,
):
    ego, group = pl.program_id(0), pl.program_id(1)
    count, width = q_ref.shape
    scale = (width // GROUP) ** (-0.5)
    buckets = 32
    chunk = 32
    q, k, v, dattn = q_ref[...], k_ref[...], v_ref[...], dattn_ref[...]

    @pl.when(group == 0)
    def _():
        def fill(n, carry):
            row = jnp.broadcast_to(spd_ref[0, pl.ds(n, 1), :], (buckets, count))
            hit = row == lax.broadcasted_iota(jnp.int32, (buckets, count), 0)
            onehot[pl.ds(pl.multiple_of(n * buckets, buckets), buckets), :] = jnp.where(hit, 1.0, 0.0).astype(jnp.bfloat16)
            return carry

        lax.fori_loop(0, count, fill, 0, unroll=8)

    dq = jnp.zeros((count, width), jnp.float32)
    dk = jnp.zeros((count, width), jnp.float32)
    dv = jnp.zeros((count, width), jnp.float32)
    over_rows = (((0,), (0,)), ((), ()))
    for j in range(GROUP):
        dprobs = lax.dot_general(
            dattn, only_head(v, j), (((1,), (1,)), ((), ())), preferred_element_type=jnp.float32
        )
        slope_parts, prob_parts = [], []
        for c in range(count // chunk):
            rows = slice(c * chunk, c * chunk + chunk)
            probs = probs_ref[0, j, rows, :]
            part = dprobs[rows]
            slope = probs * (part - jnp.sum(part * probs, -1, keepdims=True))
            for a in range(count // 128):
                slopes[group * (count // 128) + a, pl.ds(c * chunk * GROUP + j, chunk, stride=GROUP), :] = slope[:, a * 128 : a * 128 + 128]
            slope_parts.append((slope * scale).astype(jnp.bfloat16))
            prob_parts.append(probs.astype(jnp.bfloat16))
        slope_b = jnp.concatenate(slope_parts, 0)
        probs_b = jnp.concatenate(prob_parts, 0)
        dq = dq + jnp.dot(slope_b, only_head(k, j), preferred_element_type=jnp.float32)
        dk = dk + lax.dot_general(slope_b, only_head(q, j), over_rows, preferred_element_type=jnp.float32)
        dv = dv + lax.dot_general(probs_b, only_head(dattn, j), over_rows, preferred_element_type=jnp.float32)
    dq_ref[...] = dq.astype(dq_ref.dtype)
    dk_ref[...] = dk.astype(dk_ref.dtype)
    dv_ref[...] = dv.astype(dv_ref.dtype)

    @pl.when(group == pl.num_programs(1) - 1)
    def _():
        halves = count // 128
        groups = slopes.shape[0] // halves
        corner[...] = jnp.zeros_like(corner)

        def collect(i, carry):
            total = corner[...]
            for n in range(4):
                first = pl.multiple_of((i * 4 + n) * 8 * GROUP, 8 * GROUP)
                rows = pl.ds(first, 8 * GROUP)
                left = jnp.concatenate(
                    [
                        jnp.concatenate([slopes[g * halves + a, rows, :] for a in range(halves)], 1)
                        for g in range(groups)
                    ],
                    0,
                ).astype(jnp.bfloat16)
                first = pl.multiple_of((i * 4 + n) * 8 * buckets, 8 * buckets)
                right = onehot[pl.ds(first, 8 * buckets), :]
                total = total + lax.dot_general(
                    left, right, (((1,), (1,)), ((), ())), preferred_element_type=jnp.float32
                )
            corner[...] = total
            return carry

        lax.fori_loop(0, count // 32, collect, 0)
        shape = corner.shape
        node_row = lax.rem(lax.div(lax.broadcasted_iota(jnp.int32, shape, 0), GROUP), 8)
        node_col = lax.div(lax.broadcasted_iota(jnp.int32, shape, 1), buckets)
        kept = jnp.where(node_row == node_col, corner[...], 0.0)
        tall = []
        for g in range(groups):
            heads = kept[g * 8 * GROUP : g * 8 * GROUP + GROUP]
            for n in range(1, 8):
                heads = heads + kept[(g * 8 + n) * GROUP : (g * 8 + n) * GROUP + GROUP]
            tall.append(heads)
        bias_ref[0] = jnp.concatenate(tall, 0)


def attention_specs(count, width, heads):
    wide = width // heads * GROUP
    groups = heads // GROUP
    column = lambda part: pl.BlockSpec((count, wide), lambda e, g, part=part: (e, part * groups + g))
    probs = pl.BlockSpec((1, GROUP, count, count), lambda e, g: (e, g, 0, 0))
    spd = pl.BlockSpec((1, count, count), lambda e, g: (e, 0, 0))
    return column, probs, spd, groups


def attention_forward(qkv, bias):
    egos, heads, count, _ = bias.shape
    width = qkv.shape[1] // 3
    column, probs, _, groups = attention_specs(count, width, heads)
    return pl.pallas_call(
        attend_kernel,
        name="attend",
        grid=(egos, groups),
        out_shape=(
            jax.ShapeDtypeStruct((egos * count, width), jnp.bfloat16),
            jax.ShapeDtypeStruct((egos, heads, count, count), jnp.float32),
        ),
        in_specs=[column(0), column(1), column(2), probs],
        out_specs=(column(0), probs),
        compiler_params=pltpu.CompilerParams(vmem_limit_bytes=40 * 1024 * 1024),
    )(qkv, qkv, qkv, bias)


def attention_backward(qkv, dattn, probs, spd):
    egos, heads, count, _ = probs.shape
    width = qkv.shape[1] // 3
    column, probs_spec, spd_spec, groups = attention_specs(count, width, heads)
    flat = jax.ShapeDtypeStruct((egos * count, width), jnp.bfloat16)
    dq, dk, dv, bias = pl.pallas_call(
        attend_back_kernel,
        name="attend_back",
        grid=(egos, groups),
        out_shape=(flat, flat, flat, jax.ShapeDtypeStruct((egos, heads, 256), jnp.float32)),
        in_specs=[column(0), column(1), column(2), column(0), probs_spec, spd_spec],
        out_specs=(column(0), column(0), column(0), pl.BlockSpec((1, heads, 256), lambda e, g: (e, 0, 0))),
        scratch_shapes=[
            pltpu.VMEM((groups * (count // 128), count * GROUP, 128), jnp.float32),
            pltpu.VMEM((count * 32, count), jnp.bfloat16),
            pltpu.VMEM((groups * 8 * GROUP, 256), jnp.float32),
        ],
        compiler_params=pltpu.CompilerParams(vmem_limit_bytes=48 * 1024 * 1024),
    )(qkv, qkv, qkv, dattn, probs, spd)
    return dq, dk, dv, bias.reshape(egos, heads, 8, 32).sum((0, 2)).T


def slot_kernel(member_ref, dx_ref, out_ref):
    slots, tokens = out_ref.shape[1], dx_ref.shape[0]
    shape = (slots, tokens)
    hit = jnp.broadcast_to(member_ref[...], shape) == lax.broadcasted_iota(jnp.int32, shape, 0)
    placed = jnp.where(hit, 1.0, 0.0).astype(jnp.bfloat16)
    dx = dx_ref[...]
    high = dx.astype(jnp.bfloat16)
    low = (dx - high.astype(jnp.float32)).astype(jnp.bfloat16)
    total = jnp.dot(placed, high, preferred_element_type=jnp.float32) + jnp.dot(
        placed, low, preferred_element_type=jnp.float32
    )
    for c in range(out_ref.shape[0]):
        out_ref[c] = total[:, c * 128 : c * 128 + 128].astype(out_ref.dtype)


def slot_gradients(member_slot, dx, slots):
    tokens, width = dx.shape
    return pl.pallas_call(
        slot_kernel,
        name="slot_gradients",
        grid=(width // 256,),
        out_shape=jax.ShapeDtypeStruct((width // 128, slots, 128), jnp.bfloat16),
        in_specs=[pl.BlockSpec((1, tokens), lambda i: (0, 0)), pl.BlockSpec((tokens, 256), lambda i: (0, i))],
        out_specs=pl.BlockSpec((2, slots, 128), lambda i: (i, 0, 0)),
        compiler_params=pltpu.CompilerParams(vmem_limit_bytes=12 * 1024 * 1024),
    )(member_slot.reshape(1, tokens), dx)


def place_kernel(lists_ref, grads_ref, out_ref):
    block, entries = out_ref.shape[0], lists_ref.shape[1]
    base = pl.program_id(0) * block
    total = jnp.zeros(out_ref.shape, jnp.float32)
    step = 1024
    for a in range(0, entries, step):
        shape = (block, step)
        hit = jnp.broadcast_to(lists_ref[:, a : a + step], shape) == lax.broadcasted_iota(jnp.int32, shape, 0) + base
        total = total + jnp.dot(
            jnp.where(hit, 1.0, 0.0).astype(jnp.bfloat16), grads_ref[a : a + step], preferred_element_type=jnp.float32
        )
    out_ref[...] = total.astype(out_ref.dtype)


def place_gradients(lists, grads, rows):
    entries, width = grads.shape
    return pl.pallas_call(
        place_kernel,
        name="place_gradients",
        grid=(rows // 512,),
        out_shape=jax.ShapeDtypeStruct((rows, width), jnp.bfloat16),
        in_specs=[pl.BlockSpec((1, entries), lambda i: (0, 0)), pl.BlockSpec((entries, width), lambda i: (0, 0))],
        out_specs=pl.BlockSpec((512, width), lambda i: (i, 0)),
        compiler_params=pltpu.CompilerParams(vmem_limit_bytes=12 * 1024 * 1024),
    )(lists.reshape(1, entries), grads)


def coordinates():
    dp, store = lax.axis_index("dp"), lax.axis_index("store")
    return lax.div(dp, 2), lax.rem(dp, 2), lax.div(store, 4), lax.rem(store, 4)


def peer(y, core, x, z):
    return (y * 2 + core, x * 4 + z)


def along(axis, offset):
    y, core, x, z = coordinates()
    place = [y, x, z]
    place[axis] = lax.rem(place[axis] + offset, 4)
    return peer(place[0], core, place[1], place[2]), place[axis]


def reduce_kernel(
    g_down, g_up, g_out, g_q, g_k, g_v, small,
    o_qkv, o_out, o_up, o_down, o_small,
    own, got, part0, recv0, part1, recv1, part2, recv2, small_core, small_all,
    own_sem, core_send, core_recv, send, recv, sc_send, sc_recv, s_send, s_recv,
):
    y, core, x, z = coordinates()
    here = (y, x, z)
    other = peer(y, 1 - core, x, z)
    everyone = [other] + [along(a, k)[0] for a in range(3) for k in (1, 2, 3)]

    barrier = pltpu.get_barrier_semaphore()
    for device in everyone:
        pl.semaphore_signal(barrier, inc=1, device_id=device, device_id_type=MESH)
    pl.semaphore_wait(barrier, len(everyone))

    sources = [g_down, g_up, g_out, g_q, g_k, g_v]
    outs = [o_down, o_up, o_out] + [o_qkv] * 3
    columns = [0, 0, 0, 0, 1024, 2048]
    sends = []

    local, cross = [], []
    tiny = pltpu.make_async_remote_copy(
        src_ref=small, dst_ref=small_core, send_sem=sc_send, recv_sem=sc_recv,
        device_id=other, device_id_type=MESH)
    tiny.start()
    for j in range(PIECES):
        remote = pltpu.make_async_remote_copy(
            src_ref=sources[j].at[:, 1 - core], dst_ref=got.at[j],
            send_sem=core_send.at[j], recv_sem=core_recv.at[j],
            device_id=other, device_id_type=MESH)
        remote.start()
        cross.append(remote)
        keep = pltpu.make_async_copy(sources[j].at[:, core], own.at[j], own_sem.at[j])
        keep.start()
        local.append(keep)

    tiny.wait()

    def spread_small(axis):
        copies = []
        for k in (1, 2, 3):
            device, _ = along(axis, k)
            copy = pltpu.make_async_remote_copy(
                src_ref=small_all.at[axis, here[axis]], dst_ref=small_all.at[axis, here[axis]],
                send_sem=s_send.at[axis, k - 1], recv_sem=s_recv.at[axis, k - 1],
                device_id=device, device_id_type=MESH)
            copy.start()
            copies.append(copy)
        return copies

    def total_small(axis):
        return (small_all[axis, 0] + small_all[axis, 1]) + (small_all[axis, 2] + small_all[axis, 3])

    small_all[0, here[0]] = small[...] + small_core[...]
    tiny_copies = spread_small(0)

    def scatter(j, stage, part):
        order = ORDERS[j % 3]
        axis = order[stage]
        left = [a for a in (0, 1, 2) if a not in order[:stage]]
        where = left.index(axis)
        landing = (recv0, recv1, recv2)[stage]
        copies = []
        for k in (1, 2, 3):
            device, place = along(axis, k)
            block = (j,) + (slice(None),) * where + (place,)
            copy = pltpu.make_async_remote_copy(
                src_ref=part.at[block], dst_ref=landing.at[j, k - 1],
                send_sem=send.at[stage, j, k - 1], recv_sem=recv.at[stage, j, k - 1],
                device_id=device, device_id_type=MESH)
            copy.start()
            copies.append(copy)
        return copies

    flight = [None] * PIECES
    for j in range(PIECES):
        local[j].wait()
        cross[j].wait_recv()

        def add_cores(i, carry, j=j):
            yy, xx = lax.div(i, 4), lax.rem(i, 4)
            rows = pl.ds(pl.multiple_of(xx * 32, 32), 32)
            total = own[j, yy, rows, :].astype(jnp.float32) + got[j, yy, rows, :].astype(jnp.float32)
            for zz in range(4):
                mine = total[8 * zz : 8 * zz + 8]
                part0[j, yy, xx, zz] = jnp.concatenate([mine[:, :512], mine[:, 512:]], 0).astype(jnp.bfloat16)
            return carry

        lax.fori_loop(0, 16, add_cores, 0)
        flight[j] = scatter(j, 0, part0)

    for copy in tiny_copies:
        copy.wait()
    small_all[1, here[1]] = total_small(0)
    tiny_copies = spread_small(1)

    for j in range(PIECES):
        for copy in flight[j]:
            copy.wait_recv()
        sends += flight[j]
        axis = ORDERS[j % 3][0]

        def add_first(i, carry, j=j, axis=axis):
            a, b = lax.div(i, 4), lax.rem(i, 4)
            block = [a, b]
            block.insert(axis, here[axis])
            total = part0[(j,) + tuple(block)].astype(jnp.float32)
            for k in range(3):
                total = total + recv0[j, k, a, b].astype(jnp.float32)
            part1[j, a, b] = total.astype(jnp.bfloat16)
            return carry

        lax.fori_loop(0, 16, add_first, 0)
        flight[j] = scatter(j, 1, part1)

    for copy in tiny_copies:
        copy.wait()
    small_all[2, here[2]] = total_small(1)
    tiny_copies = spread_small(2)

    for j in range(PIECES):
        for copy in flight[j]:
            copy.wait_recv()
        sends += flight[j]
        order = ORDERS[j % 3]
        where = [a for a in (0, 1, 2) if a != order[0]].index(order[1])

        def add_second(i, carry, j=j, axis=order[1], where=where):
            block = [i]
            block.insert(where, here[axis])
            total = part1[(j,) + tuple(block)].astype(jnp.float32)
            for k in range(3):
                total = total + recv1[j, k, i].astype(jnp.float32)
            part2[j, i] = total.astype(jnp.bfloat16)
            return carry

        lax.fori_loop(0, 4, add_second, 0)
        flight[j] = scatter(j, 2, part2)

    for copy in tiny_copies:
        copy.wait()
    o_small[...] = total_small(2)

    for j in range(PIECES):
        for copy in flight[j]:
            copy.wait_recv()
        sends += flight[j]
        axis = ORDERS[j % 3][2]
        total = part2[j, here[axis]].astype(jnp.float32)
        for k in range(3):
            total = total + recv2[j, k].astype(jnp.float32)
        joined = jnp.concatenate([total[:8], total[8:]], 1).astype(jnp.bfloat16)
        outs[j][:, columns[j] : columns[j] + 1024] = joined

    for copy in cross + sends:
        copy.wait_send()


def reduce_gradients(gradients, small):
    bf16, f32 = jnp.bfloat16, jnp.float32
    hbm = pl.BlockSpec(memory_space=pl.ANY)
    vmem = pl.BlockSpec(memory_space=pltpu.VMEM)
    dma = pltpu.SemaphoreType.DMA
    split = lambda g: g.reshape(4, 2, 128, g.shape[1])
    return pl.pallas_call(
        reduce_kernel,
        name="reduce_gradients",
        out_shape=(
            jax.ShapeDtypeStruct((8, 3072), bf16),
            jax.ShapeDtypeStruct((8, 1024), bf16),
            jax.ShapeDtypeStruct((8, 1024), bf16),
            jax.ShapeDtypeStruct((8, 1024), bf16),
            jax.ShapeDtypeStruct(small.shape, f32),
        ),
        in_specs=[hbm] * PIECES + [vmem],
        out_specs=[vmem] * 5,
        scratch_shapes=[
            pltpu.VMEM((PIECES, 4, 128, 1024), bf16),
            pltpu.VMEM((PIECES, 4, 128, 1024), bf16),
            pltpu.VMEM((PIECES, 4, 4, 4, 16, 512), bf16),
            pltpu.VMEM((PIECES, 3, 4, 4, 16, 512), bf16),
            pltpu.VMEM((PIECES, 4, 4, 16, 512), bf16),
            pltpu.VMEM((PIECES, 3, 4, 16, 512), bf16),
            pltpu.VMEM((PIECES, 4, 16, 512), bf16),
            pltpu.VMEM((PIECES, 3, 16, 512), bf16),
            pltpu.VMEM(small.shape, f32),
            pltpu.VMEM((3, 4) + small.shape, f32),
            dma((PIECES,)),
            dma((PIECES,)),
            dma((PIECES,)),
            dma((3, PIECES, 3)),
            dma((3, PIECES, 3)),
            dma,
            dma,
            dma((3, 3)),
            dma((3, 3)),
        ],
        compiler_params=pltpu.CompilerParams(
            collective_id=0, has_side_effects=True, vmem_limit_bytes=40 * 1024 * 1024
        ),
    )(*[split(g) for g in gradients], small)


def body(
    node_table,
    touched,
    member_slot,
    distances,
    cotangent,
    w_qkv,
    w_out,
    w_up,
    w_down,
    gains,
    bias_table,
):
    bf16, f32 = jnp.bfloat16, jnp.float32
    both = ("dp", "store")
    shard_rows, width = node_table.shape
    owners, cap = touched.shape[1:]
    egos, count = member_slot.shape
    tokens, slots_held = egos * count, owners * cap
    dot = lambda a, b: jnp.dot(a, b, preferred_element_type=f32)
    back = lambda a, b: lax.dot_general(a, b, (((1,), (1,)), ((), ())), preferred_element_type=f32)
    weight = lambda a, b: lax.dot_general(
        a, b, (((0,), (0,)), ((), ())), preferred_element_type=f32
    ).astype(bf16)

    x, lists, bias = fetch(node_table, touched, member_slot, distances, bias_table)
    x = x.astype(f32)
    dout = cotangent.reshape(tokens, width)

    h1, x_hat, x_rstd = layer_normalize(x, gains[0])
    h1 = h1.astype(bf16)
    qkv = dot(h1, w_qkv).astype(bf16)
    attended, probs = attention_forward(qkv, bias)
    y = x + dot(attended, w_out)
    h2, y_hat, y_rstd = layer_normalize(y, gains[1])
    h2 = h2.astype(bf16)
    act, slope = gelu_parts(dot(h2, w_up))
    act = act.astype(bf16)
    layer_out = (y + dot(act, w_down)).astype(bf16)

    du = (back(dout, w_down) * slope).astype(bf16)
    dy, gain_two = layer_normalize_backward(back(du, w_up), gains[1], y_hat, y_rstd)
    dy = dout.astype(f32) + dy
    dyb = dy.astype(bf16)
    dattn = back(dyb, w_out).astype(bf16)
    layer_out, dattn = lax.optimization_barrier((layer_out, dattn))
    dq, dk, dv, grad_bias = attention_backward(qkv, dattn, probs, distances)
    dh1 = (
        back(dq, w_qkv[:, :width])
        + back(dk, w_qkv[:, width : 2 * width])
        + back(dv, w_qkv[:, 2 * width :])
    )
    dx, gain_one = layer_normalize_backward(dh1, gains[0], x_hat, x_rstd)
    dx = dy + dx

    slot_grads = slot_gradients(member_slot, dx, slots_held)
    returned = lax.all_to_all(
        slot_grads.reshape(-1, cap, 128), both, split_axis=0, concat_axis=0, tiled=True
    )
    gradients = (
        weight(act, dout), weight(h2, du), weight(attended, dyb),
        weight(h1, dq), weight(h1, dk), weight(h1, dv),
    )
    small = jnp.concatenate(
        [gain_one.reshape(8, 128), gain_two.reshape(8, 128), grad_bias.reshape(8, 128)]
    )
    sum_qkv, sum_out, sum_up, sum_down, small = reduce_gradients(gradients, small)
    grad_table = place_gradients(lists, returned.reshape(-1, 128), shard_rows)
    return (
        layer_out.reshape(egos, count, width),
        grad_table,
        sum_qkv,
        sum_out,
        sum_up,
        sum_down,
        small[:16].reshape(2, width),
        small[16:].reshape(32, 32),
    )


def solution(mesh):
    in_specs = (
        P("store", None),
        P(("dp", "store"), None, None),
        P(("dp", "store"), None),
        P(("dp", "store"), None, None),
        P(("dp", "store"), None, None),
        P(),
        P(),
        P(),
        P(),
        P(),
        P(),
    )
    out_specs = (
        P(("dp", "store"), None, None),
        P("store", "dp"),
        P(("dp", "store"), None),
        P(("dp", "store"), None),
        P(("dp", "store"), None),
        P(("dp", "store"), None),
        P(),
        P(),
    )
    return jax.shard_map(body, mesh=mesh, in_specs=in_specs, out_specs=out_specs, check_vma=False)
```
